32 devices in a mesh: fsdp: 16 (over z, x, core), seq: 2 (over y).
Axes of the slice: x: 2, y: 2, z: 4, core: 2. Of those that a mesh axis runs over, the one named last changes fastest.
Arguments:
- inputs: bfloat16 [64, 512, 768], P('fsdp', 'seq'), may hold values from -6 to 6
- segment_ids: int32 [64, 512], P('fsdp'), may hold values from 0 to 7, as said below
- token_flags: int32 [64, 512], P('fsdp'), may hold values from 0 to 1, as said below
- output_grad: bfloat16 [64, 512, 768], P('fsdp', 'seq'), may hold values from -6 to 6
- attention_weights: float32 [768, 3072], P(None, ('fsdp', 'seq'))
- feedforward_weights: float32 [768, 6144], P(None, ('fsdp', 'seq')), may hold values from -0.21875 to 0.21875
- layer_vectors: float32 [3, 3072], P(None, ('fsdp', 'seq'))
- attention_first: float32 [768, 3072], P(None, ('fsdp', 'seq')), may hold values from -512 to 512
- attention_second: float32 [768, 3072], P(None, ('fsdp', 'seq')), may hold values from 4096 to 65536
- feedforward_first: float32 [768, 6144], P(None, ('fsdp', 'seq')), may hold values from -512 to 512
- feedforward_second: float32 [768, 6144], P(None, ('fsdp', 'seq')), may hold values from 4096 to 65536
- vector_first: float32 [3, 3072], P(None, ('fsdp', 'seq')), may hold values from -1024 to 1024
- vector_second: float32 [3, 3072], P(None, ('fsdp', 'seq')), may hold values from 16384 to 262144
Outputs:
- layer_output: bfloat16 [64, 512, 768], P('fsdp', 'seq')
- input_grad: bfloat16 [64, 512, 768], P('fsdp', 'seq')
- pooled: float32 [64, 8, 768], P('fsdp', None, 'seq')
- stream_rms: float32 [3], replicated
- attention_new: float32 [768, 3072], P(None, ('fsdp', 'seq'))
- attention_first_new: float32 [768, 3072], P(None, ('fsdp', 'seq'))
- attention_second_new: float32 [768, 3072], P(None, ('fsdp', 'seq'))
- attention_low: bfloat16 [768, 3072], P(None, ('fsdp', 'seq'))
- feedforward_new: float32 [768, 6144], P(None, ('fsdp', 'seq'))
- feedforward_first_new: float32 [768, 6144], P(None, ('fsdp', 'seq'))
- feedforward_second_new: float32 [768, 6144], P(None, ('fsdp', 'seq'))
- feedforward_low: bfloat16 [768, 6144], P(None, ('fsdp', 'seq'))
- vectors_new: float32 [3, 3072], P(None, ('fsdp', 'seq'))
- vector_first_new: float32 [3, 3072], P(None, ('fsdp', 'seq'))
- vector_second_new: float32 [3, 3072], P(None, ('fsdp', 'seq'))
- vectors_low: bfloat16 [3, 3072], P(None, ('fsdp', 'seq'))
The draws below stay inside these ranges and needn't reach their ends.
Inputs may be any that keep to these rules, and one draw needn't show every extreme that they name: `segment_ids`: within each row the ids never fall and every id from 0 to 7 occurs. `token_flags`: the first position of every row is 1.
All inputs are finite; a program needn't handle non-finite values.
Results may differ from the reference program's by a relative error of at most 0.015.
Values may be sent and summed in bfloat16 or wider, within the bound.
A program may use at most 192 MiB of HBM per device.

```python
import math
import jax
import jax.numpy as jnp
import numpy as np
from jax import lax

D = 768
HEADS = 12
HEAD_DIM = 64
FF = 3072
LENGTH = 512
SEGMENTS = 8
STEP = 5
ROWS = 64


def draw_segment_ids(key, part):
    key = jax.random.fold_in(key, 19)
    low_edge = LENGTH // 2 - LENGTH // 8
    high_edge = LENGTH // 2 + LENGTH // 8
    places = np.arange(1, LENGTH)
    allowed = np.concatenate([places[places < low_edge], places[places >= high_edge]])
    candidates = jnp.asarray(allowed, dtype=jnp.int32)
    row_keys = jax.random.split(key, ROWS)

    def one_row(row_key):
        shuffled = jax.random.permutation(row_key, candidates.shape[0])
        boundaries = candidates[shuffled[:SEGMENTS - 1]]
        positions = jnp.arange(LENGTH, dtype=jnp.int32)
        return jnp.sum((boundaries[None, :] <= positions[:, None]).astype(jnp.int32), axis=1)
    return jax.vmap(one_row)(row_keys).astype(jnp.int32)


def draw_token_flags(key, part):
    key = jax.random.fold_in(key, 17)
    row_index = jnp.arange(ROWS, dtype=jnp.int32)[:, None]
    position = jnp.arange(LENGTH, dtype=jnp.int32)[None, :]
    threshold = (ROWS - 1 + 2 * row_index) * (LENGTH - 1 + 2 * position)
    rolled = jax.random.randint(key, (ROWS, LENGTH), 0, 9 * (ROWS - 1) * (LENGTH - 1), dtype=jnp.int32)
    return jnp.where((rolled < threshold) | (position == 0), 1, 0).astype(jnp.int32)


def draw_attention_weights(key, part):
    key = jax.random.fold_in(key, 11)
    base_noise = jax.random.normal(key, (D, 4 * D), jnp.float32)
    column = jnp.arange(4 * D)[None, :]
    column_scale = jnp.where(column < 3 * D, D ** (-0.5), (LENGTH / (SEGMENTS * D)) ** 0.5)
    return (base_noise * column_scale).astype(jnp.float32)


def draw_layer_vectors(key, part):
    key = jax.random.fold_in(key, 13)
    bias_noise = jax.random.normal(key, (3, 4 * D), jnp.float32)
    spread = jax.random.uniform(jax.random.fold_in(key, 1), (3, 4 * D), jnp.float32, -1.0, 1.0)
    row_index = jnp.arange(3)[:, None]
    quarter = jnp.arange(4 * D)[None, :] // D
    is_gain = (row_index == 2) & ((quarter == 0) | (quarter == 2))
    return jnp.where(is_gain, 1.0 + 0.4 * spread, 0.3 * bias_noise).astype(jnp.float32)


def block_levels(key, shape, cuts, smallest, top_value):
    loudness, own = 1.0, jax.random.fold_in(key, 6)
    for dim, blocks in cuts:
        steps = jnp.exp(jax.random.uniform(jax.random.fold_in(own, dim), (blocks,), jnp.float32, smallest / len(cuts), top_value / len(cuts)))
        loudness = loudness * jnp.repeat(steps, shape[dim] // blocks).reshape([-1 if axis == dim else 1 for axis in range(len(shape))])
    return loudness


def normal_values(stream_key, extent, deviation, bound, cuts=(), kind=jnp.bfloat16):
    level = block_levels(stream_key, extent, cuts, -0.22, 0.18) if cuts else 1.0
    values = jax.random.normal(stream_key, extent, jnp.float32) * deviation * level
    return jnp.minimum(jnp.maximum(values, -bound), bound).astype(kind)


def setup_inputs(seed: int = 0) -> dict:
    seeds = jax.random.split(jax.random.key(seed), 14)
    inputs = normal_values(seeds[0], (ROWS, LENGTH, D), 1.0, 6.0, ((0, 16), (1, 2)))
    segment_ids = draw_segment_ids(jax.random.fold_in(seeds[13], 71), 0)
    token_flags = draw_token_flags(jax.random.fold_in(seeds[13], 71), 0)
    output_grad = normal_values(seeds[3], (ROWS, LENGTH, D), 1.0, 6.0, ((0, 16), (1, 2)))
    attention_weights = draw_attention_weights(jax.random.fold_in(seeds[13], 71), 0)
    feedforward_weights = normal_values(seeds[5], (D, 2 * FF), D ** -0.5, 0.21875, ((1, 32),), jnp.float32)
    layer_vectors = draw_layer_vectors(jax.random.fold_in(seeds[13], 71), 0)
    attention_first = normal_values(seeds[7], (D, 4 * D), (0.5 * (ROWS * LENGTH) ** 0.5), 512.0, ((1, 32),), jnp.float32)
    attention_second = jnp.clip(jnp.exp(math.log(65536.0) - 2.7725887 * jax.random.uniform(seeds[8], (D, 4 * D), jnp.float32) ** block_levels(seeds[8], (D, 4 * D), ((1, 32),), -0.2, 0.2)), 4096.0, 65536.0)
    feedforward_first = normal_values(seeds[9], (D, 2 * FF), (0.5 * (ROWS * LENGTH) ** 0.5), 512.0, ((1, 32),), jnp.float32)
    feedforward_second = jnp.clip(jnp.exp(math.log(65536.0) - 2.7725887 * jax.random.uniform(seeds[10], (D, 2 * FF), jnp.float32) ** block_levels(seeds[10], (D, 2 * FF), ((1, 32),), -0.2, 0.2)), 4096.0, 65536.0)
    vector_first = normal_values(seeds[11], (3, 4 * D), ((ROWS * LENGTH) ** 0.5), 1024.0, ((1, 32),), jnp.float32)
    vector_second = jnp.clip(jnp.exp(math.log(262144.0) - 2.7725887 * jax.random.uniform(seeds[12], (3, 4 * D), jnp.float32) ** block_levels(seeds[12], (3, 4 * D), ((1, 32),), -0.2, 0.2)), 16384.0, 262144.0)
    return dict(inputs=inputs, segment_ids=segment_ids, token_flags=token_flags, output_grad=output_grad, attention_weights=attention_weights, feedforward_weights=feedforward_weights, layer_vectors=layer_vectors, attention_first=attention_first, attention_second=attention_second, feedforward_first=feedforward_first, feedforward_second=feedforward_second, vector_first=vector_first, vector_second=vector_second)


@jax.custom_vjp
def low(v):
    return lax.optimization_barrier(v.astype(jnp.bfloat16)).astype(jnp.float32)

@jax.custom_vjp
def low_back(v):
    return v

def low_keep(v):
    return (low(v), None)

def low_pass(kept, grad):
    return (grad,)

def back_keep(v):
    return (v, None)

def back_low(kept, grad):
    return (low(grad),)
low.defvjp(low_keep, low_pass)
low_back.defvjp(back_keep, back_low)
norm_epsilon = 1e-12
adam_epsilon = 1e-08
beta_first = 0.5
beta_second = 0.5
weight_decay = 0.01
rate_attention = 0.04
rate_feedforward = 0.03
rate_vectors = 0.2
masked_score = -1e+30

def dense_product(left_side, right_side):
    return jnp.dot(left_side, right_side, precision=lax.Precision.HIGHEST, preferred_element_type=jnp.float32)

def normalize(stream, gain, shift):
    average = lax.optimization_barrier(jnp.mean(stream, axis=-1, keepdims=True))
    centered = stream - average
    variance = lax.optimization_barrier(jnp.mean(centered * centered, axis=-1, keepdims=True))
    return centered * lax.rsqrt(variance + norm_epsilon) * gain + shift

def block_forward(pieces, attention_low, feedforward_low, vector_low):
    block_rows, block_ids, block_flags = pieces
    group_rows = block_rows.shape[0]
    tokens = block_rows.reshape(-1, D)
    score_scale = HEAD_DIM ** (-0.5)
    projected = dense_product(tokens, attention_low[:, :3 * D])
    queries = low_back(low((projected[:, :D] + vector_low[0, :D]) * score_scale))
    key_part = low_back(low(projected[:, D:2 * D]))
    value_part = low_back(low(projected[:, 2 * D:] + vector_low[0, D:2 * D]))
    head_shape = (group_rows, LENGTH, HEADS, HEAD_DIM)
    scores = jnp.einsum('rqhd,rkhd->rhqk', queries.reshape(head_shape), key_part.reshape(head_shape), precision=lax.Precision.HIGHEST)
    scores = low_back(scores)
    same_segment = block_ids[:, None, :, None] == block_ids[:, None, None, :]
    scores = jnp.where(same_segment, scores, masked_score)
    largest = lax.optimization_barrier(jnp.max(scores, axis=-1, keepdims=True))
    exponent = jnp.exp(scores - largest)
    soft_weights = low(exponent / lax.optimization_barrier(jnp.sum(exponent, axis=-1, keepdims=True)))
    context = jnp.einsum('rhqk,rkhd->rqhd', soft_weights, value_part.reshape(head_shape), precision=lax.Precision.HIGHEST)
    context = low_back(low(context.reshape(-1, D)))
    attention_out = low_back(dense_product(context, attention_low[:, 3 * D:]) + vector_low[0, 2 * D:3 * D])
    first_norm = low(normalize(tokens + attention_out, vector_low[2, :D], vector_low[2, D:2 * D]))
    up_value = low_back(dense_product(first_norm, feedforward_low[:, :FF]) + vector_low[1])
    activated = low(jax.nn.gelu(up_value, approximate=False))
    feed_out = low_back(dense_product(activated, feedforward_low[:, FF:].T) + vector_low[0, 3 * D:])
    result = normalize(first_norm + feed_out, vector_low[2, 2 * D:3 * D], vector_low[2, 3 * D:])
    flag_values = block_flags.reshape(-1).astype(jnp.float32)
    squares = jnp.stack([jnp.sum(flag_values * lax.optimization_barrier(jnp.mean(tokens * tokens, axis=-1))), jnp.sum(flag_values * lax.optimization_barrier(jnp.mean(attention_out * attention_out, axis=-1))), jnp.sum(flag_values * lax.optimization_barrier(jnp.mean(feed_out * feed_out, axis=-1)))])
    return (result.reshape(group_rows, LENGTH, D), squares)

def adamw_update(weight, gradient, first_moment, second_moment, step_rate, decay_rate):
    first_new = beta_first * first_moment + (1.0 - beta_first) * gradient
    second_new = beta_second * second_moment + (1.0 - beta_second) * gradient * gradient
    correction_first = 1.0 - beta_first ** STEP
    correction_second = 1.0 - beta_second ** STEP
    update = first_new / correction_first / (jnp.sqrt(second_new / correction_second) + adam_epsilon)
    weight_new = weight - step_rate * (update + decay_rate * weight)
    return (weight_new, first_new, second_new, weight_new.astype(jnp.bfloat16))

def reference(inputs, segment_ids, token_flags, output_grad, attention_weights, feedforward_weights, layer_vectors, attention_first, attention_second, feedforward_first, feedforward_second, vector_first, vector_second):
    group_rows = math.gcd(ROWS, 8)
    blocks = ROWS // group_rows

    def layer_forward(stream, attention_full, feedforward_full, vector_full):
        attention_low = low(attention_full)
        feedforward_low = low(feedforward_full)
        vector_low = low(vector_full)

        def one_block(pieces):
            return block_forward(pieces, attention_low, feedforward_low, vector_low)
        results, squares = lax.map(jax.checkpoint(one_block), (stream.reshape(blocks, group_rows, LENGTH, D), segment_ids.reshape(blocks, group_rows, LENGTH), token_flags.reshape(blocks, group_rows, LENGTH)))
        return (results.reshape(ROWS, LENGTH, D), lax.optimization_barrier(jnp.sum(squares, axis=0)))
    result, pullback, squares = jax.vjp(layer_forward, inputs.astype(jnp.float32), attention_weights, feedforward_weights, layer_vectors, has_aux=True)
    stream_grad, attention_grad, feedforward_grad, vector_grad = pullback(output_grad.astype(jnp.float32))
    layer_output = result.astype(jnp.bfloat16)
    input_grad = stream_grad.astype(jnp.bfloat16)
    members = (segment_ids[:, None, :] == jnp.arange(SEGMENTS, dtype=jnp.int32)[None, :, None]).astype(jnp.float32)
    members = members * token_flags[:, None, :].astype(jnp.float32)
    sums = jnp.einsum('rsl,rld->rsd', members, layer_output.astype(jnp.float32), precision=lax.Precision.HIGHEST)
    counts = lax.optimization_barrier(jnp.sum(members, axis=2))
    pooled = sums / jnp.maximum(counts, 1.0)[:, :, None]
    flag_total = jnp.sum(token_flags.astype(jnp.float32))
    stream_rms = jnp.sqrt(squares / flag_total)
    attention_new, attention_first_new, attention_second_new, attention_low = adamw_update(attention_weights, attention_grad, attention_first, attention_second, rate_attention, weight_decay)
    feedforward_new, feedforward_first_new, feedforward_second_new, feedforward_low = adamw_update(feedforward_weights, feedforward_grad, feedforward_first, feedforward_second, rate_feedforward, weight_decay)
    vectors_new, vector_first_new, vector_second_new, vectors_low = adamw_update(layer_vectors, vector_grad, vector_first, vector_second, rate_vectors, 0.0)
    return (layer_output, input_grad, pooled, stream_rms, attention_new, attention_first_new, attention_second_new, attention_low, feedforward_new, feedforward_first_new, feedforward_second_new, feedforward_low, vectors_new, vector_first_new, vector_second_new, vectors_low)
```

```python
import math
import types

import jax
import jax.numpy as jnp
from jax import lax
from jax.experimental import pallas as pl
from jax.experimental.pallas import tpu as pltpu
from jax.sharding import PartitionSpec as P

D = 768
HEADS = 12
HEAD_DIM = 64
FF = 3072
SEGMENTS = 8
STEP = 5


norm_epsilon = 1e-12
adam_epsilon = 1e-08
beta_first = 0.5
beta_second = 0.5
weight_decay = 0.01
rate_attention = 0.04
rate_feedforward = 0.03
rate_vectors = 0.2
masked_score = -1e30


def plain_dot(left_side, right_side):
    return jnp.dot(left_side, right_side, preferred_element_type=jnp.float32)


def contract_rows(left_side, right_side):
    return lax.dot_general(
        left_side, right_side, (((0,), (0,)), ((), ())), preferred_element_type=jnp.float32
    )


def contract_columns(left_side, right_side):
    return lax.dot_general(
        left_side, right_side, (((1,), (1,)), ((), ())), preferred_element_type=jnp.float32
    )


def normalize(stream):
    average = jnp.mean(stream, axis=-1, keepdims=True)
    centered = stream - average
    variance = jnp.mean(centered * centered, axis=-1, keepdims=True)
    inverse = lax.rsqrt(variance + norm_epsilon)
    return (centered * inverse, inverse)


def norm_back(grad_normed, normed, inverse):
    return inverse * (
        grad_normed
        - jnp.mean(grad_normed, axis=-1, keepdims=True)
        - normed * jnp.mean(grad_normed * normed, axis=-1, keepdims=True)
    )


def gelu_slope(value):
    return 0.5 * (1.0 + lax.erf(value * math.sqrt(0.5))) + value * jnp.exp(
        -0.5 * value * value
    ) / math.sqrt(2.0 * math.pi)


def masked_scores(queries, key_part, query_ids, key_ids):
    scores = jnp.einsum("rqhd,rkhd->rhqk", queries, key_part, preferred_element_type=jnp.float32)
    same_segment = query_ids[:, None, :, None] == key_ids[:, None, None, :]
    return jnp.where(same_segment, scores, masked_score)


def attend_block(pieces):
    queries, key_part, value_part, query_ids, key_ids = pieces
    scores = masked_scores(queries, key_part, query_ids, key_ids)
    largest = jnp.max(scores, axis=-1, keepdims=True)
    exponent = jnp.exp(scores - largest)
    denominator = jnp.sum(exponent, axis=-1, keepdims=True)
    soft_weights = (exponent / denominator).astype(jnp.bfloat16)
    context = jnp.einsum(
        "rhqk,rkhd->rqhd", soft_weights, value_part, preferred_element_type=jnp.float32
    )
    return (context, (largest + jnp.log(denominator))[..., 0])


def attend_back(pieces):
    queries, key_part, value_part, query_ids, key_ids, log_total, grad_context = pieces
    scores = masked_scores(queries, key_part, query_ids, key_ids)
    soft_again = jnp.exp(scores - log_total[..., None])
    grad_soft = jnp.einsum(
        "rqhd,rkhd->rhqk", grad_context, value_part, preferred_element_type=jnp.float32
    )
    inner_sum = jnp.sum(soft_again * grad_soft, axis=-1, keepdims=True)
    grad_scores = (soft_again * (grad_soft - inner_sum)).astype(jnp.bfloat16)
    grad_queries = jnp.einsum(
        "rhqk,rkhd->rqhd", grad_scores, key_part, preferred_element_type=jnp.float32
    )
    grad_keys = jnp.einsum(
        "rhqk,rqhd->rkhd", grad_scores, queries, preferred_element_type=jnp.float32
    )
    grad_values = jnp.einsum(
        "rhqk,rqhd->rkhd",
        soft_again.astype(jnp.bfloat16),
        grad_context,
        preferred_element_type=jnp.float32,
    )
    return (grad_queries, grad_keys, grad_values)


def adamw_update(weight, gradient, first_moment, second_moment, step_rate, decay_rate):
    first_new = beta_first * first_moment + (1.0 - beta_first) * gradient
    second_new = beta_second * second_moment + (1.0 - beta_second) * gradient * gradient
    correction_first = 1.0 - beta_first**STEP
    correction_second = 1.0 - beta_second**STEP
    update = (
        first_new / correction_first / (jnp.sqrt(second_new / correction_second) + adam_epsilon)
    )
    weight_new = weight - step_rate * (update + decay_rate * weight)
    return (weight_new, first_new, second_new, weight_new.astype(jnp.bfloat16))


def plain_shards(
    inputs,
    segment_ids,
    token_flags,
    output_grad,
    attention_weights,
    feedforward_weights,
    layer_vectors,
    attention_first,
    attention_second,
    feedforward_first,
    feedforward_second,
    vector_first,
    vector_second,
):
    row_count, local_span, model_width = inputs.shape
    full_length = segment_ids.shape[1]
    score_scale = HEAD_DIM ** (-0.5)
    inputs_here, grad_here = (inputs, output_grad)
    offset = lax.axis_index("seq") * local_span
    query_ids = lax.dynamic_slice_in_dim(segment_ids, offset, local_span, 1)
    work_flags = lax.dynamic_slice_in_dim(token_flags, offset, local_span, 1).astype(jnp.float32)
    work_span = inputs_here.shape[1]
    attention_full, feedforward_full, vector_low = (
        lax.all_gather(attention_weights.astype(jnp.bfloat16), ("fsdp", "seq"), axis=1, tiled=True),
        lax.all_gather(
            feedforward_weights.astype(jnp.bfloat16), ("fsdp", "seq"), axis=1, tiled=True
        ),
        lax.all_gather(layer_vectors.astype(jnp.bfloat16), ("fsdp", "seq"), axis=1, tiled=True),
    )
    vector_wide = vector_low.astype(jnp.float32)
    tokens = inputs_here.reshape(-1, D)
    tokens_wide = tokens.astype(jnp.float32)
    projected = plain_dot(tokens, attention_full[:, : 3 * D])
    queries = ((projected[:, :D] + vector_wide[0, :D]) * score_scale).astype(jnp.bfloat16)
    key_part = projected[:, D : 2 * D].astype(jnp.bfloat16)
    value_part = (projected[:, 2 * D :] + vector_wide[0, D : 2 * D]).astype(jnp.bfloat16)
    key_rows, value_rows = (
        lax.all_gather(key_part.reshape(row_count, work_span, D), "seq", axis=1, tiled=True),
        lax.all_gather(value_part.reshape(row_count, work_span, D), "seq", axis=1, tiled=True),
    )
    group_rows = math.gcd(row_count, max(1, 512 // work_span))
    block_count = row_count // group_rows
    query_blocks = queries.reshape(block_count, group_rows, work_span, HEADS, HEAD_DIM)
    key_blocks = key_rows.reshape(block_count, group_rows, full_length, HEADS, HEAD_DIM)
    value_blocks = value_rows.reshape(block_count, group_rows, full_length, HEADS, HEAD_DIM)
    query_id_blocks = query_ids.reshape(block_count, group_rows, work_span)
    key_id_blocks = segment_ids.reshape(block_count, group_rows, full_length)
    context, log_total = lax.map(
        attend_block, (query_blocks, key_blocks, value_blocks, query_id_blocks, key_id_blocks)
    )
    context_low = context.reshape(-1, D).astype(jnp.bfloat16)
    attention_out = (
        plain_dot(context_low, attention_full[:, 3 * D :]) + vector_wide[0, 2 * D : 3 * D]
    )
    first_normed, first_inverse = normalize(tokens_wide + attention_out)
    first_norm = (first_normed * vector_wide[2, :D] + vector_wide[2, D : 2 * D]).astype(
        jnp.bfloat16
    )
    up_value = plain_dot(first_norm, feedforward_full[:, :FF]) + vector_wide[1]
    activated = jax.nn.gelu(up_value, approximate=False).astype(jnp.bfloat16)
    feed_out = contract_columns(activated, feedforward_full[:, FF:]) + vector_wide[0, 3 * D :]
    second_normed, second_inverse = normalize(first_norm.astype(jnp.float32) + feed_out)
    layer_output = (second_normed * vector_wide[2, 2 * D : 3 * D] + vector_wide[2, 3 * D :]).astype(
        jnp.bfloat16
    )
    output_rows = layer_output.reshape(row_count, work_span, D)
    flat_flags = work_flags.reshape(-1)
    squares = jnp.stack(
        [
            jnp.sum(flat_flags * jnp.mean(tokens_wide * tokens_wide, axis=-1)),
            jnp.sum(flat_flags * jnp.mean(attention_out * attention_out, axis=-1)),
            jnp.sum(flat_flags * jnp.mean(feed_out * feed_out, axis=-1)),
        ]
    )
    square_total, flag_total = lax.psum((squares, jnp.sum(flat_flags)), ("fsdp", "seq"))
    stream_rms = jnp.sqrt(square_total / flag_total)
    segment_range = jnp.arange(SEGMENTS, dtype=jnp.int32)
    members = (query_ids[:, None, :] == segment_range[None, :, None]).astype(
        jnp.float32
    ) * work_flags[:, None, :]
    partial_pool = jnp.einsum(
        "rsl,rld->rsd",
        members.astype(jnp.bfloat16),
        output_rows,
        preferred_element_type=jnp.float32,
    )
    pool_share = lax.psum_scatter(
        partial_pool.astype(jnp.bfloat16), "seq", scatter_dimension=2, tiled=True
    ).astype(jnp.float32)
    full_members = (segment_ids[:, None, :] == segment_range[None, :, None]).astype(jnp.float32)
    full_members = full_members * token_flags[:, None, :].astype(jnp.float32)
    counts = jnp.sum(full_members, axis=2)
    pooled = pool_share / jnp.maximum(counts, 1.0)[:, :, None]
    attention_back, feedforward_back, vector_again = (
        lax.all_gather(attention_weights.astype(jnp.bfloat16), ("fsdp", "seq"), axis=1, tiled=True),
        lax.all_gather(
            feedforward_weights.astype(jnp.bfloat16), ("fsdp", "seq"), axis=1, tiled=True
        ),
        lax.all_gather(layer_vectors.astype(jnp.bfloat16), ("fsdp", "seq"), axis=1, tiled=True),
    )
    vector_back = vector_again.astype(jnp.float32)
    grad_out = grad_here.reshape(-1, D).astype(jnp.float32)
    grad_gain_second = jnp.sum(grad_out * second_normed, axis=0)
    grad_shift_second = jnp.sum(grad_out, axis=0)
    grad_second = norm_back(grad_out * vector_back[2, 2 * D : 3 * D], second_normed, second_inverse)
    grad_feed = grad_second.astype(jnp.bfloat16)
    grad_bias_down = jnp.sum(grad_feed.astype(jnp.float32), axis=0)
    grad_down = contract_rows(grad_feed, activated)
    grad_activated = plain_dot(grad_feed, feedforward_back[:, FF:])
    grad_up = (grad_activated * gelu_slope(up_value)).astype(jnp.bfloat16)
    grad_bias_up = jnp.sum(grad_up.astype(jnp.float32), axis=0)
    grad_up_weight = contract_rows(first_norm, grad_up)
    grad_first = grad_second + contract_columns(grad_up, feedforward_back[:, :FF])
    grad_feedforward = jnp.concatenate([grad_up_weight, grad_down], axis=1)
    grad_gain_first = jnp.sum(grad_first * first_normed, axis=0)
    grad_shift_first = jnp.sum(grad_first, axis=0)
    grad_stream = norm_back(grad_first * vector_back[2, :D], first_normed, first_inverse)
    grad_attention_out = grad_stream.astype(jnp.bfloat16)
    grad_bias_out = jnp.sum(grad_attention_out.astype(jnp.float32), axis=0)
    grad_out_weight = contract_rows(context_low, grad_attention_out)
    grad_context = contract_columns(grad_attention_out, attention_back[:, 3 * D :]).astype(
        jnp.bfloat16
    )
    grad_query, grad_key_rows, grad_value_rows = lax.map(
        attend_back,
        (
            query_blocks,
            key_blocks,
            value_blocks,
            query_id_blocks,
            key_id_blocks,
            log_total,
            grad_context.reshape(block_count, group_rows, work_span, HEADS, HEAD_DIM),
        ),
    )
    key_share, value_share = (
        lax.psum_scatter(
            grad_key_rows.reshape(row_count, full_length, D).astype(jnp.bfloat16),
            "seq",
            scatter_dimension=1,
            tiled=True,
        ).astype(jnp.float32),
        lax.psum_scatter(
            grad_value_rows.reshape(row_count, full_length, D).astype(jnp.bfloat16),
            "seq",
            scatter_dimension=1,
            tiled=True,
        ).astype(jnp.float32),
    )
    grad_query_low = grad_query.reshape(-1, D).astype(jnp.bfloat16) * score_scale
    grad_key_low = key_share.reshape(-1, D).astype(jnp.bfloat16)
    grad_value_low = value_share.reshape(-1, D).astype(jnp.bfloat16)
    grad_projected = jnp.concatenate([grad_query_low, grad_key_low, grad_value_low], axis=1)
    grad_bias_query = jnp.sum(grad_query_low.astype(jnp.float32), axis=0)
    grad_bias_value = jnp.sum(grad_value_low.astype(jnp.float32), axis=0)
    grad_in_weight = contract_rows(tokens, grad_projected)
    input_rows = (
        grad_stream + contract_columns(grad_projected, attention_back[:, : 3 * D])
    ).astype(jnp.bfloat16)
    input_rows = input_rows.reshape(row_count, work_span, D)
    grad_attention = jnp.concatenate([grad_in_weight, grad_out_weight], axis=1)
    grad_vectors = jnp.stack(
        [
            jnp.concatenate([grad_bias_query, grad_bias_value, grad_bias_out, grad_bias_down]),
            grad_bias_up,
            jnp.concatenate(
                [grad_gain_first, grad_shift_first, grad_gain_second, grad_shift_second]
            ),
        ]
    )
    attention_share, feedforward_share, vector_share = (
        lax.psum_scatter(grad_attention, ("fsdp", "seq"), scatter_dimension=1, tiled=True),
        lax.psum_scatter(grad_feedforward, ("fsdp", "seq"), scatter_dimension=1, tiled=True),
        lax.psum_scatter(grad_vectors, ("fsdp", "seq"), scatter_dimension=1, tiled=True),
    )
    attention_new, attention_first_new, attention_second_new, attention_low = adamw_update(
        attention_weights,
        attention_share,
        attention_first,
        attention_second,
        rate_attention,
        weight_decay,
    )
    feedforward_new, feedforward_first_new, feedforward_second_new, feedforward_low = adamw_update(
        feedforward_weights,
        feedforward_share,
        feedforward_first,
        feedforward_second,
        rate_feedforward,
        weight_decay,
    )
    vectors_new, vector_first_new, vector_second_new, vectors_low = adamw_update(
        layer_vectors, vector_share, vector_first, vector_second, rate_vectors, 0.0
    )
    return (
        output_rows,
        input_rows,
        pooled,
        stream_rms,
        attention_new,
        attention_first_new,
        attention_second_new,
        attention_low,
        feedforward_new,
        feedforward_first_new,
        feedforward_second_new,
        feedforward_low,
        vectors_new,
        vector_first_new,
        vector_second_new,
        vectors_low,
    )


MESH = pl.DeviceIdType.MESH
F32 = jnp.float32
BF16 = jnp.bfloat16

NZ, NX, NC, NY = 4, 2, 2, 2
ROW = 512
OWN_ROWS = 2
TOKENS = OWN_ROWS * ROW
SHARD_A = 96
SHARD_F = 192
EXTRA = 16
FULL_A = SHARD_A + EXTRA
PIECES = 3
PIECE = SHARD_F // PIECES
BLOCK = FF // PIECES
SPLIT_A = 80
SPLIT_F = 48


def tn_dot(left_side, right_side):
    return contract_rows(left_side, right_side)


def nt_dot(left_side, right_side):
    return contract_columns(left_side, right_side)


def column_sum(value):
    return jnp.sum(value, axis=0, keepdims=True)


def row_mean(value):
    return jnp.mean(value, axis=-1, keepdims=True)


def remote(src, dst, send, recv, where):
    return pltpu.make_async_remote_copy(
        src_ref=src,
        dst_ref=dst,
        send_sem=send,
        recv_sem=recv,
        device_id=where,
        device_id_type=MESH,
    )


class Place:
    def __init__(self):
        f = lax.axis_index("fsdp")
        self.z = f // (NX * NC)
        self.x = (f // NC) % NX
        self.c = f % NC
        self.y = lax.axis_index("seq")

    def at(self, z=None, x=None, c=None, y=None):
        z = self.z if z is None else z
        x = self.x if x is None else x
        c = self.c if c is None else c
        y = self.y if y is None else y
        return ((z * NX + x) * NC + c, y)

    def core(self):
        return self.at(c=1 - self.c)

    def first(self, order):
        return self.at(y=1 - self.y) if order == 0 else self.at(x=1 - self.x)

    def last(self, order):
        return self.at(x=1 - self.x) if order == 0 else self.at(y=1 - self.y)


class Gather:
    def __init__(self, me, buf, start, size, order, index, sems):
        self.me, self.buf, self.order, self.index = me, buf, order, index
        self.rows = pl.ds(start, size)
        self.sems = sems

    def own(self):
        me = self.me
        return self.buf.at[me.z, me.x, me.c, me.y, self.rows]

    def near(self):
        me = self.me
        if self.order == 0:
            return self.buf.at[me.z, me.x, me.c, 1 - me.y, self.rows]
        return self.buf.at[me.z, 1 - me.x, me.c, me.y, self.rows]

    def bundle(self, zz, far):
        me = self.me
        if self.order == 0:
            x = 1 - me.x if far else me.x
            return self.buf.at[zz, x, me.c, :, self.rows]
        y = 1 - me.y if far else me.y
        return self.buf.at[zz, :, me.c, y, self.rows]

    def quad(self, zz, other):
        c = 1 - self.me.c if other else self.me.c
        return self.buf.at[zz, :, c, :, self.rows]

    def first_copy(self, arriving=False):
        s, i = self.sems, self.index
        ref = self.near() if arriving else self.own()
        return remote(ref, ref, s.a_s.at[i], s.a_r.at[i], self.me.first(self.order))

    def line_copy(self, zz, up):
        s, i = self.sems, self.index
        ref = self.bundle(zz, False)
        step = 1 if up else -1
        return remote(
            ref,
            ref,
            (s.up_s if up else s.dn_s).at[i, zz],
            s.z_r.at[i, zz],
            self.me.at(z=self.me.z + step),
        )

    def last_copy(self, zz, arriving=False):
        s, i = self.sems, self.index
        ref = self.bundle(zz, arriving)
        return remote(ref, ref, s.b_s.at[i, zz], s.b_r.at[i, zz], self.me.last(self.order))

    def core_copy(self, zz, arriving=False):
        s, i = self.sems, self.index
        ref = self.quad(zz, arriving)
        return remote(ref, ref, s.c_s.at[i, zz], s.c_r.at[i, zz], self.me.core())

    def both_ways(self, step, act):
        z = self.me.z

        @pl.when(z - step >= 0)
        def _():
            act(z - step, True)

        @pl.when(z + step <= NZ - 1)
        def _():
            act(z + step, False)

    def send_line(self, zz, up):
        z = self.me.z
        if up:

            @pl.when(z < NZ - 1)
            def _():
                self.line_copy(zz, True).start()

        else:

            @pl.when(z > 0)
            def _():
                self.line_copy(zz, False).start()

    def start(self):
        self.first_copy().start()

    def spread(self):
        self.first_copy(True).wait_recv()
        z = self.me.z
        self.send_line(z, True)
        self.send_line(z, False)
        self.last_copy(z).start()

    def line(self, step):
        def act(zz, up):
            self.line_copy(zz, up).wait_recv()
            self.send_line(zz, up)
            self.last_copy(zz).start()

        self.both_ways(step, act)

    def cross(self, step):
        def act(zz, up):
            self.last_copy(zz, True).wait_recv()
            self.core_copy(zz).start()

        if step == 0:
            act(self.me.z, True)
        else:
            self.both_ways(step, act)

    def finish(self):
        for zz in range(NZ):
            self.core_copy(zz, True).wait_recv()

    def drain(self):
        z = self.me.z
        self.first_copy().wait_send()
        for zz in range(NZ):
            self.last_copy(zz).wait_send()
            self.core_copy(zz).wait_send()

            @pl.when((zz <= z) & (z < NZ - 1))
            def _():
                self.line_copy(zz, True).wait_send()

            @pl.when((zz >= z) & (z > 0))
            def _():
                self.line_copy(zz, False).wait_send()


class Scatter:
    def __init__(self, me, buf, start, size, order, index, sems, landing, out, slot):
        self.me, self.buf, self.order, self.index = me, buf, order, index
        self.rows = pl.ds(start, size)
        self.sems = sems
        self.rc, self.rb, self.rz, self.ra = landing
        self.out = out
        self.slot = pl.ds(slot, size)

    def part(self, zz, far, other=False):
        me = self.me
        c = 1 - me.c if other else me.c
        if self.order == 0:
            return self.buf.at[zz, 1 - me.x if far else me.x, c, :, self.rows]
        return self.buf.at[zz, :, c, 1 - me.y if far else me.y, self.rows]

    def planes(self, far, other):
        me = self.me
        c = 1 - me.c if other else me.c
        if self.order == 0:
            return self.buf.at[:, 1 - me.x if far else me.x, c, :, self.rows]
        return self.buf.at[:, :, c, 1 - me.y if far else me.y, self.rows]

    def got_core(self, far, zz=None):
        half = 1 if far else 0
        if zz is None:
            return self.rc.at[half, :, :, self.slot]
        return self.rc.at[half, zz, :, self.slot]

    def core_copy(self, far):
        s, i = self.sems, self.index
        half = 1 if far else 0
        return remote(
            self.planes(far, True),
            self.got_core(far),
            s.rc_s.at[i, half],
            s.rc_r.at[i, half],
            self.me.core(),
        )

    def last_copy(self, zz):
        s, i = self.sems, self.index
        return remote(
            self.part(zz, True),
            self.rb.at[zz],
            s.rb_s.at[i, zz],
            s.rb_r.at[i, zz],
            self.me.last(self.order),
        )

    def line_slot(self, zz, at, down):
        return zz if down else jnp.where(zz == at, NZ, zz)

    def line_copy(self, zz, down):
        s, i = self.sems, self.index
        to = self.me.z - 1 if down else self.me.z + 1
        slot = self.line_slot(zz, to, down)
        return remote(
            self.part(zz, False),
            self.rz.at[slot],
            s.rz_s.at[i, zz],
            s.rz_r.at[i, slot],
            self.me.at(z=to),
        )

    def line_wait(self, slot):
        s, i = self.sems, self.index
        remote(
            self.rz.at[slot],
            self.rz.at[slot],
            s.rz_s.at[i, 0],
            s.rz_r.at[i, slot],
            self.me.core(),
        ).wait_recv()

    def home(self, mine):
        me = self.me
        if self.order == 0:
            y = me.y if mine else 1 - me.y
            return self.buf.at[me.z, me.x, me.c, y, self.rows], y
        x = me.x if mine else 1 - me.x
        return self.buf.at[me.z, x, me.c, me.y, self.rows], x

    def first_copy(self):
        s, i = self.sems, self.index
        return remote(
            self.home(False)[0],
            self.ra,
            s.ra_s.at[i],
            s.ra_r.at[i],
            self.me.first(self.order),
        )

    def by_distance(self, dist, act):
        z = self.me.z
        if dist == 0:
            act(z, True)
            return

        @pl.when(z - dist >= 0)
        def _():
            act(z - dist, True)

        @pl.when(z + dist <= NZ - 1)
        def _():
            act(z + dist, False)

    def start(self):
        self.core_copy(True).start()
        self.core_copy(False).start()

    def cross(self):
        self.core_copy(True).wait_recv()
        for dist in range(NZ - 1, -1, -1):

            def act(zz, down):
                ref = self.part(zz, True)
                got = self.got_core(True, zz)
                ref[...] = (ref[...].astype(F32) + got[...].astype(F32)).astype(BF16)
                self.last_copy(zz).start()

            self.by_distance(dist, act)

    def keep(self):
        self.core_copy(False).wait_recv()
        for zz in range(NZ):
            ref = self.part(zz, False)
            got = self.got_core(False, zz)
            ref[...] = (ref[...].astype(F32) + got[...].astype(F32)).astype(BF16)

    def line(self, dist):
        z = self.me.z

        def act(zz, down):
            self.last_copy(zz).wait_recv()
            ref = self.part(zz, False)
            outer = z < NZ - 1 if down else z > 0
            total = ref[...].astype(F32) + self.rb[zz].astype(F32)

            @pl.when(outer)
            def _():
                self.line_wait(zz)
                ref[...] = (total + self.rz[zz].astype(F32)).astype(BF16)

            @pl.when(jnp.logical_not(outer))
            def _():
                ref[...] = total.astype(BF16)

            self.line_copy(zz, down).start()

        self.by_distance(dist, act)

    def settle(self):
        z = self.me.z
        self.last_copy(z).wait_recv()
        far_ref, far = self.home(False)
        near_ref, near = self.home(True)
        self.out[self.rows, :] = near_ref[...].astype(F32) + self.rb[z, near].astype(F32)
        total = far_ref[...].astype(F32) + self.rb[z, far].astype(F32)

        @pl.when(z == 0)
        def _():
            self.line_wait(z)
            far_ref[...] = (total + self.rz[z, far].astype(F32)).astype(BF16)
            self.out[self.rows, :] += self.rz[z, near].astype(F32)

        @pl.when(z == NZ - 1)
        def _():
            self.line_wait(NZ)
            far_ref[...] = (total + self.rz[NZ, far].astype(F32)).astype(BF16)
            self.out[self.rows, :] += self.rz[NZ, near].astype(F32)

        @pl.when((z > 0) & (z < NZ - 1))
        def _():
            self.line_wait(z)
            self.line_wait(NZ)
            far_ref[...] = (
                total + (self.rz[z, far].astype(F32) + self.rz[NZ, far].astype(F32))
            ).astype(BF16)
            self.out[self.rows, :] += self.rz[z, near].astype(F32) + self.rz[NZ, near].astype(
                F32
            )

        self.first_copy().start()

    def finish(self):
        self.first_copy().wait_recv()
        self.out[self.rows, :] += self.ra[...].astype(F32)

    def drain(self):
        z = self.me.z
        self.core_copy(True).wait_send()
        self.core_copy(False).wait_send()
        self.first_copy().wait_send()
        for zz in range(NZ):
            self.last_copy(zz).wait_send()

            @pl.when(zz < z)
            def _():
                self.line_copy(zz, True).wait_send()

            @pl.when(zz > z)
            def _():
                self.line_copy(zz, False).wait_send()


class Queue:
    def __init__(self):
        self.events = []
        self.done = 0

    def add(self, *events):
        self.events.extend(events)

    def mark(self):
        return len(self.events)

    def take(self, count):
        some = self.events[self.done : self.done + count]
        self.done += len(some)

        def run():
            for event in some:
                event()

        return run if some else None

    def tick(self, count=1):
        run = self.take(count)
        if run is not None:
            run()

    def until(self, mark):
        if mark > self.done:
            self.tick(mark - self.done)

    def loop(self, count, body, each=1):
        runs = [self.take(each) for _ in range(count)]

        @pl.loop(0, count)
        def _(i):
            body(i)
            for place, run in enumerate(runs):
                if run is not None:
                    pl.when(i == place)(run)


def repeat(count, body):
    pl.loop(0, count)(body)


def flatten(value):
    return value.reshape(-1, value.shape[-1])


def attention_pair(queries, keys, values, bias):
    first = lax.broadcasted_iota(jnp.int32, keys.shape, 1) < HEAD_DIM
    zero = jnp.zeros((), BF16)
    values_turned = values.T
    contexts, totals = [], []
    for half in range(2):
        keys_half = jnp.where(first if half == 0 else ~first, keys, zero)
        scores = nt_dot(keys_half, queries) + bias
        largest = jnp.max(scores, axis=0, keepdims=True)
        exponent = jnp.exp(scores - largest)
        total = column_sum(exponent)
        soft = (exponent * (1.0 / total)).astype(BF16)
        contexts.append(
            plain_dot(values_turned[half * HEAD_DIM : (half + 1) * HEAD_DIM, :], soft)
        )
        totals.append(largest + jnp.log(total))
    return jnp.concatenate(contexts, 0).T, jnp.concatenate(totals, 0)


def attention_pair_back(queries, keys, values, grad_context, bias, log_total):
    first = lax.broadcasted_iota(jnp.int32, keys.shape, 1) < HEAD_DIM
    zero = jnp.zeros((), BF16)
    keys_turned = keys.T
    grad_queries = []
    grad_keys = grad_values = 0.0
    for half in range(2):
        mask = first if half == 0 else ~first
        scores = nt_dot(jnp.where(mask, keys, zero), queries) + bias
        soft = jnp.exp(scores - log_total[half : half + 1, :])
        grad_soft = nt_dot(jnp.where(mask, values, zero), grad_context)
        inner = column_sum(soft * grad_soft)
        grad_scores = (soft * (grad_soft - inner)).astype(BF16)
        grad_values += plain_dot(soft.astype(BF16), jnp.where(mask, grad_context, zero))
        grad_keys += plain_dot(grad_scores, jnp.where(mask, queries, zero))
        grad_queries.append(
            plain_dot(keys_turned[half * HEAD_DIM : (half + 1) * HEAD_DIM, :], grad_scores)
        )
    return jnp.concatenate(grad_queries, 0).T, grad_keys, grad_values


def select_columns(permuted):
    row = lax.broadcasted_iota(jnp.int32, (8 * 128, D), 0)
    col = lax.broadcasted_iota(jnp.int32, (8 * 128, D), 1)
    lane = row % 128
    source = (row // 128) * SHARD_A + lane
    if permuted:
        piece = col // 256
        rest = col % 256
        col = (rest // PIECE) * SHARD_F + piece * PIECE + rest % PIECE
    return jnp.where((source == col) & (lane < SHARD_A), 1.0, 0.0).astype(BF16)


SEM_SHAPES = dict(
    a_s=(8,),
    a_r=(8,),
    z_r=(8, NZ),
    up_s=(8, NZ),
    dn_s=(8, NZ),
    b_s=(8, NZ),
    b_r=(8, NZ),
    c_s=(8, NZ),
    c_r=(8, NZ),
    rc_s=(10, 2),
    rc_r=(10, 2),
    rb_s=(10, NZ),
    rb_r=(10, NZ),
    rz_s=(10, NZ),
    rz_r=(10, NZ + 1),
    ra_s=(10,),
    ra_r=(10,),
    x_s=(4, 2),
    x_r=(4, 2),
    own=(4, 2),
    pool_s=(1,),
    pool_r=(1,),
    stat_s=(5,),
    stat_r=(5,),
    load=(3,),
)


def gather_pieces():
    return [(0, SPLIT_A, FULL_A - SPLIT_A)] + [
        (k * PIECE, SPLIT_F, PIECE - SPLIT_F) for k in range(PIECES)
    ]


def scatter_pieces():
    return gather_pieces()[1:] + [
        (0, SPLIT_F, PIECE - SPLIT_F),
        (PIECE, FULL_A - 2 * PIECE + SPLIT_F, PIECE - SPLIT_F),
    ]


def scratch():
    return dict(
        wa=pltpu.VMEM((NZ, NX, NC, NY, FULL_A, D), BF16),
        wf=pltpu.VMEM((NZ, NX, NC, NY, SHARD_F, D), BF16),
        rc=pltpu.VMEM((2, NZ, 2, PIECE, D), BF16),
        xs=pltpu.VMEM((TOKENS, D), BF16),
        dys=pltpu.VMEM((TOKENS, D), BF16),
        ctx=pltpu.VMEM((TOKENS, D), BF16),
        n1=pltpu.VMEM((TOKENS, D), BF16),
        fn=pltpu.VMEM((TOKENS, D), BF16),
        fg=pltpu.VMEM((TOKENS, D), BF16),
        qkv=pltpu.VMEM((TOKENS, 3 * D), BF16),
        act=pltpu.VMEM((PIECES, TOKENS, BLOCK), BF16),
        slope=pltpu.VMEM((PIECES, TOKENS, BLOCK), BF16),
        acc=pltpu.VMEM((TOKENS, D), F32),
        bias=pltpu.VMEM((OWN_ROWS, ROW, ROW), BF16),
        totals=pltpu.VMEM((OWN_ROWS * HEADS // 2, 2, ROW), F32),
        side=pltpu.VMEM((TOKENS, 128), F32),
        vec=pltpu.VMEM((16, 4 * D), F32),
        bu=pltpu.VMEM((PIECES, 16, BLOCK), F32),
        gvec=pltpu.VMEM((8, 4 * D), F32),
        gbu=pltpu.VMEM((PIECES, 8, BLOCK), F32),
        stat=pltpu.VMEM((8, 128), F32),
        stat_in=pltpu.VMEM((5, 8, 128), F32),
        pool_out=pltpu.VMEM((OWN_ROWS, 8, D), F32),
        pool_in=pltpu.VMEM((OWN_ROWS, 8, D // 2), F32),
        credit=pltpu.SemaphoreType.REGULAR,
        free=pltpu.SemaphoreType.REGULAR,
    )


def landing_shapes():
    shapes = []
    for _ in range(PIECES):
        for size in (SPLIT_F, PIECE - SPLIT_F):
            shapes += [
                pltpu.VMEM((NZ, 2, size, D), BF16),
                pltpu.VMEM((NZ + 1, 2, size, D), BF16),
                pltpu.VMEM((size, D), BF16),
            ]
    return shapes


def fused_kernel(
    x_in,
    dy_in,
    wa_in,
    wf_in,
    ids,
    flags,
    flag_column,
    out_y,
    out_dx,
    out_pooled,
    out_stats,
    grad_a,
    grad_f,
    *more,
):
    names, sem_names = tuple(scratch()), tuple(SEM_SHAPES)
    landings = len(landing_shapes())
    r = types.SimpleNamespace(**dict(zip(names, more)))
    landing_refs = more[len(names) : len(names) + landings]
    sems = types.SimpleNamespace(**dict(zip(sem_names, more[len(names) + landings :])))
    me = Place()
    z, x, c, y = me.z, me.x, me.c, me.y
    wa, wf, xs, dys, ctx = r.wa, r.wf, r.xs, r.dys, r.ctx
    n1, fn, fg, qkv, acc = r.n1, r.fn, r.fg, r.qkv, r.acc
    act, slope, vec, gvec, stat = r.act, r.slope, r.vec, r.gvec, r.stat

    def tile(i, size):
        return pl.ds(pl.multiple_of(i * size, size), size)

    def vector(row, quarter):
        return vec[row : row + 1, quarter * D : (quarter + 1) * D]

    barrier = pltpu.get_barrier_semaphore()
    for where in (
        me.core(),
        me.at(x=1 - x),
        me.at(y=1 - y),
        me.at(z=(z + 2) % NZ),
    ):
        pl.semaphore_signal(barrier, inc=1, device_id=where, device_id_type=MESH)

    @pl.when(z > 0)
    def _():
        pl.semaphore_signal(barrier, inc=1, device_id=me.at(z=z - 1), device_id_type=MESH)

    @pl.when(z < NZ - 1)
    def _():
        pl.semaphore_signal(barrier, inc=1, device_id=me.at(z=z + 1), device_id_type=MESH)

    load_a = pltpu.make_async_copy(wa_in, wa.at[z, x, c, y], sems.load.at[0])
    load_f = pltpu.make_async_copy(wf_in, wf.at[z, x, c, y], sems.load.at[1])
    load_s = pltpu.make_async_copy(flag_column, r.side, sems.load.at[2])
    load_a.start()
    load_f.start()
    load_s.start()

    def row_copy(kind, src, dst, slot):
        return remote(
            src, dst, sems.x_s.at[kind, slot], sems.x_r.at[kind, slot], me.at(y=1 - y)
        )

    def own_copy(kind, src, dst, slot):
        return pltpu.make_async_copy(src, dst, sems.own.at[kind, slot])

    def span(slot, half):
        return pl.ds(pl.multiple_of(slot * ROW + half * (ROW // 2), ROW // 2), ROW // 2)

    def take_rows(kind, source, target):
        sends = [
            row_copy(kind, source.at[2 * (1 - y) + slot], target.at[span(slot, y)], slot)
            for slot in range(OWN_ROWS)
        ]
        owns = [
            own_copy(kind, source.at[2 * y + slot], target.at[span(slot, y)], slot)
            for slot in range(OWN_ROWS)
        ]
        arrivals = [
            row_copy(kind, source.at[2 * y + slot], target.at[span(slot, 1 - y)], slot)
            for slot in range(OWN_ROWS)
        ]
        return sends, owns, arrivals

    def give_rows(kind, source, target):
        sends = [
            row_copy(kind, source.at[span(slot, 1 - y)], target.at[2 * y + slot], slot)
            for slot in range(OWN_ROWS)
        ]
        owns = [
            own_copy(kind, source.at[span(slot, y)], target.at[2 * y + slot], slot)
            for slot in range(OWN_ROWS)
        ]
        arrivals = [
            row_copy(kind, source.at[span(slot, y)], target.at[2 * (1 - y) + slot], slot)
            for slot in range(OWN_ROWS)
        ]
        return sends, owns, arrivals

    x_sends, x_owns, x_arrivals = take_rows(0, x_in, xs)
    dy_sends, dy_owns, dy_arrivals = take_rows(1, dy_in, dys)
    out_sends, out_owns, out_arrivals = give_rows(2, dys, out_y)
    dx_sends, dx_owns, dx_arrivals = give_rows(3, n1, out_dx)

    def start_all(copies):
        def run():
            for copy in copies:
                copy.start()

        return run

    gathers, scatters = [], []
    for piece, (first_row, *sizes) in enumerate(gather_pieces()):
        buf = wa if piece == 0 else wf
        starts = (first_row, first_row + sizes[0])
        gathers.append(
            [
                Gather(me, buf, starts[order], sizes[order], order, 2 * piece + order, sems)
                for order in range(2)
            ]
        )
    for piece, (first_row, *sizes) in enumerate(scatter_pieces()):
        out = grad_f if piece < PIECES else grad_a
        pair = []
        for order in range(2):
            size, i = sizes[order], 2 * (piece % PIECES) + order
            landing = (
                r.rc,
                landing_refs[3 * i].at[:, :, 0:size],
                landing_refs[3 * i + 1].at[:, :, 0:size],
                landing_refs[3 * i + 2].at[0:size],
            )
            slot = order * sizes[0]
            pair.append(
                Scatter(
                    me, wf, first_row + slot, size, order, 2 * piece + order, sems, landing, out,
                    slot,
                )
            )
        scatters.append(pair)

    def both(pair, method, *args):
        def run():
            for one in pair:
                method(one, *args)

        return run

    queue = Queue()
    att, later = gathers[0], gathers[1:]

    def enter():
        load_a.wait()
        pl.semaphore_wait(
            barrier,
            4 + jnp.where(z > 0, 1, 0).astype(jnp.int32) + jnp.where(z < NZ - 1, 1, 0).astype(
                jnp.int32
            ),
        )

    def enter_f():
        load_f.wait()

    queue.add(
        enter,
        both(att, Gather.start),
        start_all(x_sends + x_owns),
        enter_f,
        *[both(pair, Gather.start) for pair in later],
        both(att, Gather.spread),
        start_all(dy_owns),
        both(att, Gather.line, 1),
        both(att, Gather.cross, 0),
        both(att, Gather.line, 2),
        both(att, Gather.cross, 1),
        both(att, Gather.line, 3),
        both(later[0], Gather.spread),
        both(att, Gather.cross, 2),
        both(att, Gather.cross, 3),
        both(later[0], Gather.line, 1),
        both(att, Gather.finish),
    )
    marks = [queue.mark()]
    for k, pair in enumerate(later):
        queue.add(
            both(pair, Gather.cross, 0),
            both(pair, Gather.line, 2),
            both(pair, Gather.cross, 1),
            both(pair, Gather.line, 3),
        )
        if k == 0:
            queue.add(start_all(dy_sends))
        if k + 1 < PIECES:
            queue.add(both(later[k + 1], Gather.spread))
        queue.add(both(pair, Gather.cross, 2), both(pair, Gather.cross, 3))
        if k + 1 < PIECES:
            queue.add(both(later[k + 1], Gather.line, 1))
        queue.add(both(pair, Gather.finish))
        marks.append(queue.mark())

    queue.tick(8)

    gvec[...] = jnp.zeros_like(gvec)
    r.gbu[...] = jnp.zeros_like(r.gbu)
    stat[...] = jnp.zeros_like(stat)
    for slot in range(OWN_ROWS):
        wide = jnp.broadcast_to(ids[slot].astype(F32), (128, ROW))
        tall = wide.T
        for j in range(ROW // 128):
            across = wide[:, j * 128 : (j + 1) * 128]
            across = jnp.broadcast_to(across[0:1, :], (ROW, 128))
            r.bias[slot, :, j * 128 : (j + 1) * 128] = jnp.where(
                tall == across, 0.0, masked_score
            ).astype(BF16)
    queue.until(marks[0])

    ctx[...] = select_columns(False)
    fg[...] = select_columns(True)
    for q in range(4):
        blocks = jnp.concatenate(
            [
                wa[q, j // 4, (j // 2) % 2, j % 2, SHARD_A:FULL_A, 0:128]
                for j in range(8)
            ],
            axis=1,
        )
        vec[:, q * D : (q + 1) * D] = plain_dot(blocks, ctx[...])
        moved = plain_dot(blocks, fg[...])
        for k in range(PIECES):
            r.bu[k, :, q * 256 : (q + 1) * 256] = moved[:, k * 256 : (k + 1) * 256]

    load_s.wait()
    for copy in x_owns:
        copy.wait()
    for copy in x_arrivals:
        copy.wait_recv()

    scale = HEAD_DIM ** (-0.5)

    def project(i):
        rows = tile(i, 512)
        tokens = xs[rows, :]
        wide = tokens.astype(F32)
        stat[0:1, :] += lane_sums(wide * wide * r.side[rows, 1:2])
        for j in range(3):
            weights = flatten(wa[j, :, :, :, 0:SHARD_A, :])
            value = nt_dot(tokens, weights)
            if j == 0:
                value = (value + vector(0, 0)) * scale
            if j == 2:
                value = value + vector(0, 1)
            qkv[rows, j * D : (j + 1) * D] = value.astype(BF16)

    def lane_sums(value):
        total = column_sum(value)
        return sum(total[:, j * 128 : (j + 1) * 128] for j in range(D // 128))

    queue.loop(2, project)

    def columns(pair, block):
        return pl.ds(pl.multiple_of(block * D + pair * 128, 128), 128)

    def attend(i):
        slot, pair = i // (HEADS // 2), i % (HEADS // 2)
        rows = tile(slot, ROW)
        context, total = attention_pair(
            qkv[rows, columns(pair, 0)],
            qkv[rows, columns(pair, 1)],
            qkv[rows, columns(pair, 2)],
            r.bias[slot].astype(F32),
        )
        ctx[rows, columns(pair, 0)] = context.astype(BF16)
        r.totals[i] = total

    queue.loop(OWN_ROWS * HEADS // 2, attend)

    def attention_output(i):
        rows = tile(i, 256)
        weights = flatten(wa[3, :, :, :, 0:SHARD_A, :])
        out = nt_dot(ctx[rows, :], weights) + vector(0, 2)
        stat[1:2, :] += lane_sums(out * out * r.side[rows, 1:2])
        normed, inverse = normalize(xs[rows, :].astype(F32) + out)
        n1[rows, :] = normed.astype(BF16)
        r.side[rows, 0:1] = inverse
        fn[rows, :] = (normed * vector(2, 0) + vector(2, 1)).astype(BF16)

    queue.loop(4, attention_output)

    def up_rows(k):
        return flatten(flatten_lead(wf[0:2, :, :, :, k * PIECE : (k + 1) * PIECE, :]))

    def down_rows(k):
        return flatten(flatten_lead(wf[2:4, :, :, :, k * PIECE : (k + 1) * PIECE, :]))

    def flatten_lead(value):
        return value.reshape(-1, PIECE, D)

    for k in range(PIECES):
        queue.until(marks[k + 1])

        def feed(i, k=k):
            rows = tile(i, 512)
            up = nt_dot(fn[rows, :], up_rows(k)) + r.bu[k, 1:2, :]
            half = 0.5 * (1.0 + lax.erf(up * math.sqrt(0.5)))
            activated = (up * half).astype(BF16)
            act[k, rows, :] = activated
            slope[k, rows, :] = (
                half + up * (jnp.exp(-0.5 * up * up) * (1.0 / math.sqrt(2.0 * math.pi)))
            ).astype(BF16)
            value = plain_dot(activated, down_rows(k))
            if k == 0:
                acc[rows, :] = value
            else:
                acc[rows, :] += value

        queue.loop(2, feed)
    queue.until(queue.mark())

    for copy in dy_owns:
        copy.wait()
    for copy in dy_arrivals:
        copy.wait_recv()
    for pair in gathers:
        for one in pair:
            one.drain()

    def second(i):
        rows = tile(i, 128)
        feed_out = acc[rows, :] + vector(0, 3)
        stat[2:3, :] += lane_sums(feed_out * feed_out * r.side[rows, 1:2])
        normed, inverse = normalize(fn[rows, :].astype(F32) + feed_out)
        grad = dys[rows, :].astype(F32)
        dys[rows, :] = (normed * vector(2, 2) + vector(2, 3)).astype(BF16)
        gvec[2:3, 2 * D : 3 * D] += column_sum(grad * normed)
        gvec[2:3, 3 * D :] += column_sum(grad)
        back = norm_back(grad * vector(2, 2), normed, inverse)
        acc[rows, :] = back
        low = back.astype(BF16)
        fg[rows, :] = low
        gvec[0:1, 3 * D :] += column_sum(low.astype(F32))

    repeat(TOKENS // 128, second)

    start_all(out_sends + out_owns)()

    segments = lax.broadcasted_iota(jnp.int32, (SEGMENTS, ROW), 0)
    for slot in range(OWN_ROWS):
        member = jnp.where(segments == ids[slot], 1.0, 0.0) * flags[slot]
        sums = plain_dot(member.astype(BF16), dys[slot * ROW : (slot + 1) * ROW, :])
        counts = jnp.sum(member, axis=1, keepdims=True)
        r.pool_out[slot] = sums / jnp.maximum(counts, 1.0)
        total = flags[slot]
        stat[3:4, :] += sum(total[:, j * 128 : (j + 1) * 128] for j in range(ROW // 128))

    def half_lanes(which):
        return pl.ds(pl.multiple_of(which * (D // 2), 128), D // 2)

    pool_copy = remote(
        r.pool_out.at[:, :, half_lanes(1 - y)],
        r.pool_in,
        sems.pool_s.at[0],
        sems.pool_r.at[0],
        me.at(y=1 - y),
    )
    pool_copy.start()

    stat_partners = [
        me.core(),
        me.at(x=1 - x),
        me.at(y=1 - y),
        me.at(z=z + 1 - 2 * (z % 2)),
        me.at(z=(z + 2) % NZ),
    ]

    def stat_copy(step):
        return remote(
            stat,
            r.stat_in.at[step],
            sems.stat_s.at[step],
            sems.stat_r.at[step],
            stat_partners[step],
        )

    def stat_start(step):
        return lambda: stat_copy(step).start()

    def stat_end(step):
        def run():
            stat_copy(step).wait()
            stat[...] += r.stat_in[step]

        return run

    back = Queue()
    credit = r.credit

    def core_start(pair, wait):
        def run():
            if wait:
                pl.semaphore_wait(credit, 1)
            for one in pair:
                one.start()

        return run

    def core_keep(pair, signal):
        def run():
            for one in pair:
                one.keep()
            if signal:
                pl.semaphore_signal(credit, inc=1, device_id=me.core(), device_id_type=MESH)

        return run

    def scatter_events(n):
        pair = scatters[n]
        return [
            core_start(pair, n > 0),
            both(pair, Scatter.cross),
            core_keep(pair, n + 1 < len(scatters)),
            both(pair, Scatter.line, 3),
            both(pair, Scatter.line, 2),
            both(pair, Scatter.line, 1),
            both(pair, Scatter.settle),
            both(pair, Scatter.finish),
        ]

    back.add(stat_start(0))
    for k in range(PIECES):

        def feed_back(i, k=k):
            rows = tile(i, 512)
            grad = nt_dot(fg[rows, :], down_rows(k)) * slope[k, rows, :].astype(F32)
            low = grad.astype(BF16)
            slope[k, rows, :] = low
            r.gbu[k, 0:1, :] += column_sum(low.astype(F32))
            acc[rows, :] += plain_dot(low, up_rows(k))

        back.loop(2, feed_back)

        def weights_back(i, k=k):
            cols = tile(i, BLOCK // 2)
            down = tn_dot(act[k, :, cols], fg[...]).astype(BF16)
            up = tn_dot(slope[k, :, cols], fn[...]).astype(BF16)
            where = (slice(None), slice(None), slice(None), pl.ds(k * PIECE, PIECE))
            wf[(2 + i, *where)] = down.reshape(NX, NC, NY, PIECE, D)
            wf[(i, *where)] = up.reshape(NX, NC, NY, PIECE, D)

        back.loop(2, weights_back)
        back.add(*scatter_events(k))
        if k < 2:
            back.add(stat_end(2 * k), stat_start(2 * k + 1), stat_end(2 * k + 1), stat_start(2 * k + 2))
        else:
            back.add(stat_end(4))

    def first(i):
        rows = tile(i, 128)
        grad = acc[rows, :]
        normed = n1[rows, :].astype(F32)
        gvec[2:3, 0:D] += column_sum(grad * normed)
        gvec[2:3, D : 2 * D] += column_sum(grad)
        stream = norm_back(grad * vector(2, 0), normed, r.side[rows, 0:1])
        acc[rows, :] = stream
        low = stream.astype(BF16)
        fg[rows, :] = low
        gvec[0:1, 2 * D : 3 * D] += column_sum(low.astype(F32))

    back.loop(TOKENS // 128, first, 0)

    def context_back(i):
        rows = tile(i, 512)
        fn[rows, :] = plain_dot(fg[rows, :], flatten(wa[3, :, :, :, 0:SHARD_A, :])).astype(BF16)

    back.loop(2, context_back)

    def attend_back_pair(i):
        slot, pair = i // (HEADS // 2), i % (HEADS // 2)
        rows = tile(slot, ROW)
        grads = attention_pair_back(
            qkv[rows, columns(pair, 0)],
            qkv[rows, columns(pair, 1)],
            qkv[rows, columns(pair, 2)],
            fn[rows, columns(pair, 0)],
            r.bias[slot].astype(F32),
            r.totals[i],
        )
        for j in range(3):
            low = grads[j].astype(BF16)
            if j == 0:
                low = low * jnp.asarray(scale, BF16)
            qkv[rows, columns(pair, j)] = low
            if j != 1:
                gvec[0:1, columns(pair, j // 2)] += column_sum(low.astype(F32))

    back.loop(OWN_ROWS * HEADS // 2, attend_back_pair, 2)
    back.until(back.mark())
    for pair in scatters[:PIECES]:
        for one in pair:
            one.drain()

    free = r.free
    for where in (me.at(x=1 - x), me.at(y=1 - y)):
        pl.semaphore_signal(free, inc=1, device_id=where, device_id_type=MESH)

    @pl.when(z > 0)
    def _():
        pl.semaphore_signal(free, inc=1, device_id=me.at(z=z - 1), device_id_type=MESH)

    @pl.when(z < NZ - 1)
    def _():
        pl.semaphore_signal(free, inc=1, device_id=me.at(z=z + 1), device_id_type=MESH)

    for j in range(3):

        def inner_back(i, j=j):
            cols = pl.ds(pl.multiple_of(j * D + i * (D // 2), 128), D // 2)
            value = tn_dot(qkv[:, cols], xs[...]).astype(BF16)
            wf[j, i, :, :, 0:SHARD_A, :] = value.reshape(NC, NY, SHARD_A, D)

        repeat(2, inner_back)

    def outer_back(i):
        cols = pl.ds(pl.multiple_of(i * (D // 2), 128), D // 2)
        value = tn_dot(fg[:, cols], ctx[...]).astype(BF16)
        wf[3, i, :, :, 0:SHARD_A, :] = value.reshape(NC, NY, SHARD_A, D)

    repeat(2, outer_back)

    ctx[...] = select_columns(False)
    fg[...] = select_columns(True)
    row = lax.broadcasted_iota(jnp.int32, (8, 1), 0)
    for q in range(4):
        plain = nt_dot(gvec[:, q * D : (q + 1) * D].astype(BF16), ctx[...])
        piled = jnp.concatenate(
            [r.gbu[k, :, q * 256 : (q + 1) * 256] for k in range(PIECES)], axis=1
        )
        moved = nt_dot(piled.astype(BF16), fg[...])
        low = jnp.where(row == 1, jnp.broadcast_to(moved[0:1, :], plain.shape), plain)
        low = jnp.concatenate([low, jnp.zeros_like(low)], axis=0).astype(BF16)
        for j in range(8):
            wf[q, j // 4, (j // 2) % 2, j % 2, SHARD_A:FULL_A, 0:128] = low[
                :, j * 128 : (j + 1) * 128
            ]
    line_ends = jnp.where(z > 0, 1, 0).astype(jnp.int32) + jnp.where(z < NZ - 1, 1, 0).astype(
        jnp.int32
    )
    pl.semaphore_wait(free, 2 + line_ends)
    early, late = scatter_events(PIECES), scatter_events(PIECES + 1)
    back.add(*early[:3], *late[:2], early[3], late[2])
    for k in range(3, 7):
        back.add(early[k + 1], late[k])
    back.add(late[7])
    back.tick(1)

    def input_back(i):
        rows = tile(i, 512)
        value = acc[rows, :]
        for j in range(3):
            value += plain_dot(
                qkv[rows, j * D : (j + 1) * D], flatten(wa[j, :, :, :, 0:SHARD_A, :])
            )
        n1[rows, :] = value.astype(BF16)

    back.loop(2, input_back)
    start_all(dx_sends + dx_owns)()
    back.until(back.mark())

    for pair in scatters[PIECES:]:
        for one in pair:
            one.drain()
    pool_copy.wait()
    for slot in range(OWN_ROWS):
        out_pooled[2 * y + slot] = r.pool_out[slot, :, half_lanes(y)]
        out_pooled[2 * (1 - y) + slot] = r.pool_in[slot]
    out_stats[...] = stat[...]
    for copies in (x_sends, dy_sends, out_sends, dx_sends):
        for copy in copies:
            copy.wait_send()
    for copies in (out_owns, dx_owns):
        for copy in copies:
            copy.wait()
    for copies in (out_arrivals, dx_arrivals):
        for copy in copies:
            copy.wait_recv()


def fused_call(inputs, output_grad, attention_low, feedforward_low, ids, flags, flag_column):
    row_count, local_span, width = inputs.shape
    any_space = pl.BlockSpec(memory_space=pl.ANY)
    vmem = pl.BlockSpec(memory_space=pltpu.VMEM)
    semaphores = [pltpu.SemaphoreType.DMA(shape) for shape in SEM_SHAPES.values()]
    return pl.pallas_call(
        fused_kernel,
        out_shape=(
            jax.ShapeDtypeStruct(inputs.shape, BF16),
            jax.ShapeDtypeStruct(inputs.shape, BF16),
            jax.ShapeDtypeStruct((row_count, SEGMENTS, D // NY), F32),
            jax.ShapeDtypeStruct((8, 128), F32),
            jax.ShapeDtypeStruct((FULL_A, D), F32),
            jax.ShapeDtypeStruct((SHARD_F, D), F32),
        ),
        in_specs=[any_space] * 4 + [vmem] * 2 + [any_space],
        out_specs=(any_space, any_space, vmem, vmem, vmem, vmem),
        scratch_shapes=list(scratch().values()) + landing_shapes() + semaphores,
        compiler_params=pltpu.CompilerParams(
            collective_id=0, has_side_effects=True, vmem_limit_bytes=65_000 * 1024
        ),
        name="layer",
    )(inputs, output_grad, attention_low, feedforward_low, ids, flags, flag_column)


def fused_shards(
    inputs,
    segment_ids,
    token_flags,
    output_grad,
    attention_weights,
    feedforward_weights,
    layer_vectors,
    attention_first,
    attention_second,
    feedforward_first,
    feedforward_second,
    vector_first,
    vector_second,
):
    seq = lax.axis_index("seq")
    ids = lax.dynamic_slice_in_dim(segment_ids, seq * OWN_ROWS, OWN_ROWS, 0)
    flags = lax.dynamic_slice_in_dim(token_flags, seq * OWN_ROWS, OWN_ROWS, 0).astype(F32)
    flag_column = jnp.broadcast_to(flags.reshape(TOKENS, 1), (TOKENS, 128))
    vector_rows = jnp.pad(layer_vectors, ((0, EXTRA - 3), (0, D - SHARD_A)))
    attention_low = jnp.concatenate([attention_weights.T, vector_rows], axis=0).astype(BF16)
    feedforward_low = feedforward_weights.T.astype(BF16)
    output_rows, input_rows, pooled, stats, grad_a, grad_f = fused_call(
        inputs,
        output_grad,
        attention_low,
        feedforward_low,
        ids.reshape(OWN_ROWS, 1, ROW),
        flags.reshape(OWN_ROWS, 1, ROW),
        flag_column,
    )
    totals = jnp.sum(stats[0:4], axis=1)
    stream_rms = jnp.sqrt(totals[0:3] / D / totals[3])
    attention_new = adamw_update(
        attention_weights,
        grad_a[0:SHARD_A].T,
        attention_first,
        attention_second,
        rate_attention,
        weight_decay,
    )
    feedforward_new = adamw_update(
        feedforward_weights,
        grad_f.T,
        feedforward_first,
        feedforward_second,
        rate_feedforward,
        weight_decay,
    )
    vectors_new = adamw_update(
        layer_vectors,
        grad_a[SHARD_A : SHARD_A + 3, 0:SHARD_A],
        vector_first,
        vector_second,
        rate_vectors,
        0.0,
    )
    return (
        output_rows,
        input_rows,
        pooled,
        stream_rms,
        *attention_new,
        *feedforward_new,
        *vectors_new,
    )


def solution(mesh):
    fused = mesh.shape["fsdp"] == NZ * NX * NC and mesh.shape["seq"] == NY
    rows = P("fsdp", "seq", None)
    table = P("fsdp", None)
    owned = P(None, ("fsdp", "seq"))
    return jax.shard_map(
        fused_shards if fused else plain_shards,
        mesh=mesh,
        in_specs=(rows, table, table, rows) + (owned,) * 9,
        out_specs=(rows, rows, P("fsdp", None, "seq"), P()) + (owned,) * 12,
        check_vma=False,
    )
```

```python
import functools
import math
import types

import jax
import jax.numpy as jnp
from jax import lax
from jax.experimental import pallas as pl
from jax.experimental.pallas import tpu as pltpu
from jax.sharding import PartitionSpec as P

D = 768
HEADS = 12
HEAD_DIM = 64
FF = 3072
SEGMENTS = 8
STEP = 5


norm_epsilon = 1e-12
adam_epsilon = 1e-08
beta_first = 0.5
beta_second = 0.5
weight_decay = 0.01
rate_attention = 0.04
rate_feedforward = 0.03
rate_vectors = 0.2
masked_score = -1e30


def plain_dot(left_side, right_side):
    return jnp.dot(left_side, right_side, preferred_element_type=jnp.float32)


def contract_rows(left_side, right_side):
    return lax.dot_general(
        left_side, right_side, (((0,), (0,)), ((), ())), preferred_element_type=jnp.float32
    )


def contract_columns(left_side, right_side):
    return lax.dot_general(
        left_side, right_side, (((1,), (1,)), ((), ())), preferred_element_type=jnp.float32
    )


def normalize(stream):
    average = jnp.mean(stream, axis=-1, keepdims=True)
    centered = stream - average
    variance = jnp.mean(centered * centered, axis=-1, keepdims=True)
    inverse = lax.rsqrt(variance + norm_epsilon)
    return (centered * inverse, inverse)


def norm_back(grad_normed, normed, inverse):
    return inverse * (
        grad_normed
        - jnp.mean(grad_normed, axis=-1, keepdims=True)
        - normed * jnp.mean(grad_normed * normed, axis=-1, keepdims=True)
    )


def gelu_slope(value):
    return 0.5 * (1.0 + lax.erf(value * math.sqrt(0.5))) + value * jnp.exp(
        -0.5 * value * value
    ) / math.sqrt(2.0 * math.pi)


def masked_scores(queries, key_part, query_ids, key_ids):
    scores = jnp.einsum("rqhd,rkhd->rhqk", queries, key_part, preferred_element_type=jnp.float32)
    same_segment = query_ids[:, None, :, None] == key_ids[:, None, None, :]
    return jnp.where(same_segment, scores, masked_score)


def attend_block(pieces):
    queries, key_part, value_part, query_ids, key_ids = pieces
    scores = masked_scores(queries, key_part, query_ids, key_ids)
    largest = jnp.max(scores, axis=-1, keepdims=True)
    exponent = jnp.exp(scores - largest)
    denominator = jnp.sum(exponent, axis=-1, keepdims=True)
    soft_weights = (exponent / denominator).astype(jnp.bfloat16)
    context = jnp.einsum(
        "rhqk,rkhd->rqhd", soft_weights, value_part, preferred_element_type=jnp.float32
    )
    return (context, (largest + jnp.log(denominator))[..., 0])


def attend_back(pieces):
    queries, key_part, value_part, query_ids, key_ids, log_total, grad_context = pieces
    scores = masked_scores(queries, key_part, query_ids, key_ids)
    soft_again = jnp.exp(scores - log_total[..., None])
    grad_soft = jnp.einsum(
        "rqhd,rkhd->rhqk", grad_context, value_part, preferred_element_type=jnp.float32
    )
    inner_sum = jnp.sum(soft_again * grad_soft, axis=-1, keepdims=True)
    grad_scores = (soft_again * (grad_soft - inner_sum)).astype(jnp.bfloat16)
    grad_queries = jnp.einsum(
        "rhqk,rkhd->rqhd", grad_scores, key_part, preferred_element_type=jnp.float32
    )
    grad_keys = jnp.einsum(
        "rhqk,rqhd->rkhd", grad_scores, queries, preferred_element_type=jnp.float32
    )
    grad_values = jnp.einsum(
        "rhqk,rqhd->rkhd",
        soft_again.astype(jnp.bfloat16),
        grad_context,
        preferred_element_type=jnp.float32,
    )
    return (grad_queries, grad_keys, grad_values)


def adamw_update(weight, gradient, first_moment, second_moment, step_rate, decay_rate):
    first_new = beta_first * first_moment + (1.0 - beta_first) * gradient
    second_new = beta_second * second_moment + (1.0 - beta_second) * gradient * gradient
    correction_first = 1.0 - beta_first**STEP
    correction_second = 1.0 - beta_second**STEP
    update = (
        first_new / correction_first / (jnp.sqrt(second_new / correction_second) + adam_epsilon)
    )
    weight_new = weight - step_rate * (update + decay_rate * weight)
    return (weight_new, first_new, second_new, weight_new.astype(jnp.bfloat16))


def plain_shards(
    inputs,
    segment_ids,
    token_flags,
    output_grad,
    attention_weights,
    feedforward_weights,
    layer_vectors,
    attention_first,
    attention_second,
    feedforward_first,
    feedforward_second,
    vector_first,
    vector_second,
):
    row_count, local_span, model_width = inputs.shape
    full_length = segment_ids.shape[1]
    score_scale = HEAD_DIM ** (-0.5)
    inputs_here, grad_here = (inputs, output_grad)
    offset = lax.axis_index("seq") * local_span
    query_ids = lax.dynamic_slice_in_dim(segment_ids, offset, local_span, 1)
    work_flags = lax.dynamic_slice_in_dim(token_flags, offset, local_span, 1).astype(jnp.float32)
    work_span = inputs_here.shape[1]
    attention_full, feedforward_full, vector_low = (
        lax.all_gather(attention_weights.astype(jnp.bfloat16), ("fsdp", "seq"), axis=1, tiled=True),
        lax.all_gather(
            feedforward_weights.astype(jnp.bfloat16), ("fsdp", "seq"), axis=1, tiled=True
        ),
        lax.all_gather(layer_vectors.astype(jnp.bfloat16), ("fsdp", "seq"), axis=1, tiled=True),
    )
    vector_wide = vector_low.astype(jnp.float32)
    tokens = inputs_here.reshape(-1, D)
    tokens_wide = tokens.astype(jnp.float32)
    projected = plain_dot(tokens, attention_full[:, : 3 * D])
    queries = ((projected[:, :D] + vector_wide[0, :D]) * score_scale).astype(jnp.bfloat16)
    key_part = projected[:, D : 2 * D].astype(jnp.bfloat16)
    value_part = (projected[:, 2 * D :] + vector_wide[0, D : 2 * D]).astype(jnp.bfloat16)
    key_rows, value_rows = (
        lax.all_gather(key_part.reshape(row_count, work_span, D), "seq", axis=1, tiled=True),
        lax.all_gather(value_part.reshape(row_count, work_span, D), "seq", axis=1, tiled=True),
    )
    group_rows = math.gcd(row_count, max(1, 512 // work_span))
    block_count = row_count // group_rows
    query_blocks = queries.reshape(block_count, group_rows, work_span, HEADS, HEAD_DIM)
    key_blocks = key_rows.reshape(block_count, group_rows, full_length, HEADS, HEAD_DIM)
    value_blocks = value_rows.reshape(block_count, group_rows, full_length, HEADS, HEAD_DIM)
    query_id_blocks = query_ids.reshape(block_count, group_rows, work_span)
    key_id_blocks = segment_ids.reshape(block_count, group_rows, full_length)
    context, log_total = lax.map(
        attend_block, (query_blocks, key_blocks, value_blocks, query_id_blocks, key_id_blocks)
    )
    context_low = context.reshape(-1, D).astype(jnp.bfloat16)
    attention_out = (
        plain_dot(context_low, attention_full[:, 3 * D :]) + vector_wide[0, 2 * D : 3 * D]
    )
    first_normed, first_inverse = normalize(tokens_wide + attention_out)
    first_norm = (first_normed * vector_wide[2, :D] + vector_wide[2, D : 2 * D]).astype(
        jnp.bfloat16
    )
    up_value = plain_dot(first_norm, feedforward_full[:, :FF]) + vector_wide[1]
    activated = jax.nn.gelu(up_value, approximate=False).astype(jnp.bfloat16)
    feed_out = contract_columns(activated, feedforward_full[:, FF:]) + vector_wide[0, 3 * D :]
    second_normed, second_inverse = normalize(first_norm.astype(jnp.float32) + feed_out)
    layer_output = (second_normed * vector_wide[2, 2 * D : 3 * D] + vector_wide[2, 3 * D :]).astype(
        jnp.bfloat16
    )
    output_rows = layer_output.reshape(row_count, work_span, D)
    flat_flags = work_flags.reshape(-1)
    squares = jnp.stack(
        [
            jnp.sum(flat_flags * jnp.mean(tokens_wide * tokens_wide, axis=-1)),
            jnp.sum(flat_flags * jnp.mean(attention_out * attention_out, axis=-1)),
            jnp.sum(flat_flags * jnp.mean(feed_out * feed_out, axis=-1)),
        ]
    )
    square_total, flag_total = lax.psum((squares, jnp.sum(flat_flags)), ("fsdp", "seq"))
    stream_rms = jnp.sqrt(square_total / flag_total)
    segment_range = jnp.arange(SEGMENTS, dtype=jnp.int32)
    members = (query_ids[:, None, :] == segment_range[None, :, None]).astype(
        jnp.float32
    ) * work_flags[:, None, :]
    partial_pool = jnp.einsum(
        "rsl,rld->rsd",
        members.astype(jnp.bfloat16),
        output_rows,
        preferred_element_type=jnp.float32,
    )
    pool_share = lax.psum_scatter(
        partial_pool.astype(jnp.bfloat16), "seq", scatter_dimension=2, tiled=True
    ).astype(jnp.float32)
    full_members = (segment_ids[:, None, :] == segment_range[None, :, None]).astype(jnp.float32)
    full_members = full_members * token_flags[:, None, :].astype(jnp.float32)
    counts = jnp.sum(full_members, axis=2)
    pooled = pool_share / jnp.maximum(counts, 1.0)[:, :, None]
    attention_back, feedforward_back, vector_again = (
        lax.all_gather(attention_weights.astype(jnp.bfloat16), ("fsdp", "seq"), axis=1, tiled=True),
        lax.all_gather(
            feedforward_weights.astype(jnp.bfloat16), ("fsdp", "seq"), axis=1, tiled=True
        ),
        lax.all_gather(layer_vectors.astype(jnp.bfloat16), ("fsdp", "seq"), axis=1, tiled=True),
    )
    vector_back = vector_again.astype(jnp.float32)
    grad_out = grad_here.reshape(-1, D).astype(jnp.float32)
    grad_gain_second = jnp.sum(grad_out * second_normed, axis=0)
    grad_shift_second = jnp.sum(grad_out, axis=0)
    grad_second = norm_back(grad_out * vector_back[2, 2 * D : 3 * D], second_normed, second_inverse)
    grad_feed = grad_second.astype(jnp.bfloat16)
    grad_bias_down = jnp.sum(grad_feed.astype(jnp.float32), axis=0)
    grad_down = contract_rows(grad_feed, activated)
    grad_activated = plain_dot(grad_feed, feedforward_back[:, FF:])
    grad_up = (grad_activated * gelu_slope(up_value)).astype(jnp.bfloat16)
    grad_bias_up = jnp.sum(grad_up.astype(jnp.float32), axis=0)
    grad_up_weight = contract_rows(first_norm, grad_up)
    grad_first = grad_second + contract_columns(grad_up, feedforward_back[:, :FF])
    grad_feedforward = jnp.concatenate([grad_up_weight, grad_down], axis=1)
    grad_gain_first = jnp.sum(grad_first * first_normed, axis=0)
    grad_shift_first = jnp.sum(grad_first, axis=0)
    grad_stream = norm_back(grad_first * vector_back[2, :D], first_normed, first_inverse)
    grad_attention_out = grad_stream.astype(jnp.bfloat16)
    grad_bias_out = jnp.sum(grad_attention_out.astype(jnp.float32), axis=0)
    grad_out_weight = contract_rows(context_low, grad_attention_out)
    grad_context = contract_columns(grad_attention_out, attention_back[:, 3 * D :]).astype(
        jnp.bfloat16
    )
    grad_query, grad_key_rows, grad_value_rows = lax.map(
        attend_back,
        (
            query_blocks,
            key_blocks,
            value_blocks,
            query_id_blocks,
            key_id_blocks,
            log_total,
            grad_context.reshape(block_count, group_rows, work_span, HEADS, HEAD_DIM),
        ),
    )
    key_share, value_share = (
        lax.psum_scatter(
            grad_key_rows.reshape(row_count, full_length, D).astype(jnp.bfloat16),
            "seq",
            scatter_dimension=1,
            tiled=True,
        ).astype(jnp.float32),
        lax.psum_scatter(
            grad_value_rows.reshape(row_count, full_length, D).astype(jnp.bfloat16),
            "seq",
            scatter_dimension=1,
            tiled=True,
        ).astype(jnp.float32),
    )
    grad_query_low = grad_query.reshape(-1, D).astype(jnp.bfloat16) * score_scale
    grad_key_low = key_share.reshape(-1, D).astype(jnp.bfloat16)
    grad_value_low = value_share.reshape(-1, D).astype(jnp.bfloat16)
    grad_projected = jnp.concatenate([grad_query_low, grad_key_low, grad_value_low], axis=1)
    grad_bias_query = jnp.sum(grad_query_low.astype(jnp.float32), axis=0)
    grad_bias_value = jnp.sum(grad_value_low.astype(jnp.float32), axis=0)
    grad_in_weight = contract_rows(tokens, grad_projected)
    input_rows = (
        grad_stream + contract_columns(grad_projected, attention_back[:, : 3 * D])
    ).astype(jnp.bfloat16)
    input_rows = input_rows.reshape(row_count, work_span, D)
    grad_attention = jnp.concatenate([grad_in_weight, grad_out_weight], axis=1)
    grad_vectors = jnp.stack(
        [
            jnp.concatenate([grad_bias_query, grad_bias_value, grad_bias_out, grad_bias_down]),
            grad_bias_up,
            jnp.concatenate(
                [grad_gain_first, grad_shift_first, grad_gain_second, grad_shift_second]
            ),
        ]
    )
    attention_share, feedforward_share, vector_share = (
        lax.psum_scatter(grad_attention, ("fsdp", "seq"), scatter_dimension=1, tiled=True),
        lax.psum_scatter(grad_feedforward, ("fsdp", "seq"), scatter_dimension=1, tiled=True),
        lax.psum_scatter(grad_vectors, ("fsdp", "seq"), scatter_dimension=1, tiled=True),
    )
    attention_new, attention_first_new, attention_second_new, attention_low = adamw_update(
        attention_weights,
        attention_share,
        attention_first,
        attention_second,
        rate_attention,
        weight_decay,
    )
    feedforward_new, feedforward_first_new, feedforward_second_new, feedforward_low = adamw_update(
        feedforward_weights,
        feedforward_share,
        feedforward_first,
        feedforward_second,
        rate_feedforward,
        weight_decay,
    )
    vectors_new, vector_first_new, vector_second_new, vectors_low = adamw_update(
        layer_vectors, vector_share, vector_first, vector_second, rate_vectors, 0.0
    )
    return (
        output_rows,
        input_rows,
        pooled,
        stream_rms,
        attention_new,
        attention_first_new,
        attention_second_new,
        attention_low,
        feedforward_new,
        feedforward_first_new,
        feedforward_second_new,
        feedforward_low,
        vectors_new,
        vector_first_new,
        vector_second_new,
        vectors_low,
    )


MESH = pl.DeviceIdType.MESH
F32 = jnp.float32
BF16 = jnp.bfloat16

NZ, NX, NC, NY = 4, 2, 2, 2
ROW = 512
OWN_ROWS = 2
TOKENS = OWN_ROWS * ROW
SHARD_A = 96
SHARD_F = 192
EXTRA = 16
FULL_A = SHARD_A + EXTRA
PIECES = 3
PIECE = SHARD_F // PIECES
BLOCK = FF // PIECES
SPLIT_F = 48


def tn_dot(left_side, right_side):
    return contract_rows(left_side, right_side)


def nt_dot(left_side, right_side):
    return contract_columns(left_side, right_side)


def column_sum(value):
    return jnp.sum(value, axis=0, keepdims=True)


def row_mean(value):
    return jnp.mean(value, axis=-1, keepdims=True)


def remote(src, dst, send, recv, where):
    return pltpu.make_async_remote_copy(
        src_ref=src,
        dst_ref=dst,
        send_sem=send,
        recv_sem=recv,
        device_id=where,
        device_id_type=MESH,
    )


PLAN = (
    (0, 15, 30, 45), (), (16, 260), (1,),
    (
        17, 18, 23, 46, 60, 75, 2, 3, 8, 31, 19, 20, 261, 47, 48, 9, 4, 5,
        24, 32, 33, 25, 90, 105, 10, 21, 22, 53, 49, 50, 76, 38, 26, 27, 6, 7,
        34, 35, 61, 11, 12, 51, 52, 77, 78, 39, 40, 13, 14, 36, 37, 41, 42, 54,
        55, 62, 63, 28, 29, 120, 135, 68, 79, 80, 106, 56, 57, 43, 44, 83, 58, 59,
        64, 65, 91,
    ),
    (81, 82, 84, 85, 86, 87, 107, 108), (), (66, 67, 69, 70, 88, 89, 113),
    (71, 72, 92, 93, 114, 115), (98, 109, 110, 136), (73, 74, 262),
    (94, 95, 111, 112, 99, 117, 116, 121, 138, 137, 143), (100,), (96, 97, 263), (101, 102),
    (122, 123), (128, 139, 140), (103, 104, 118, 119, 144, 145), (124, 125, 141, 142), (),
    (129, 130), (126, 127), (), (131, 132), (), (), (133, 134, 146, 147, 148, 149), (), (), (),
    (), (), (), (), (), (), (), (), (), (), (150, 161), (), (151, 152, 162, 163), (),
    (153, 154, 164, 165, 172, 183), (), (173, 174, 184, 185), (155, 156, 166, 167),
    (186, 187, 194, 205), (), (), (175, 176), (), (), (), (), (195,),
    (157, 158, 168, 169, 196, 206, 207), (188, 189), (208, 209), (177, 178),
    (159, 170, 190, 191, 197, 198), (160,), (179, 180, 192, 210, 211), (), (171, 193, 199, 200),
    (181, 212, 213), (), (182, 201, 202, 214), (215,), (), (), (), (203,), (), (), (), (204,), (),
    (), (216, 227), (217,), (218, 228, 229, 264, 265),
    (
        219, 220, 238, 249, 230, 231, 239, 240, 250, 251, 221, 222, 232, 233, 223, 224, 234, 235,
        241, 242, 225, 236, 243, 244, 237, 245, 246, 252, 253, 247, 254, 255, 226, 256, 257, 248,
        258, 259,
    ),

)


class Place:
    def __init__(self):
        f = lax.axis_index("fsdp")
        self.z = f // (NX * NC)
        self.x = (f // NC) % NX
        self.c = f % NC
        self.y = lax.axis_index("seq")

    def at(self, z=None, x=None, c=None, y=None):
        z = self.z if z is None else z
        x = self.x if x is None else x
        c = self.c if c is None else c
        y = self.y if y is None else y
        return ((z * NX + x) * NC + c, y)

    def core(self):
        return self.at(c=1 - self.c)

    def first(self, order):
        return self.at(y=1 - self.y) if order == 0 else self.at(x=1 - self.x)

    def last(self, order):
        return self.at(x=1 - self.x) if order == 0 else self.at(y=1 - self.y)


class Gather:
    def __init__(self, me, buf, start, size, order, index, sems):
        self.me, self.buf, self.order, self.index = me, buf, order, index
        self.rows = pl.ds(start, size)
        self.sems = sems

    def own(self):
        me = self.me
        return self.buf.at[me.z, me.x, me.c, me.y, self.rows]

    def near(self):
        me = self.me
        if self.order == 0:
            return self.buf.at[me.z, me.x, me.c, 1 - me.y, self.rows]
        return self.buf.at[me.z, 1 - me.x, me.c, me.y, self.rows]

    def bundle(self, zz, far):
        me = self.me
        if self.order == 0:
            x = 1 - me.x if far else me.x
            return self.buf.at[zz, x, me.c, :, self.rows]
        y = 1 - me.y if far else me.y
        return self.buf.at[zz, :, me.c, y, self.rows]

    def quad(self, zz, other):
        c = 1 - self.me.c if other else self.me.c
        return self.buf.at[zz, :, c, :, self.rows]

    def first_copy(self, arriving=False):
        s, i = self.sems, self.index
        ref = self.near() if arriving else self.own()
        return remote(ref, ref, s.a_s.at[i], s.a_r.at[i], self.me.first(self.order))

    def line_copy(self, zz, up):
        s, i = self.sems, self.index
        ref = self.bundle(zz, False)
        step = 1 if up else -1
        return remote(
            ref,
            ref,
            (s.up_s if up else s.dn_s).at[i, zz],
            s.z_r.at[i, zz],
            self.me.at(z=self.me.z + step),
        )

    def last_copy(self, zz, arriving=False):
        s, i = self.sems, self.index
        ref = self.bundle(zz, arriving)
        return remote(ref, ref, s.b_s.at[i, zz], s.b_r.at[i, zz], self.me.last(self.order))

    def core_copy(self, zz, arriving=False):
        s, i = self.sems, self.index
        ref = self.quad(zz, arriving)
        return remote(ref, ref, s.c_s.at[i, zz], s.c_r.at[i, zz], self.me.core())

    def one_way(self, step, up, act):
        zz = self.me.z - step if up else self.me.z + step
        pl.when((zz >= 0) if up else (zz < NZ))(lambda: act(zz))

    def send_line(self, zz, up):
        z = self.me.z
        if up:

            @pl.when(z < NZ - 1)
            def _():
                self.line_copy(zz, True).start()

        else:

            @pl.when(z > 0)
            def _():
                self.line_copy(zz, False).start()

    def start(self):
        self.first_copy().start()

    def spread(self):
        self.first_copy(True).wait_recv()
        z = self.me.z
        self.send_line(z, True)
        self.send_line(z, False)
        self.last_copy(z).start()

    def line(self, step, up):
        def act(zz):
            self.line_copy(zz, up).wait_recv()
            self.send_line(zz, up)
            self.last_copy(zz).start()

        self.one_way(step, up, act)

    def cross(self, step, up):
        def act(zz):
            self.last_copy(zz, True).wait_recv()
            self.core_copy(zz).start()

        self.one_way(step, up, act)

    def finish(self):
        for zz in range(NZ):
            self.core_copy(zz, True).wait_recv()

    def events(self):
        ways = ((1, True), (1, False), (2, True), (2, False), (3, True), (3, False))
        return (
            [self.start, self.spread]
            + [functools.partial(self.line, *way) for way in ways]
            + [functools.partial(self.cross, *way) for way in ((0, True),) + ways]
        )

    def drain(self):
        z = self.me.z
        self.first_copy().wait_send()
        for zz in range(NZ):
            self.last_copy(zz).wait_send()
            self.core_copy(zz).wait_send()

            @pl.when((zz <= z) & (z < NZ - 1))
            def _():
                self.line_copy(zz, True).wait_send()

            @pl.when((zz >= z) & (z > 0))
            def _():
                self.line_copy(zz, False).wait_send()


class Scatter:
    def __init__(self, me, buf, start, size, order, index, sems, landing, out, slot, credits):
        self.me, self.buf, self.order, self.index = me, buf, order, index
        self.rows = pl.ds(start, size)
        self.sems = sems
        self.rc, self.rb, self.rz, self.ra = landing
        self.out = out
        self.slot = pl.ds(slot, size)
        self.after, self.before = credits

    def part(self, zz, far, other=False):
        me = self.me
        c = 1 - me.c if other else me.c
        if self.order == 0:
            return self.buf.at[zz, 1 - me.x if far else me.x, c, :, self.rows]
        return self.buf.at[zz, :, c, 1 - me.y if far else me.y, self.rows]

    def planes(self, far, other):
        me = self.me
        c = 1 - me.c if other else me.c
        if self.order == 0:
            return self.buf.at[:, 1 - me.x if far else me.x, c, :, self.rows]
        return self.buf.at[:, :, c, 1 - me.y if far else me.y, self.rows]

    def got_core(self, far, zz=None):
        half = 1 if far else 0
        if zz is None:
            return self.rc.at[half, :, :, self.slot]
        return self.rc.at[half, zz, :, self.slot]

    def core_copy(self, far):
        s, i = self.sems, self.index
        half = 1 if far else 0
        return remote(
            self.planes(far, True),
            self.got_core(far),
            s.rc_s.at[i, half],
            s.rc_r.at[i, half],
            self.me.core(),
        )

    def last_copy(self, zz):
        s, i = self.sems, self.index
        return remote(
            self.part(zz, True),
            self.rb.at[zz],
            s.rb_s.at[i, zz],
            s.rb_r.at[i, zz],
            self.me.last(self.order),
        )

    def line_slot(self, zz, at, down):
        return zz if down else jnp.where(zz == at, NZ, zz)

    def line_copy(self, zz, down):
        s, i = self.sems, self.index
        to = self.me.z - 1 if down else self.me.z + 1
        slot = self.line_slot(zz, to, down)
        return remote(
            self.part(zz, False),
            self.rz.at[slot],
            s.rz_s.at[i, zz],
            s.rz_r.at[i, slot],
            self.me.at(z=to),
        )

    def line_wait(self, slot):
        s, i = self.sems, self.index
        remote(
            self.rz.at[slot],
            self.rz.at[slot],
            s.rz_s.at[i, 0],
            s.rz_r.at[i, slot],
            self.me.core(),
        ).wait_recv()

    def home(self, mine):
        me = self.me
        if self.order == 0:
            y = me.y if mine else 1 - me.y
            return self.buf.at[me.z, me.x, me.c, y, self.rows], y
        x = me.x if mine else 1 - me.x
        return self.buf.at[me.z, x, me.c, me.y, self.rows], x

    def first_copy(self):
        s, i = self.sems, self.index
        return remote(
            self.home(False)[0],
            self.ra,
            s.ra_s.at[i],
            s.ra_r.at[i],
            self.me.first(self.order),
        )

    def by_distance(self, dist, act):
        act_down, act_up = (lambda zz: act(zz, True)), (lambda zz: act(zz, False))
        self.one_way(dist, True, act_down)
        if dist > 0:
            self.one_way(dist, False, act_up)

    def one_way(self, dist, down, act):
        zz = self.me.z - dist if down else self.me.z + dist
        pl.when((zz >= 0) if down else (zz < NZ))(lambda: act(zz))

    def start(self):
        if self.after is not None:
            pl.semaphore_wait(self.after, 1)
        self.core_copy(True).start()
        self.core_copy(False).start()

    def cross(self):
        self.core_copy(True).wait_recv()
        for dist in range(NZ - 1, -1, -1):

            def act(zz, down):
                ref = self.part(zz, True)
                got = self.got_core(True, zz)
                ref[...] = (ref[...].astype(F32) + got[...].astype(F32)).astype(BF16)
                self.last_copy(zz).start()

            self.by_distance(dist, act)

    def keep(self):
        self.core_copy(False).wait_recv()
        for zz in range(NZ):
            ref = self.part(zz, False)
            got = self.got_core(False, zz)
            ref[...] = (ref[...].astype(F32) + got[...].astype(F32)).astype(BF16)
        if self.before is not None:
            pl.semaphore_signal(
                self.before, inc=1, device_id=self.me.core(), device_id_type=MESH
            )

    def line(self, dist, down):
        z = self.me.z

        def act(zz):
            self.last_copy(zz).wait_recv()
            ref = self.part(zz, False)
            outer = z < NZ - 1 if down else z > 0
            total = ref[...].astype(F32) + self.rb[zz].astype(F32)

            @pl.when(outer)
            def _():
                self.line_wait(zz)
                ref[...] = (total + self.rz[zz].astype(F32)).astype(BF16)

            @pl.when(jnp.logical_not(outer))
            def _():
                ref[...] = total.astype(BF16)

            self.line_copy(zz, down).start()

        self.one_way(dist, down, act)

    def events(self):
        ways = ((3, True), (3, False), (2, True), (2, False), (1, True), (1, False))
        return (
            [self.start, self.cross, self.keep]
            + [functools.partial(self.line, *way) for way in ways]
            + [self.settle, self.finish]
        )

    def settle(self):
        z = self.me.z
        self.last_copy(z).wait_recv()
        far_ref, far = self.home(False)
        near_ref, near = self.home(True)
        self.out[self.rows, :] = near_ref[...].astype(F32) + self.rb[z, near].astype(F32)
        total = far_ref[...].astype(F32) + self.rb[z, far].astype(F32)

        @pl.when(z == 0)
        def _():
            self.line_wait(z)
            far_ref[...] = (total + self.rz[z, far].astype(F32)).astype(BF16)
            self.out[self.rows, :] += self.rz[z, near].astype(F32)

        @pl.when(z == NZ - 1)
        def _():
            self.line_wait(NZ)
            far_ref[...] = (total + self.rz[NZ, far].astype(F32)).astype(BF16)
            self.out[self.rows, :] += self.rz[NZ, near].astype(F32)

        @pl.when((z > 0) & (z < NZ - 1))
        def _():
            self.line_wait(z)
            self.line_wait(NZ)
            far_ref[...] = (
                total + (self.rz[z, far].astype(F32) + self.rz[NZ, far].astype(F32))
            ).astype(BF16)
            self.out[self.rows, :] += self.rz[z, near].astype(F32) + self.rz[NZ, near].astype(
                F32
            )

        self.first_copy().start()

    def finish(self):
        self.first_copy().wait_recv()
        self.out[self.rows, :] += self.ra[...].astype(F32)

    def drain(self):
        z = self.me.z
        self.core_copy(True).wait_send()
        self.core_copy(False).wait_send()
        self.first_copy().wait_send()
        for zz in range(NZ):
            self.last_copy(zz).wait_send()

            @pl.when(zz < z)
            def _():
                self.line_copy(zz, True).wait_send()

            @pl.when(zz > z)
            def _():
                self.line_copy(zz, False).wait_send()


class Schedule:
    def __init__(self, events):
        self.events, self.place = events, 0

    def take(self):
        chosen = PLAN[self.place]
        self.place += 1

        def run():
            for number in chosen:
                self.events[number]()

        return run if chosen else None

    def step(self, count=1):
        for _ in range(count):
            run = self.take()
            if run is not None:
                run()

    def loop(self, count, body):
        runs = [self.take() for _ in range(count)]

        @pl.loop(0, count)
        def _(i):
            body(i)
            for place, run in enumerate(runs):
                if run is not None:
                    pl.when(i == place)(run)


def repeat(count, body):
    pl.loop(0, count)(body)


def flatten(value):
    return value.reshape(-1, value.shape[-1])


def attention_pair(queries, keys, values, bias):
    first = lax.broadcasted_iota(jnp.int32, keys.shape, 1) < HEAD_DIM
    zero = jnp.zeros((), BF16)
    values_turned = values.T
    contexts, totals = [], []
    for half in range(2):
        keys_half = jnp.where(first if half == 0 else ~first, keys, zero)
        scores = nt_dot(keys_half, queries) + bias
        largest = jnp.max(scores, axis=0, keepdims=True)
        exponent = jnp.exp(scores - largest)
        total = column_sum(exponent)
        soft = (exponent * (1.0 / total)).astype(BF16)
        contexts.append(
            plain_dot(values_turned[half * HEAD_DIM : (half + 1) * HEAD_DIM, :], soft)
        )
        totals.append(largest + jnp.log(total))
    return jnp.concatenate(contexts, 0).T, jnp.concatenate(totals, 0)


def attention_pair_back(queries, keys, values, grad_context, bias, log_total):
    first = lax.broadcasted_iota(jnp.int32, keys.shape, 1) < HEAD_DIM
    zero = jnp.zeros((), BF16)
    keys_turned = keys.T
    grad_queries = []
    grad_keys = grad_values = 0.0
    for half in range(2):
        mask = first if half == 0 else ~first
        scores = nt_dot(jnp.where(mask, keys, zero), queries) + bias
        soft = jnp.exp(scores - log_total[half : half + 1, :])
        grad_soft = nt_dot(jnp.where(mask, values, zero), grad_context)
        inner = column_sum(soft * grad_soft)
        grad_scores = (soft * (grad_soft - inner)).astype(BF16)
        grad_values += plain_dot(soft.astype(BF16), jnp.where(mask, grad_context, zero))
        grad_keys += plain_dot(grad_scores, jnp.where(mask, queries, zero))
        grad_queries.append(
            plain_dot(keys_turned[half * HEAD_DIM : (half + 1) * HEAD_DIM, :], grad_scores)
        )
    return jnp.concatenate(grad_queries, 0).T, grad_keys, grad_values


def select_columns(permuted):
    row = lax.broadcasted_iota(jnp.int32, (8 * 128, D), 0)
    col = lax.broadcasted_iota(jnp.int32, (8 * 128, D), 1)
    lane = row % 128
    source = (row // 128) * SHARD_A + lane
    if permuted:
        piece = col // 256
        rest = col % 256
        col = (rest // PIECE) * SHARD_F + piece * PIECE + rest % PIECE
    return jnp.where((source == col) & (lane < SHARD_A), 1.0, 0.0).astype(BF16)


SEM_SHAPES = dict(
    a_s=(10,),
    a_r=(10,),
    z_r=(10, NZ),
    up_s=(10, NZ),
    dn_s=(10, NZ),
    b_s=(10, NZ),
    b_r=(10, NZ),
    c_s=(10, NZ),
    c_r=(10, NZ),
    rc_s=(10, 2),
    rc_r=(10, 2),
    rb_s=(10, NZ),
    rb_r=(10, NZ),
    rz_s=(10, NZ),
    rz_r=(10, NZ + 1),
    ra_s=(10,),
    ra_r=(10,),
    x_s=(4, 2),
    x_r=(4, 2),
    own=(4, 2),
    pool_s=(1,),
    pool_r=(1,),
    stat_s=(5,),
    stat_r=(5,),
    load=(3,),
)


def pieces():
    rest = PIECE - SPLIT_F
    return [(0, SPLIT_F, rest), (PIECE, FULL_A - PIECE - rest, rest)] + [
        (k * PIECE, SPLIT_F, rest) for k in range(PIECES)
    ]


def scratch():
    return dict(
        wa=pltpu.VMEM((NZ, NX, NC, NY, FULL_A, D), BF16),
        wf=pltpu.VMEM((NZ, NX, NC, NY, SHARD_F, D), BF16),
        rc=pltpu.VMEM((2, NZ, 2, PIECE, D), BF16),
        xs=pltpu.VMEM((TOKENS, D), BF16),
        dys=pltpu.VMEM((TOKENS, D), BF16),
        ctx=pltpu.VMEM((TOKENS, D), BF16),
        n1=pltpu.VMEM((TOKENS, D), BF16),
        fn=pltpu.VMEM((TOKENS, D), BF16),
        fg=pltpu.VMEM((TOKENS, D), BF16),
        qkv=pltpu.VMEM((TOKENS, 3 * D), BF16),
        act=pltpu.VMEM((PIECES, TOKENS, BLOCK), BF16),
        slope=pltpu.VMEM((PIECES, TOKENS, BLOCK), BF16),
        acc=pltpu.VMEM((TOKENS, D), F32),
        bias=pltpu.VMEM((OWN_ROWS, ROW, ROW), BF16),
        totals=pltpu.VMEM((OWN_ROWS * HEADS // 2, 2, ROW), F32),
        side=pltpu.VMEM((TOKENS, 128), F32),
        vec=pltpu.VMEM((16, 4 * D), F32),
        bu=pltpu.VMEM((PIECES, 16, BLOCK), F32),
        gvec=pltpu.VMEM((8, 4 * D), F32),
        gbu=pltpu.VMEM((PIECES, 8, BLOCK), F32),
        stat=pltpu.VMEM((8, 128), F32),
        stat_in=pltpu.VMEM((5, 8, 128), F32),
        pool_out=pltpu.VMEM((OWN_ROWS, 8, D), F32),
        pool_in=pltpu.VMEM((OWN_ROWS, 8, D // 2), F32),
        credit=pltpu.SemaphoreType.REGULAR((2,)),
        free=pltpu.SemaphoreType.REGULAR,
    )


def landing_shapes():
    shapes = []
    for _ in range(PIECES):
        for size in (SPLIT_F, PIECE - SPLIT_F):
            shapes += [
                pltpu.VMEM((NZ, 2, size, D), BF16),
                pltpu.VMEM((NZ + 1, 2, size, D), BF16),
                pltpu.VMEM((size, D), BF16),
            ]
    return shapes


def fused_kernel(
    x_in,
    dy_in,
    wa_in,
    wf_in,
    ids,
    flags,
    flag_column,
    out_y,
    out_dx,
    out_pooled,
    out_stats,
    grad_a,
    grad_f,
    *more,
):
    names, sem_names = tuple(scratch()), tuple(SEM_SHAPES)
    landings = len(landing_shapes())
    r = types.SimpleNamespace(**dict(zip(names, more)))
    landing_refs = more[len(names) : len(names) + landings]
    sems = types.SimpleNamespace(**dict(zip(sem_names, more[len(names) + landings :])))
    me = Place()
    z, x, c, y = me.z, me.x, me.c, me.y
    wa, wf, xs, dys, ctx = r.wa, r.wf, r.xs, r.dys, r.ctx
    n1, fn, fg, qkv, acc = r.n1, r.fn, r.fg, r.qkv, r.acc
    act, slope, vec, gvec, stat = r.act, r.slope, r.vec, r.gvec, r.stat

    def tile(i, size):
        return pl.ds(pl.multiple_of(i * size, size), size)

    def vector(row, quarter):
        return vec[row : row + 1, quarter * D : (quarter + 1) * D]

    barrier = pltpu.get_barrier_semaphore()
    for where in (
        me.core(),
        me.at(x=1 - x),
        me.at(y=1 - y),
        me.at(z=(z + 2) % NZ),
    ):
        pl.semaphore_signal(barrier, inc=1, device_id=where, device_id_type=MESH)

    @pl.when(z > 0)
    def _():
        pl.semaphore_signal(barrier, inc=1, device_id=me.at(z=z - 1), device_id_type=MESH)

    @pl.when(z < NZ - 1)
    def _():
        pl.semaphore_signal(barrier, inc=1, device_id=me.at(z=z + 1), device_id_type=MESH)

    load_a = pltpu.make_async_copy(wa_in, wa.at[z, x, c, y], sems.load.at[0])
    load_f = pltpu.make_async_copy(wf_in, wf.at[z, x, c, y], sems.load.at[1])
    load_s = pltpu.make_async_copy(flag_column, r.side, sems.load.at[2])
    load_a.start()
    load_f.start()
    load_s.start()

    def row_copy(kind, src, dst, slot):
        return remote(
            src, dst, sems.x_s.at[kind, slot], sems.x_r.at[kind, slot], me.at(y=1 - y)
        )

    def own_copy(kind, src, dst, slot):
        return pltpu.make_async_copy(src, dst, sems.own.at[kind, slot])

    def span(slot, half):
        return pl.ds(pl.multiple_of(slot * ROW + half * (ROW // 2), ROW // 2), ROW // 2)

    def take_rows(kind, source, target):
        sends = [
            row_copy(kind, source.at[2 * (1 - y) + slot], target.at[span(slot, y)], slot)
            for slot in range(OWN_ROWS)
        ]
        owns = [
            own_copy(kind, source.at[2 * y + slot], target.at[span(slot, y)], slot)
            for slot in range(OWN_ROWS)
        ]
        arrivals = [
            row_copy(kind, source.at[2 * y + slot], target.at[span(slot, 1 - y)], slot)
            for slot in range(OWN_ROWS)
        ]
        return sends, owns, arrivals

    def give_rows(kind, source, target):
        sends = [
            row_copy(kind, source.at[span(slot, 1 - y)], target.at[2 * y + slot], slot)
            for slot in range(OWN_ROWS)
        ]
        owns = [
            own_copy(kind, source.at[span(slot, y)], target.at[2 * y + slot], slot)
            for slot in range(OWN_ROWS)
        ]
        arrivals = [
            row_copy(kind, source.at[span(slot, y)], target.at[2 * (1 - y) + slot], slot)
            for slot in range(OWN_ROWS)
        ]
        return sends, owns, arrivals

    x_sends, x_owns, x_arrivals = take_rows(0, x_in, xs)
    dy_sends, dy_owns, dy_arrivals = take_rows(1, dy_in, dys)
    out_sends, out_owns, out_arrivals = give_rows(2, dys, out_y)
    dx_sends, dx_owns, dx_arrivals = give_rows(3, n1, out_dx)

    def start_all(copies):
        def run():
            for copy in copies:
                copy.start()

        return run

    gathers, scatters = [], []
    for piece, (first_row, *sizes) in enumerate(pieces()):
        for order in range(2):
            buf = wa if piece < 2 else wf
            start = first_row + order * sizes[0]
            gathers.append(Gather(me, buf, start, sizes[order], order, 2 * piece + order, sems))
    for piece, (first_row, *sizes) in enumerate(pieces()[2:] + pieces()[:2]):
        out = grad_f if piece < PIECES else grad_a
        for order in range(2):
            size, i = sizes[order], 2 * (piece % PIECES) + order
            landing = (
                r.rc,
                landing_refs[3 * i].at[:, :, 0:size],
                landing_refs[3 * i + 1].at[:, :, 0:size],
                landing_refs[3 * i + 2].at[0:size],
            )
            credit = r.credit.at[order]
            credits = (credit if piece > 0 else None, credit if piece < PIECES + 1 else None)
            slot = order * sizes[0]
            scatters.append(
                Scatter(
                    me, wf, first_row + slot, size, order, 2 * piece + order, sems, landing, out,
                    slot, credits,
                )
            )

    exchange = [copy.start for copy in x_sends + dy_sends + dx_sends]
    events = [event for one in gathers + scatters for event in one.events()] + exchange
    plan = Schedule(events)

    for copy in x_owns + dy_owns:
        copy.start()
    line_ends = jnp.where(z > 0, 1, 0).astype(jnp.int32) + jnp.where(z < NZ - 1, 1, 0).astype(
        jnp.int32
    )
    load_a.wait()
    pl.semaphore_wait(barrier, 4 + line_ends)
    plan.step()
    load_f.wait()

    gvec[...] = jnp.zeros_like(gvec)
    r.gbu[...] = jnp.zeros_like(r.gbu)
    stat[...] = jnp.zeros_like(stat)
    for slot in range(OWN_ROWS):
        wide = jnp.broadcast_to(ids[slot].astype(F32), (128, ROW))
        tall = wide.T
        for j in range(ROW // 128):
            across = wide[:, j * 128 : (j + 1) * 128]
            across = jnp.broadcast_to(across[0:1, :], (ROW, 128))
            r.bias[slot, :, j * 128 : (j + 1) * 128] = jnp.where(
                tall == across, 0.0, masked_score
            ).astype(BF16)
        plan.step()
    ctx[...] = select_columns(False)
    fg[...] = select_columns(True)
    plan.step()
    plan.step()
    for one in gathers[:4]:
        one.finish()

    for q in range(4):
        blocks = jnp.concatenate(
            [
                wa[q, j // 4, (j // 2) % 2, j % 2, SHARD_A:FULL_A, 0:128]
                for j in range(8)
            ],
            axis=1,
        )
        vec[:, q * D : (q + 1) * D] = plain_dot(blocks, ctx[...])
        moved = plain_dot(blocks, fg[...])
        for k in range(PIECES):
            r.bu[k, :, q * 256 : (q + 1) * 256] = moved[:, k * 256 : (k + 1) * 256]

    plan.step()
    load_s.wait()
    plan.step()
    for copy in x_owns:
        copy.wait()
    for copy in x_arrivals:
        copy.wait_recv()

    scale = HEAD_DIM ** (-0.5)

    def project(i):
        rows = tile(i, 512)
        tokens = xs[rows, :]
        wide = tokens.astype(F32)
        stat[0:1, :] += lane_sums(wide * wide * r.side[rows, 1:2])
        for j in range(3):
            weights = flatten(wa[j, :, :, :, 0:SHARD_A, :])
            value = nt_dot(tokens, weights)
            if j == 0:
                value = (value + vector(0, 0)) * scale
            if j == 2:
                value = value + vector(0, 1)
            qkv[rows, j * D : (j + 1) * D] = value.astype(BF16)

    def lane_sums(value):
        total = column_sum(value)
        return sum(total[:, j * 128 : (j + 1) * 128] for j in range(D // 128))

    plan.loop(2, project)

    def columns(pair, block):
        return pl.ds(pl.multiple_of(block * D + pair * 128, 128), 128)

    def attend(i):
        slot, pair = i // (HEADS // 2), i % (HEADS // 2)
        rows = tile(slot, ROW)
        context, total = attention_pair(
            qkv[rows, columns(pair, 0)],
            qkv[rows, columns(pair, 1)],
            qkv[rows, columns(pair, 2)],
            r.bias[slot].astype(F32),
        )
        ctx[rows, columns(pair, 0)] = context.astype(BF16)
        r.totals[i] = total

    plan.loop(OWN_ROWS * HEADS // 2, attend)

    def attention_output(i):
        rows = tile(i, 256)
        weights = flatten(wa[3, :, :, :, 0:SHARD_A, :])
        out = nt_dot(ctx[rows, :], weights) + vector(0, 2)
        stat[1:2, :] += lane_sums(out * out * r.side[rows, 1:2])
        normed, inverse = normalize(xs[rows, :].astype(F32) + out)
        n1[rows, :] = normed.astype(BF16)
        r.side[rows, 0:1] = inverse
        fn[rows, :] = (normed * vector(2, 0) + vector(2, 1)).astype(BF16)

    plan.loop(4, attention_output)

    def up_rows(k):
        return flatten(flatten_lead(wf[0:2, :, :, :, k * PIECE : (k + 1) * PIECE, :]))

    def down_rows(k):
        return flatten(flatten_lead(wf[2:4, :, :, :, k * PIECE : (k + 1) * PIECE, :]))

    def flatten_lead(value):
        return value.reshape(-1, PIECE, D)

    for k in range(PIECES):
        plan.step()
        for one in gathers[4 + 2 * k : 6 + 2 * k]:
            one.finish()

        def feed(i, k=k):
            rows = tile(i, 512)
            up = nt_dot(fn[rows, :], up_rows(k)) + r.bu[k, 1:2, :]
            half = 0.5 * (1.0 + lax.erf(up * math.sqrt(0.5)))
            activated = (up * half).astype(BF16)
            act[k, rows, :] = activated
            slope[k, rows, :] = (
                half + up * (jnp.exp(-0.5 * up * up) * (1.0 / math.sqrt(2.0 * math.pi)))
            ).astype(BF16)
            value = plain_dot(activated, down_rows(k))
            if k == 0:
                acc[rows, :] = value
            else:
                acc[rows, :] += value

        plan.loop(2, feed)
    plan.step()

    for copy in dy_owns:
        copy.wait()
    for copy in dy_arrivals:
        copy.wait_recv()
    for one in gathers:
        one.drain()

    def second(i):
        rows = tile(i, 128)
        feed_out = acc[rows, :] + vector(0, 3)
        stat[2:3, :] += lane_sums(feed_out * feed_out * r.side[rows, 1:2])
        normed, inverse = normalize(fn[rows, :].astype(F32) + feed_out)
        grad = dys[rows, :].astype(F32)
        dys[rows, :] = (normed * vector(2, 2) + vector(2, 3)).astype(BF16)
        gvec[2:3, 2 * D : 3 * D] += column_sum(grad * normed)
        gvec[2:3, 3 * D :] += column_sum(grad)
        back = norm_back(grad * vector(2, 2), normed, inverse)
        acc[rows, :] = back
        low = back.astype(BF16)
        fg[rows, :] = low
        gvec[0:1, 3 * D :] += column_sum(low.astype(F32))

    repeat(TOKENS // 128, second)
    plan.step()

    start_all(out_sends + out_owns)()

    segments = lax.broadcasted_iota(jnp.int32, (SEGMENTS, ROW), 0)
    for slot in range(OWN_ROWS):
        member = jnp.where(segments == ids[slot], 1.0, 0.0) * flags[slot]
        sums = plain_dot(member.astype(BF16), dys[slot * ROW : (slot + 1) * ROW, :])
        counts = jnp.sum(member, axis=1, keepdims=True)
        r.pool_out[slot] = sums / jnp.maximum(counts, 1.0)
        total = flags[slot]
        stat[3:4, :] += sum(total[:, j * 128 : (j + 1) * 128] for j in range(ROW // 128))

    def half_lanes(which):
        return pl.ds(pl.multiple_of(which * (D // 2), 128), D // 2)

    pool_copy = remote(
        r.pool_out.at[:, :, half_lanes(1 - y)],
        r.pool_in,
        sems.pool_s.at[0],
        sems.pool_r.at[0],
        me.at(y=1 - y),
    )
    pool_copy.start()

    stat_partners = [
        me.core(),
        me.at(x=1 - x),
        me.at(y=1 - y),
        me.at(z=z + 1 - 2 * (z % 2)),
        me.at(z=(z + 2) % NZ),
    ]

    def stat_copy(step):
        return remote(
            stat,
            r.stat_in.at[step],
            sems.stat_s.at[step],
            sems.stat_r.at[step],
            stat_partners[step],
        )

    def stat_start(step):
        return lambda: stat_copy(step).start()

    def stat_end(step):
        def run():
            stat_copy(step).wait()
            stat[...] += r.stat_in[step]

        return run

    stat_start(0)()
    plan.step()
    for k in range(PIECES):

        def feed_back(i, k=k):
            rows = tile(i, 512)
            grad = nt_dot(fg[rows, :], down_rows(k)) * slope[k, rows, :].astype(F32)
            low = grad.astype(BF16)
            slope[k, rows, :] = low
            r.gbu[k, 0:1, :] += column_sum(low.astype(F32))
            acc[rows, :] += plain_dot(low, up_rows(k))

        plan.loop(2, feed_back)

        def weights_back(i, k=k):
            cols = tile(i, BLOCK // 2)
            down = tn_dot(act[k, :, cols], fg[...]).astype(BF16)
            up = tn_dot(slope[k, :, cols], fn[...]).astype(BF16)
            where = (slice(None), slice(None), slice(None), pl.ds(k * PIECE, PIECE))
            wf[(2 + i, *where)] = down.reshape(NX, NC, NY, PIECE, D)
            wf[(i, *where)] = up.reshape(NX, NC, NY, PIECE, D)

        plan.loop(2, weights_back)
        stat_end(k)()
        stat_start(k + 1)()

    def first(i):
        rows = tile(i, 128)
        grad = acc[rows, :]
        normed = n1[rows, :].astype(F32)
        gvec[2:3, 0:D] += column_sum(grad * normed)
        gvec[2:3, D : 2 * D] += column_sum(grad)
        stream = norm_back(grad * vector(2, 0), normed, r.side[rows, 0:1])
        acc[rows, :] = stream
        low = stream.astype(BF16)
        fg[rows, :] = low
        gvec[0:1, 2 * D : 3 * D] += column_sum(low.astype(F32))

    plan.loop(TOKENS // 128, first)

    def context_back(i):
        rows = tile(i, 512)
        fn[rows, :] = plain_dot(fg[rows, :], flatten(wa[3, :, :, :, 0:SHARD_A, :])).astype(BF16)

    plan.loop(2, context_back)
    stat_end(3)()
    stat_start(4)()

    def attend_back_pair(i):
        slot, pair = i // (HEADS // 2), i % (HEADS // 2)
        rows = tile(slot, ROW)
        grads = attention_pair_back(
            qkv[rows, columns(pair, 0)],
            qkv[rows, columns(pair, 1)],
            qkv[rows, columns(pair, 2)],
            fn[rows, columns(pair, 0)],
            r.bias[slot].astype(F32),
            r.totals[i],
        )
        for j in range(3):
            low = grads[j].astype(BF16)
            if j == 0:
                low = low * jnp.asarray(scale, BF16)
            qkv[rows, columns(pair, j)] = low
            if j != 1:
                gvec[0:1, columns(pair, j // 2)] += column_sum(low.astype(F32))

    plan.loop(OWN_ROWS * HEADS // 2, attend_back_pair)
    stat_end(4)()
    plan.step()
    for one in scatters[:4]:
        one.drain()

    free = r.free
    for where in (me.at(x=1 - x), me.at(y=1 - y)):
        pl.semaphore_signal(free, inc=1, device_id=where, device_id_type=MESH)

    @pl.when(z > 0)
    def _():
        pl.semaphore_signal(free, inc=1, device_id=me.at(z=z - 1), device_id_type=MESH)

    @pl.when(z < NZ - 1)
    def _():
        pl.semaphore_signal(free, inc=1, device_id=me.at(z=z + 1), device_id_type=MESH)

    for j in range(3):

        def inner_back(i, j=j):
            cols = pl.ds(pl.multiple_of(j * D + i * (D // 2), 128), D // 2)
            value = tn_dot(qkv[:, cols], xs[...]).astype(BF16)
            wf[j, i, :, :, 0:SHARD_A, :] = value.reshape(NC, NY, SHARD_A, D)

        plan.loop(2, inner_back)

    def outer_back(i):
        cols = pl.ds(pl.multiple_of(i * (D // 2), 128), D // 2)
        value = tn_dot(fg[:, cols], ctx[...]).astype(BF16)
        wf[3, i, :, :, 0:SHARD_A, :] = value.reshape(NC, NY, SHARD_A, D)

    plan.loop(2, outer_back)
    pl.semaphore_wait(free, 2 + line_ends)

    ctx[...] = select_columns(False)
    fg[...] = select_columns(True)
    row = lax.broadcasted_iota(jnp.int32, (8, 1), 0)
    for q in range(4):
        plain = nt_dot(gvec[:, q * D : (q + 1) * D].astype(BF16), ctx[...])
        piled = jnp.concatenate(
            [r.gbu[k, :, q * 256 : (q + 1) * 256] for k in range(PIECES)], axis=1
        )
        moved = nt_dot(piled.astype(BF16), fg[...])
        low = jnp.where(row == 1, jnp.broadcast_to(moved[0:1, :], plain.shape), plain)
        low = jnp.concatenate([low, jnp.zeros_like(low)], axis=0).astype(BF16)
        for j in range(8):
            wf[q, j // 4, (j // 2) % 2, j % 2, SHARD_A:FULL_A, 0:128] = low[
                :, j * 128 : (j + 1) * 128
            ]
    plan.step()

    def input_back(i):
        rows = tile(i, 512)
        value = acc[rows, :]
        for j in range(3):
            value += plain_dot(
                qkv[rows, j * D : (j + 1) * D], flatten(wa[j, :, :, :, 0:SHARD_A, :])
            )
        n1[rows, :] = value.astype(BF16)

    plan.loop(2, input_back)
    start_all(dx_owns)()
    plan.step()

    for one in scatters[4:]:
        one.drain()
    pool_copy.wait()
    for slot in range(OWN_ROWS):
        out_pooled[2 * y + slot] = r.pool_out[slot, :, half_lanes(y)]
        out_pooled[2 * (1 - y) + slot] = r.pool_in[slot]
    out_stats[...] = stat[...]
    for copies in (x_sends, dy_sends, out_sends, dx_sends):
        for copy in copies:
            copy.wait_send()
    for copies in (out_owns, dx_owns):
        for copy in copies:
            copy.wait()
    for copies in (out_arrivals, dx_arrivals):
        for copy in copies:
            copy.wait_recv()


def fused_call(inputs, output_grad, attention_low, feedforward_low, ids, flags, flag_column):
    row_count, local_span, width = inputs.shape
    any_space = pl.BlockSpec(memory_space=pl.ANY)
    vmem = pl.BlockSpec(memory_space=pltpu.VMEM)
    semaphores = [pltpu.SemaphoreType.DMA(shape) for shape in SEM_SHAPES.values()]
    return pl.pallas_call(
        fused_kernel,
        out_shape=(
            jax.ShapeDtypeStruct(inputs.shape, BF16),
            jax.ShapeDtypeStruct(inputs.shape, BF16),
            jax.ShapeDtypeStruct((row_count, SEGMENTS, D // NY), F32),
            jax.ShapeDtypeStruct((8, 128), F32),
            jax.ShapeDtypeStruct((FULL_A, D), F32),
            jax.ShapeDtypeStruct((SHARD_F, D), F32),
        ),
        in_specs=[any_space] * 4 + [vmem] * 2 + [any_space],
        out_specs=(any_space, any_space, vmem, vmem, vmem, vmem),
        scratch_shapes=list(scratch().values()) + landing_shapes() + semaphores,
        compiler_params=pltpu.CompilerParams(
            collective_id=0, has_side_effects=True, vmem_limit_bytes=65_000 * 1024
        ),
        name="layer",
    )(inputs, output_grad, attention_low, feedforward_low, ids, flags, flag_column)


def fused_shards(
    inputs,
    segment_ids,
    token_flags,
    output_grad,
    attention_weights,
    feedforward_weights,
    layer_vectors,
    attention_first,
    attention_second,
    feedforward_first,
    feedforward_second,
    vector_first,
    vector_second,
):
    seq = lax.axis_index("seq")
    ids = lax.dynamic_slice_in_dim(segment_ids, seq * OWN_ROWS, OWN_ROWS, 0)
    flags = lax.dynamic_slice_in_dim(token_flags, seq * OWN_ROWS, OWN_ROWS, 0).astype(F32)
    flag_column = jnp.broadcast_to(flags.reshape(TOKENS, 1), (TOKENS, 128))
    vector_rows = jnp.pad(layer_vectors, ((0, EXTRA - 3), (0, D - SHARD_A)))
    attention_low = jnp.concatenate([attention_weights.T, vector_rows], axis=0).astype(BF16)
    feedforward_low = feedforward_weights.T.astype(BF16)
    output_rows, input_rows, pooled, stats, grad_a, grad_f = fused_call(
        inputs,
        output_grad,
        attention_low,
        feedforward_low,
        ids.reshape(OWN_ROWS, 1, ROW),
        flags.reshape(OWN_ROWS, 1, ROW),
        flag_column,
    )
    totals = jnp.sum(stats[0:4], axis=1)
    stream_rms = jnp.sqrt(totals[0:3] / D / totals[3])
    attention_new = adamw_update(
        attention_weights,
        grad_a[0:SHARD_A].T,
        attention_first,
        attention_second,
        rate_attention,
        weight_decay,
    )
    feedforward_new = adamw_update(
        feedforward_weights,
        grad_f.T,
        feedforward_first,
        feedforward_second,
        rate_feedforward,
        weight_decay,
    )
    vectors_new = adamw_update(
        layer_vectors,
        grad_a[SHARD_A : SHARD_A + 3, 0:SHARD_A],
        vector_first,
        vector_second,
        rate_vectors,
        0.0,
    )
    return (
        output_rows,
        input_rows,
        pooled,
        stream_rms,
        *attention_new,
        *feedforward_new,
        *vectors_new,
    )


def solution(mesh):
    fused = mesh.shape["fsdp"] == NZ * NX * NC and mesh.shape["seq"] == NY
    rows = P("fsdp", "seq", None)
    table = P("fsdp", None)
    owned = P(None, ("fsdp", "seq"))
    return jax.shard_map(
        fused_shards if fused else plain_shards,
        mesh=mesh,
        in_specs=(rows, table, table, rows) + (owned,) * 9,
        out_specs=(rows, rows, P("fsdp", None, "seq"), P()) + (owned,) * 12,
        check_vma=False,
    )
```

```python
import functools
import math
import types

import jax
import jax.numpy as jnp
from jax import lax
from jax.experimental import pallas as pl
from jax.experimental.pallas import tpu as pltpu
from jax.sharding import PartitionSpec as P

D = 768
HEADS = 12
HEAD_DIM = 64
FF = 3072
SEGMENTS = 8
STEP = 5


norm_epsilon = 1e-12
adam_epsilon = 1e-08
beta_first = 0.5
beta_second = 0.5
weight_decay = 0.01
rate_attention = 0.04
rate_feedforward = 0.03
rate_vectors = 0.2
masked_score = -1e30


def plain_dot(left_side, right_side):
    return jnp.dot(left_side, right_side, preferred_element_type=jnp.float32)


def contract_rows(left_side, right_side):
    return lax.dot_general(
        left_side, right_side, (((0,), (0,)), ((), ())), preferred_element_type=jnp.float32
    )


def contract_columns(left_side, right_side):
    return lax.dot_general(
        left_side, right_side, (((1,), (1,)), ((), ())), preferred_element_type=jnp.float32
    )


def normalize(stream):
    average = jnp.mean(stream, axis=-1, keepdims=True)
    centered = stream - average
    variance = jnp.mean(centered * centered, axis=-1, keepdims=True)
    inverse = lax.rsqrt(variance + norm_epsilon)
    return (centered * inverse, inverse)


def norm_back(grad_normed, normed, inverse):
    return inverse * (
        grad_normed
        - jnp.mean(grad_normed, axis=-1, keepdims=True)
        - normed * jnp.mean(grad_normed * normed, axis=-1, keepdims=True)
    )


def gelu_slope(value):
    return 0.5 * (1.0 + lax.erf(value * math.sqrt(0.5))) + value * jnp.exp(
        -0.5 * value * value
    ) / math.sqrt(2.0 * math.pi)


def masked_scores(queries, key_part, query_ids, key_ids):
    scores = jnp.einsum("rqhd,rkhd->rhqk", queries, key_part, preferred_element_type=jnp.float32)
    same_segment = query_ids[:, None, :, None] == key_ids[:, None, None, :]
    return jnp.where(same_segment, scores, masked_score)


def attend_block(pieces):
    queries, key_part, value_part, query_ids, key_ids = pieces
    scores = masked_scores(queries, key_part, query_ids, key_ids)
    largest = jnp.max(scores, axis=-1, keepdims=True)
    exponent = jnp.exp(scores - largest)
    denominator = jnp.sum(exponent, axis=-1, keepdims=True)
    soft_weights = (exponent / denominator).astype(jnp.bfloat16)
    context = jnp.einsum(
        "rhqk,rkhd->rqhd", soft_weights, value_part, preferred_element_type=jnp.float32
    )
    return (context, (largest + jnp.log(denominator))[..., 0])


def attend_back(pieces):
    queries, key_part, value_part, query_ids, key_ids, log_total, grad_context = pieces
    scores = masked_scores(queries, key_part, query_ids, key_ids)
    soft_again = jnp.exp(scores - log_total[..., None])
    grad_soft = jnp.einsum(
        "rqhd,rkhd->rhqk", grad_context, value_part, preferred_element_type=jnp.float32
    )
    inner_sum = jnp.sum(soft_again * grad_soft, axis=-1, keepdims=True)
    grad_scores = (soft_again * (grad_soft - inner_sum)).astype(jnp.bfloat16)
    grad_queries = jnp.einsum(
        "rhqk,rkhd->rqhd", grad_scores, key_part, preferred_element_type=jnp.float32
    )
    grad_keys = jnp.einsum(
        "rhqk,rqhd->rkhd", grad_scores, queries, preferred_element_type=jnp.float32
    )
    grad_values = jnp.einsum(
        "rhqk,rqhd->rkhd",
        soft_again.astype(jnp.bfloat16),
        grad_context,
        preferred_element_type=jnp.float32,
    )
    return (grad_queries, grad_keys, grad_values)


def adamw_update(weight, gradient, first_moment, second_moment, step_rate, decay_rate):
    first_new = beta_first * first_moment + (1.0 - beta_first) * gradient
    second_new = beta_second * second_moment + (1.0 - beta_second) * gradient * gradient
    correction_first = 1.0 - beta_first**STEP
    correction_second = 1.0 - beta_second**STEP
    update = (
        first_new / correction_first / (jnp.sqrt(second_new / correction_second) + adam_epsilon)
    )
    weight_new = weight - step_rate * (update + decay_rate * weight)
    return (weight_new, first_new, second_new, weight_new.astype(jnp.bfloat16))


def plain_shards(
    inputs,
    segment_ids,
    token_flags,
    output_grad,
    attention_weights,
    feedforward_weights,
    layer_vectors,
    attention_first,
    attention_second,
    feedforward_first,
    feedforward_second,
    vector_first,
    vector_second,
):
    row_count, local_span, model_width = inputs.shape
    full_length = segment_ids.shape[1]
    score_scale = HEAD_DIM ** (-0.5)
    inputs_here, grad_here = (inputs, output_grad)
    offset = lax.axis_index("seq") * local_span
    query_ids = lax.dynamic_slice_in_dim(segment_ids, offset, local_span, 1)
    work_flags = lax.dynamic_slice_in_dim(token_flags, offset, local_span, 1).astype(jnp.float32)
    work_span = inputs_here.shape[1]
    attention_full, feedforward_full, vector_low = (
        lax.all_gather(attention_weights.astype(jnp.bfloat16), ("fsdp", "seq"), axis=1, tiled=True),
        lax.all_gather(
            feedforward_weights.astype(jnp.bfloat16), ("fsdp", "seq"), axis=1, tiled=True
        ),
        lax.all_gather(layer_vectors.astype(jnp.bfloat16), ("fsdp", "seq"), axis=1, tiled=True),
    )
    vector_wide = vector_low.astype(jnp.float32)
    tokens = inputs_here.reshape(-1, D)
    tokens_wide = tokens.astype(jnp.float32)
    projected = plain_dot(tokens, attention_full[:, : 3 * D])
    queries = ((projected[:, :D] + vector_wide[0, :D]) * score_scale).astype(jnp.bfloat16)
    key_part = projected[:, D : 2 * D].astype(jnp.bfloat16)
    value_part = (projected[:, 2 * D :] + vector_wide[0, D : 2 * D]).astype(jnp.bfloat16)
    key_rows, value_rows = (
        lax.all_gather(key_part.reshape(row_count, work_span, D), "seq", axis=1, tiled=True),
        lax.all_gather(value_part.reshape(row_count, work_span, D), "seq", axis=1, tiled=True),
    )
    group_rows = math.gcd(row_count, max(1, 512 // work_span))
    block_count = row_count // group_rows
    query_blocks = queries.reshape(block_count, group_rows, work_span, HEADS, HEAD_DIM)
    key_blocks = key_rows.reshape(block_count, group_rows, full_length, HEADS, HEAD_DIM)
    value_blocks = value_rows.reshape(block_count, group_rows, full_length, HEADS, HEAD_DIM)
    query_id_blocks = query_ids.reshape(block_count, group_rows, work_span)
    key_id_blocks = segment_ids.reshape(block_count, group_rows, full_length)
    context, log_total = lax.map(
        attend_block, (query_blocks, key_blocks, value_blocks, query_id_blocks, key_id_blocks)
    )
    context_low = context.reshape(-1, D).astype(jnp.bfloat16)
    attention_out = (
        plain_dot(context_low, attention_full[:, 3 * D :]) + vector_wide[0, 2 * D : 3 * D]
    )
    first_normed, first_inverse = normalize(tokens_wide + attention_out)
    first_norm = (first_normed * vector_wide[2, :D] + vector_wide[2, D : 2 * D]).astype(
        jnp.bfloat16
    )
    up_value = plain_dot(first_norm, feedforward_full[:, :FF]) + vector_wide[1]
    activated = jax.nn.gelu(up_value, approximate=False).astype(jnp.bfloat16)
    feed_out = contract_columns(activated, feedforward_full[:, FF:]) + vector_wide[0, 3 * D :]
    second_normed, second_inverse = normalize(first_norm.astype(jnp.float32) + feed_out)
    layer_output = (second_normed * vector_wide[2, 2 * D : 3 * D] + vector_wide[2, 3 * D :]).astype(
        jnp.bfloat16
    )
    output_rows = layer_output.reshape(row_count, work_span, D)
    flat_flags = work_flags.reshape(-1)
    squares = jnp.stack(
        [
            jnp.sum(flat_flags * jnp.mean(tokens_wide * tokens_wide, axis=-1)),
            jnp.sum(flat_flags * jnp.mean(attention_out * attention_out, axis=-1)),
            jnp.sum(flat_flags * jnp.mean(feed_out * feed_out, axis=-1)),
        ]
    )
    square_total, flag_total = lax.psum((squares, jnp.sum(flat_flags)), ("fsdp", "seq"))
    stream_rms = jnp.sqrt(square_total / flag_total)
    segment_range = jnp.arange(SEGMENTS, dtype=jnp.int32)
    members = (query_ids[:, None, :] == segment_range[None, :, None]).astype(
        jnp.float32
    ) * work_flags[:, None, :]
    partial_pool = jnp.einsum(
        "rsl,rld->rsd",
        members.astype(jnp.bfloat16),
        output_rows,
        preferred_element_type=jnp.float32,
    )
    pool_share = lax.psum_scatter(
        partial_pool.astype(jnp.bfloat16), "seq", scatter_dimension=2, tiled=True
    ).astype(jnp.float32)
    full_members = (segment_ids[:, None, :] == segment_range[None, :, None]).astype(jnp.float32)
    full_members = full_members * token_flags[:, None, :].astype(jnp.float32)
    counts = jnp.sum(full_members, axis=2)
    pooled = pool_share / jnp.maximum(counts, 1.0)[:, :, None]
    attention_back, feedforward_back, vector_again = (
        lax.all_gather(attention_weights.astype(jnp.bfloat16), ("fsdp", "seq"), axis=1, tiled=True),
        lax.all_gather(
            feedforward_weights.astype(jnp.bfloat16), ("fsdp", "seq"), axis=1, tiled=True
        ),
        lax.all_gather(layer_vectors.astype(jnp.bfloat16), ("fsdp", "seq"), axis=1, tiled=True),
    )
    vector_back = vector_again.astype(jnp.float32)
    grad_out = grad_here.reshape(-1, D).astype(jnp.float32)
    grad_gain_second = jnp.sum(grad_out * second_normed, axis=0)
    grad_shift_second = jnp.sum(grad_out, axis=0)
    grad_second = norm_back(grad_out * vector_back[2, 2 * D : 3 * D], second_normed, second_inverse)
    grad_feed = grad_second.astype(jnp.bfloat16)
    grad_bias_down = jnp.sum(grad_feed.astype(jnp.float32), axis=0)
    grad_down = contract_rows(grad_feed, activated)
    grad_activated = plain_dot(grad_feed, feedforward_back[:, FF:])
    grad_up = (grad_activated * gelu_slope(up_value)).astype(jnp.bfloat16)
    grad_bias_up = jnp.sum(grad_up.astype(jnp.float32), axis=0)
    grad_up_weight = contract_rows(first_norm, grad_up)
    grad_first = grad_second + contract_columns(grad_up, feedforward_back[:, :FF])
    grad_feedforward = jnp.concatenate([grad_up_weight, grad_down], axis=1)
    grad_gain_first = jnp.sum(grad_first * first_normed, axis=0)
    grad_shift_first = jnp.sum(grad_first, axis=0)
    grad_stream = norm_back(grad_first * vector_back[2, :D], first_normed, first_inverse)
    grad_attention_out = grad_stream.astype(jnp.bfloat16)
    grad_bias_out = jnp.sum(grad_attention_out.astype(jnp.float32), axis=0)
    grad_out_weight = contract_rows(context_low, grad_attention_out)
    grad_context = contract_columns(grad_attention_out, attention_back[:, 3 * D :]).astype(
        jnp.bfloat16
    )
    grad_query, grad_key_rows, grad_value_rows = lax.map(
        attend_back,
        (
            query_blocks,
            key_blocks,
            value_blocks,
            query_id_blocks,
            key_id_blocks,
            log_total,
            grad_context.reshape(block_count, group_rows, work_span, HEADS, HEAD_DIM),
        ),
    )
    key_share, value_share = (
        lax.psum_scatter(
            grad_key_rows.reshape(row_count, full_length, D).astype(jnp.bfloat16),
            "seq",
            scatter_dimension=1,
            tiled=True,
        ).astype(jnp.float32),
        lax.psum_scatter(
            grad_value_rows.reshape(row_count, full_length, D).astype(jnp.bfloat16),
            "seq",
            scatter_dimension=1,
            tiled=True,
        ).astype(jnp.float32),
    )
    grad_query_low = grad_query.reshape(-1, D).astype(jnp.bfloat16) * score_scale
    grad_key_low = key_share.reshape(-1, D).astype(jnp.bfloat16)
    grad_value_low = value_share.reshape(-1, D).astype(jnp.bfloat16)
    grad_projected = jnp.concatenate([grad_query_low, grad_key_low, grad_value_low], axis=1)
    grad_bias_query = jnp.sum(grad_query_low.astype(jnp.float32), axis=0)
    grad_bias_value = jnp.sum(grad_value_low.astype(jnp.float32), axis=0)
    grad_in_weight = contract_rows(tokens, grad_projected)
    input_rows = (
        grad_stream + contract_columns(grad_projected, attention_back[:, : 3 * D])
    ).astype(jnp.bfloat16)
    input_rows = input_rows.reshape(row_count, work_span, D)
    grad_attention = jnp.concatenate([grad_in_weight, grad_out_weight], axis=1)
    grad_vectors = jnp.stack(
        [
            jnp.concatenate([grad_bias_query, grad_bias_value, grad_bias_out, grad_bias_down]),
            grad_bias_up,
            jnp.concatenate(
                [grad_gain_first, grad_shift_first, grad_gain_second, grad_shift_second]
            ),
        ]
    )
    attention_share, feedforward_share, vector_share = (
        lax.psum_scatter(grad_attention, ("fsdp", "seq"), scatter_dimension=1, tiled=True),
        lax.psum_scatter(grad_feedforward, ("fsdp", "seq"), scatter_dimension=1, tiled=True),
        lax.psum_scatter(grad_vectors, ("fsdp", "seq"), scatter_dimension=1, tiled=True),
    )
    attention_new, attention_first_new, attention_second_new, attention_low = adamw_update(
        attention_weights,
        attention_share,
        attention_first,
        attention_second,
        rate_attention,
        weight_decay,
    )
    feedforward_new, feedforward_first_new, feedforward_second_new, feedforward_low = adamw_update(
        feedforward_weights,
        feedforward_share,
        feedforward_first,
        feedforward_second,
        rate_feedforward,
        weight_decay,
    )
    vectors_new, vector_first_new, vector_second_new, vectors_low = adamw_update(
        layer_vectors, vector_share, vector_first, vector_second, rate_vectors, 0.0
    )
    return (
        output_rows,
        input_rows,
        pooled,
        stream_rms,
        attention_new,
        attention_first_new,
        attention_second_new,
        attention_low,
        feedforward_new,
        feedforward_first_new,
        feedforward_second_new,
        feedforward_low,
        vectors_new,
        vector_first_new,
        vector_second_new,
        vectors_low,
    )


MESH = pl.DeviceIdType.MESH
F32 = jnp.float32
BF16 = jnp.bfloat16

NZ, NX, NC, NY = 4, 2, 2, 2
ROW = 512
OWN_ROWS = 2
TOKENS = OWN_ROWS * ROW
SHARD_A = 96
SHARD_F = 192
EXTRA = 16
FULL_A = SHARD_A + EXTRA
PIECES = 3
PIECE = SHARD_F // PIECES
BLOCK = FF // PIECES
SPLIT_F = 48
SIZES_F = (SPLIT_F, PIECE - SPLIT_F)
GATHER_A = ((48, 16), (32, 16))
SCATTER_A = ((48, 16), (32, 16))
SCATTER_O = (64, 48)


def tn_dot(left_side, right_side):
    return contract_rows(left_side, right_side)


def nt_dot(left_side, right_side):
    return contract_columns(left_side, right_side)


def column_sum(value):
    return jnp.sum(value, axis=0, keepdims=True)


def row_mean(value):
    return jnp.mean(value, axis=-1, keepdims=True)


def remote(src, dst, send, recv, where):
    return pltpu.make_async_remote_copy(
        src_ref=src,
        dst_ref=dst,
        send_sem=send,
        recv_sem=recv,
        device_id=where,
        device_id_type=MESH,
    )


PLAN = (
    (0, 15, 30, 45), (), (16, 282), (1,), (),
    (
        17, 18, 23, 46, 2, 3, 8, 31, 60, 75, 19, 20, 47, 48, 9, 4, 5, 32,
        33, 90, 105, 10, 21, 22, 283, 49, 50, 38, 6, 7, 28, 29, 34, 35, 24, 51,
        52, 11, 12, 76, 25, 53, 13, 14, 36, 37, 39, 40, 61, 77, 78, 106, 26, 27,
        41, 42, 43, 44, 54, 55, 62, 63, 91, 120, 135, 79, 80, 58, 59, 56, 57, 68,
        83, 107, 108,
    ),
    (84, 85), (), (64, 65, 69, 70, 113), (81, 82, 86, 87, 92, 93, 109, 110, 98, 114, 115, 136),
    (284,), (88, 89, 66, 67, 116, 117), (143, 285), (), (71, 72, 111, 112, 94, 95, 121),
    (73, 74, 137, 138), (99, 100), (), (96, 97), (101, 102), (122, 123), (128, 139, 140), (),
    (103, 104), (), (124, 125), (), (118, 119, 129, 141, 142, 144, 145, 130),
    (126, 127, 146, 147, 148, 149), (), (131, 132), (133, 134), (), (), (), (), (), (), (), (),
    (), (150, 161), (), (151, 152, 162, 163), (), (153, 154, 164, 165, 172, 183), (),
    (173, 174, 184, 185), (155, 156), (166, 167, 186, 187, 194, 205), (), (), (175, 176), (), (),
    (), (), (195,), (196, 206, 207), (157, 158, 168, 169), (), (188, 189, 208, 209), (216, 227),
    (177, 178, 217, 218, 228, 229), (159, 170, 190, 191, 197, 198), (210, 211), (160, 231),
    (179, 180, 192), (), (199, 200, 212, 213, 220, 286), (171, 193), (), (181, 233),
    (201, 202, 214), (), (182, 215), (), (222,), (235,), (), (203,), (236,), (), (238, 249),
    (224, 237, 204, 239, 240, 250, 251, 287),
    (
        260, 271, 225, 252, 255, 261, 241, 244, 262, 272, 273, 254, 257, 256, 243, 246, 258, 263,
        266, 245, 277, 226, 274, 268, 259, 279, 265, 247, 276, 248, 267, 278, 269, 280, 270, 281,
    ),

)


class Place:
    def __init__(self):
        f = lax.axis_index("fsdp")
        self.z = f // (NX * NC)
        self.x = (f // NC) % NX
        self.c = f % NC
        self.y = lax.axis_index("seq")

    def at(self, z=None, x=None, c=None, y=None):
        z = self.z if z is None else z
        x = self.x if x is None else x
        c = self.c if c is None else c
        y = self.y if y is None else y
        return ((z * NX + x) * NC + c, y)

    def core(self):
        return self.at(c=1 - self.c)

    def first(self, order):
        return self.at(y=1 - self.y) if order == 0 else self.at(x=1 - self.x)

    def last(self, order):
        return self.at(x=1 - self.x) if order == 0 else self.at(y=1 - self.y)


class Gather:
    def __init__(self, me, buf, start, size, order, index, sems):
        self.me, self.buf, self.order, self.index = me, buf, order, index
        self.rows = pl.ds(start, size)
        self.sems = sems

    def own(self):
        me = self.me
        return self.buf.at[me.z, me.x, me.c, me.y, self.rows]

    def near(self):
        me = self.me
        if self.order == 0:
            return self.buf.at[me.z, me.x, me.c, 1 - me.y, self.rows]
        return self.buf.at[me.z, 1 - me.x, me.c, me.y, self.rows]

    def bundle(self, zz, far):
        me = self.me
        if self.order == 0:
            x = 1 - me.x if far else me.x
            return self.buf.at[zz, x, me.c, :, self.rows]
        y = 1 - me.y if far else me.y
        return self.buf.at[zz, :, me.c, y, self.rows]

    def quad(self, zz, other):
        c = 1 - self.me.c if other else self.me.c
        return self.buf.at[zz, :, c, :, self.rows]

    def first_copy(self, arriving=False):
        s, i = self.sems, self.index
        ref = self.near() if arriving else self.own()
        return remote(ref, ref, s.a_s.at[i], s.a_r.at[i], self.me.first(self.order))

    def line_copy(self, zz, up):
        s, i = self.sems, self.index
        ref = self.bundle(zz, False)
        step = 1 if up else -1
        return remote(
            ref,
            ref,
            (s.up_s if up else s.dn_s).at[i, zz],
            s.z_r.at[i, zz],
            self.me.at(z=self.me.z + step),
        )

    def last_copy(self, zz, arriving=False):
        s, i = self.sems, self.index
        ref = self.bundle(zz, arriving)
        return remote(ref, ref, s.b_s.at[i, zz], s.b_r.at[i, zz], self.me.last(self.order))

    def core_copy(self, zz, arriving=False):
        s, i = self.sems, self.index
        ref = self.quad(zz, arriving)
        return remote(ref, ref, s.c_s.at[i, zz], s.c_r.at[i, zz], self.me.core())

    def one_way(self, step, up, act):
        zz = self.me.z - step if up else self.me.z + step
        pl.when((zz >= 0) if up else (zz < NZ))(lambda: act(zz))

    def send_line(self, zz, up):
        z = self.me.z
        if up:

            @pl.when(z < NZ - 1)
            def _():
                self.line_copy(zz, True).start()

        else:

            @pl.when(z > 0)
            def _():
                self.line_copy(zz, False).start()

    def start(self):
        self.first_copy().start()

    def spread(self):
        self.first_copy(True).wait_recv()
        z = self.me.z
        self.send_line(z, True)
        self.send_line(z, False)
        self.last_copy(z).start()

    def line(self, step, up):
        def act(zz):
            self.line_copy(zz, up).wait_recv()
            self.send_line(zz, up)
            self.last_copy(zz).start()

        self.one_way(step, up, act)

    def cross(self, step, up):
        def act(zz):
            self.last_copy(zz, True).wait_recv()
            self.core_copy(zz).start()

        self.one_way(step, up, act)

    def finish(self):
        for zz in range(NZ):
            self.core_copy(zz, True).wait_recv()

    def events(self):
        ways = ((1, True), (1, False), (2, True), (2, False), (3, True), (3, False))
        return (
            [self.start, self.spread]
            + [functools.partial(self.line, *way) for way in ways]
            + [functools.partial(self.cross, *way) for way in ((0, True),) + ways]
        )

    def drain(self):
        z = self.me.z
        self.first_copy().wait_send()
        for zz in range(NZ):
            self.last_copy(zz).wait_send()
            self.core_copy(zz).wait_send()

            @pl.when((zz <= z) & (z < NZ - 1))
            def _():
                self.line_copy(zz, True).wait_send()

            @pl.when((zz >= z) & (z > 0))
            def _():
                self.line_copy(zz, False).wait_send()


class Scatter:
    def __init__(self, me, buf, targets, start, size, order, index, sems, landing, out, slot, credits):
        self.me, self.buf, self.order, self.index = me, buf, order, index
        self.rows = pl.ds(start, size)
        self.lo, self.hi = targets
        self.sems = sems
        self.rc, self.rb, self.rz, self.ra = landing
        self.out = out
        self.slot = pl.ds(slot, size)
        self.after, self.before = credits

    def part(self, zz, far, other=False):
        me = self.me
        c = 1 - me.c if other else me.c
        if self.order == 0:
            return self.buf.at[zz, 1 - me.x if far else me.x, c, :, self.rows]
        return self.buf.at[zz, :, c, 1 - me.y if far else me.y, self.rows]

    def planes(self, far, other):
        me = self.me
        c = 1 - me.c if other else me.c
        if self.order == 0:
            return self.buf.at[self.planes_z(), 1 - me.x if far else me.x, c, :, self.rows]
        return self.buf.at[self.planes_z(), :, c, 1 - me.y if far else me.y, self.rows]

    def planes_z(self):
        return pl.ds(self.lo, self.hi - self.lo)

    def got_core(self, far, zz=None):
        half = 1 if far else 0
        if zz is None:
            return self.rc.at[half, 0 : self.hi - self.lo, :, self.slot]
        return self.rc.at[half, zz - self.lo, :, self.slot]

    def core_copy(self, far):
        s, i = self.sems, self.index
        half = 1 if far else 0
        return remote(
            self.planes(far, True),
            self.got_core(far),
            s.rc_s.at[i, half],
            s.rc_r.at[i, half],
            self.me.core(),
        )

    def last_copy(self, zz):
        s, i = self.sems, self.index
        return remote(
            self.part(zz, True),
            self.rb.at[zz - self.lo],
            s.rb_s.at[i, zz],
            s.rb_r.at[i, zz],
            self.me.last(self.order),
        )

    def line_slot(self, zz, at, down):
        if self.hi - self.lo == 1:
            return zz - self.lo
        return zz if down else jnp.where(zz == at, NZ, zz)

    def line_copy(self, zz, down):
        s, i = self.sems, self.index
        to = self.me.z - 1 if down else self.me.z + 1
        slot = self.line_slot(zz, to, down)
        return remote(
            self.part(zz, False),
            self.rz.at[slot],
            s.rz_s.at[i, zz],
            s.rz_r.at[i, slot],
            self.me.at(z=to),
        )

    def line_wait(self, slot):
        s, i = self.sems, self.index
        remote(
            self.rz.at[slot],
            self.rz.at[slot],
            s.rz_s.at[i, 0],
            s.rz_r.at[i, slot],
            self.me.core(),
        ).wait_recv()

    def home(self, mine):
        me = self.me
        if self.order == 0:
            y = me.y if mine else 1 - me.y
            return self.buf.at[me.z, me.x, me.c, y, self.rows], y
        x = me.x if mine else 1 - me.x
        return self.buf.at[me.z, x, me.c, me.y, self.rows], x

    def first_copy(self):
        s, i = self.sems, self.index
        return remote(
            self.home(False)[0],
            self.ra,
            s.ra_s.at[i],
            s.ra_r.at[i],
            self.me.first(self.order),
        )

    def by_distance(self, dist, act):
        act_down, act_up = (lambda zz: act(zz, True)), (lambda zz: act(zz, False))
        self.one_way(dist, True, act_down)
        if dist > 0:
            self.one_way(dist, False, act_up)

    def aims(self, zz):
        return (zz >= self.lo) & (zz < self.hi)

    def one_way(self, dist, down, act):
        zz = self.me.z - dist if down else self.me.z + dist
        pl.when(self.aims(zz))(lambda: act(zz))

    def start(self):
        if self.after is not None:
            pl.semaphore_wait(self.after, 1)
        self.core_copy(True).start()
        self.core_copy(False).start()

    def cross(self):
        self.core_copy(True).wait_recv()
        for dist in range(NZ - 1, -1, -1):

            def act(zz, down):
                ref = self.part(zz, True)
                got = self.got_core(True, zz)
                ref[...] = (ref[...].astype(F32) + got[...].astype(F32)).astype(BF16)
                self.last_copy(zz).start()

            self.by_distance(dist, act)

    def keep(self):
        self.core_copy(False).wait_recv()
        for zz in range(self.lo, self.hi):
            ref = self.part(zz, False)
            got = self.got_core(False, zz)
            ref[...] = (ref[...].astype(F32) + got[...].astype(F32)).astype(BF16)
        if self.before is not None:
            pl.semaphore_signal(
                self.before, inc=1, device_id=self.me.core(), device_id_type=MESH
            )

    def line(self, dist, down):
        z = self.me.z

        def act(zz):
            self.last_copy(zz).wait_recv()
            ref = self.part(zz, False)
            outer = z < NZ - 1 if down else z > 0
            total = ref[...].astype(F32) + self.rb[zz - self.lo].astype(F32)
            slot = self.line_slot(zz, z, True)

            @pl.when(outer)
            def _():
                self.line_wait(slot)
                ref[...] = (total + self.rz[slot].astype(F32)).astype(BF16)

            @pl.when(jnp.logical_not(outer))
            def _():
                ref[...] = total.astype(BF16)

            self.line_copy(zz, down).start()

        self.one_way(dist, down, act)

    def events(self):
        ways = ((3, True), (3, False), (2, True), (2, False), (1, True), (1, False))
        return (
            [self.start, self.cross, self.keep]
            + [functools.partial(self.line, *way) for way in ways]
            + [self.settle, self.finish]
        )

    def settle(self):
        pl.when(self.aims(self.me.z))(self.settle_here)

    def settle_here(self):
        z = self.me.z
        self.last_copy(z).wait_recv()
        far_ref, far = self.home(False)
        near_ref, near = self.home(True)
        here = z - self.lo
        above, below = self.line_slot(z, z, True), self.line_slot(z, z, False)
        self.out[self.rows, :] = near_ref[...].astype(F32) + self.rb[here, near].astype(F32)
        total = far_ref[...].astype(F32) + self.rb[here, far].astype(F32)

        @pl.when(z == 0)
        def _():
            self.line_wait(above)
            far_ref[...] = (total + self.rz[above, far].astype(F32)).astype(BF16)
            self.out[self.rows, :] += self.rz[above, near].astype(F32)

        @pl.when(z == NZ - 1)
        def _():
            self.line_wait(below)
            far_ref[...] = (total + self.rz[below, far].astype(F32)).astype(BF16)
            self.out[self.rows, :] += self.rz[below, near].astype(F32)

        @pl.when((z > 0) & (z < NZ - 1))
        def _():
            self.line_wait(above)
            self.line_wait(below)
            far_ref[...] = (
                total + (self.rz[above, far].astype(F32) + self.rz[below, far].astype(F32))
            ).astype(BF16)
            self.out[self.rows, :] += self.rz[above, near].astype(F32) + self.rz[
                below, near
            ].astype(F32)

        self.first_copy().start()

    def finish(self):
        @pl.when(self.aims(self.me.z))
        def _():
            self.first_copy().wait_recv()
            self.out[self.rows, :] += self.ra[...].astype(F32)

    def drain(self):
        z = self.me.z
        self.core_copy(True).wait_send()
        self.core_copy(False).wait_send()
        pl.when(self.aims(z))(lambda: self.first_copy().wait_send())
        for zz in range(self.lo, self.hi):
            self.last_copy(zz).wait_send()

            @pl.when(zz < z)
            def _():
                self.line_copy(zz, True).wait_send()

            @pl.when(zz > z)
            def _():
                self.line_copy(zz, False).wait_send()


class Schedule:
    def __init__(self, events):
        self.events, self.place = events, 0

    def take(self):
        chosen = PLAN[self.place]
        self.place += 1

        def run():
            for number in chosen:
                self.events[number]()

        return run if chosen else None

    def step(self, count=1):
        for _ in range(count):
            run = self.take()
            if run is not None:
                run()

    def loop(self, count, body):
        runs = [self.take() for _ in range(count)]

        @pl.loop(0, count)
        def _(i):
            body(i)
            for place, run in enumerate(runs):
                if run is not None:
                    pl.when(i == place)(run)


def repeat(count, body):
    pl.loop(0, count)(body)


def flatten(value):
    return value.reshape(-1, value.shape[-1])


def masked_halves(pair, other):
    first = lax.broadcasted_iota(jnp.int32, pair.shape, 1) < HEAD_DIM
    return jnp.where(first, pair, other), jnp.where(first, other, pair)


def attention_pair(queries, keys, values, ask, bar):
    values_turned = values.T
    queries_halves, keys_halves = masked_halves(queries, ask), masked_halves(keys, bar)
    scores = [nt_dot(keys_halves[half], queries_halves[half]) for half in range(2)]
    contexts, totals = [], []
    for half in range(2):
        largest = jnp.max(scores[half], axis=0, keepdims=True)
        exponent = jnp.exp(scores[half] - largest)
        total = column_sum(exponent)
        context = plain_dot(
            values_turned[half * HEAD_DIM : (half + 1) * HEAD_DIM, :], exponent.astype(BF16)
        )
        contexts.append(context * (1.0 / total))
        totals.append(largest + jnp.log(total))
    return jnp.concatenate(contexts, 0).T, jnp.concatenate(totals, 0)


def attention_pair_back(queries, keys, values, grad_context, ask, bar, log_total):
    keys_turned = keys.T
    zero = jnp.zeros_like(keys)
    queries_asked, keys_barred = masked_halves(queries, ask), masked_halves(keys, bar)
    queries_alone, values_alone = masked_halves(queries, zero), masked_halves(values, zero)
    grad_alone = masked_halves(grad_context, zero)
    width = ROW // 2
    parts = [(slice(0, width), 0), (slice(0, width), 1), (slice(width, ROW), 0), (slice(width, ROW), 1)]

    def scores_of(part):
        span, half = part
        return (
            nt_dot(keys_barred[half], queries_asked[half][span]),
            nt_dot(values_alone[half], grad_context[span]),
        )

    ahead = [scores_of(part) for part in parts[:2]]
    grad_queries = []
    grad_keys = grad_values = 0.0
    for place, (span, half) in enumerate(parts):
        if place + 2 < len(parts):
            ahead.append(scores_of(parts[place + 2]))
        scores, grad_soft = ahead[place]
        soft = jnp.exp(scores - log_total[half : half + 1, span])
        inner = column_sum(soft * grad_soft)
        grad_scores = (soft * (grad_soft - inner)).astype(BF16)
        grad_values += plain_dot(soft.astype(BF16), grad_alone[half][span])
        grad_keys += plain_dot(grad_scores, queries_alone[half][span])
        grad_queries.append(
            plain_dot(keys_turned[half * HEAD_DIM : (half + 1) * HEAD_DIM, :], grad_scores)
        )
    grad_queries = [jnp.concatenate(grad_queries[i : i + 2], 0).T for i in (0, 2)]
    return jnp.concatenate(grad_queries, 0), grad_keys, grad_values


def select_columns(permuted):
    row = lax.broadcasted_iota(jnp.int32, (8 * 128, D), 0)
    col = lax.broadcasted_iota(jnp.int32, (8 * 128, D), 1)
    lane = row % 128
    source = (row // 128) * SHARD_A + lane
    if permuted:
        piece = col // 256
        rest = col % 256
        col = (rest // PIECE) * SHARD_F + piece * PIECE + rest % PIECE
    return jnp.where((source == col) & (lane < SHARD_A), 1.0, 0.0).astype(BF16)


SEM_SHAPES = dict(
    a_s=(10,),
    a_r=(10,),
    z_r=(10, NZ),
    up_s=(10, NZ),
    dn_s=(10, NZ),
    b_s=(10, NZ),
    b_r=(10, NZ),
    c_s=(10, NZ),
    c_r=(10, NZ),
    rc_s=(12, 2),
    rc_r=(12, 2),
    rb_s=(12, NZ),
    rb_r=(12, NZ),
    rz_s=(12, NZ),
    rz_r=(12, NZ + 1),
    ra_s=(12,),
    ra_r=(12,),
    x_s=(4, 2),
    x_r=(4, 2),
    own=(4, 2),
    pool_s=(1,),
    pool_r=(1,),
    stat_s=(5,),
    stat_r=(5,),
    load=(2,),
)


def gather_pieces():
    return [(0, *GATHER_A[0]), (sum(GATHER_A[0]), *GATHER_A[1])] + [
        (k * PIECE, SPLIT_F, PIECE - SPLIT_F) for k in range(PIECES)
    ]


def scatter_pieces():
    return (
        gather_pieces()[2:]
        + [(0, *SCATTER_O)]
        + [(0, *SCATTER_A[0]), (sum(SCATTER_A[0]), *SCATTER_A[1])]
    )


def scratch():
    return dict(
        wa=pltpu.VMEM((NZ, NX, NC, NY, FULL_A, D), BF16),
        wf=pltpu.VMEM((NZ, NX, NC, NY, SHARD_F, D), BF16),
        rc=pltpu.VMEM((2, NZ, 2, PIECE, D), BF16),
        xs=pltpu.VMEM((TOKENS, D), BF16),
        dys=pltpu.VMEM((TOKENS, D), BF16),
        ctx=pltpu.VMEM((TOKENS, D), BF16),
        n1=pltpu.VMEM((TOKENS, D), BF16),
        fn=pltpu.VMEM((TOKENS, D), BF16),
        fg=pltpu.VMEM((TOKENS, D), BF16),
        qkv=pltpu.VMEM((TOKENS, 3 * D), BF16),
        act=pltpu.VMEM((PIECES, TOKENS, BLOCK), BF16),
        slope=pltpu.VMEM((PIECES, TOKENS, BLOCK), BF16),
        acc=pltpu.VMEM((TOKENS, D), F32),
        ask=pltpu.VMEM((OWN_ROWS, ROW, 128), BF16),
        bar=pltpu.VMEM((OWN_ROWS, ROW, 128), BF16),
        rco=pltpu.VMEM((2, 1, 2, FULL_A, D), BF16),
        totals=pltpu.VMEM((OWN_ROWS * HEADS // 2, 2, ROW), F32),
        side=pltpu.VMEM((TOKENS, 128), F32),
        vec=pltpu.VMEM((16, 4 * D), F32),
        bu=pltpu.VMEM((PIECES, 16, BLOCK), F32),
        gvec=pltpu.VMEM((8, 4 * D), F32),
        gbu=pltpu.VMEM((PIECES, 8, BLOCK), F32),
        stat=pltpu.VMEM((8, 128), F32),
        stat_in=pltpu.VMEM((5, 8, 128), F32),
        pool_out=pltpu.VMEM((OWN_ROWS, 8, D), F32),
        vector_pad=pltpu.VMEM((EXTRA, 128), F32),
        pool_in=pltpu.VMEM((OWN_ROWS, 8, D // 2), F32),
        credit=pltpu.SemaphoreType.REGULAR((2,)),
        free=pltpu.SemaphoreType.REGULAR,
    )


def landing_shapes():
    shapes = []
    for sizes, targets in ((SIZES_F, NZ),) * PIECES + ((SCATTER_O, 1),):
        for size in sizes:
            shapes += [
                pltpu.VMEM((targets, 2, size, D), BF16),
                pltpu.VMEM((targets + 1 if targets > 1 else 1, 2, size, D), BF16),
                pltpu.VMEM((size, D), BF16),
            ]
    return shapes


def fused_kernel(
    x_in,
    dy_in,
    wa_in,
    wf_in,
    vector_in,
    ids,
    flags,
    out_y,
    out_dx,
    out_pooled,
    out_stats,
    grad_a,
    grad_f,
    *more,
):
    names, sem_names = tuple(scratch()), tuple(SEM_SHAPES)
    landings = len(landing_shapes())
    r = types.SimpleNamespace(**dict(zip(names, more)))
    landing_refs = more[len(names) : len(names) + landings]
    sems = types.SimpleNamespace(**dict(zip(sem_names, more[len(names) + landings :])))
    me = Place()
    z, x, c, y = me.z, me.x, me.c, me.y
    wa, wf, xs, dys, ctx = r.wa, r.wf, r.xs, r.dys, r.ctx
    n1, fn, fg, qkv, acc = r.n1, r.fn, r.fg, r.qkv, r.acc
    act, slope, vec, gvec, stat = r.act, r.slope, r.vec, r.gvec, r.stat

    def tile(i, size):
        return pl.ds(pl.multiple_of(i * size, size), size)

    def row_ids(slot):
        return ids[pl.ds(2 * y + slot, 1), :]

    def row_flags(slot):
        return flags[pl.ds(2 * y + slot, 1), :].astype(F32)

    def vector(row, quarter):
        return vec[row : row + 1, quarter * D : (quarter + 1) * D]

    barrier = pltpu.get_barrier_semaphore()
    for where in (
        me.core(),
        me.at(x=1 - x),
        me.at(y=1 - y),
        me.at(z=(z + 2) % NZ),
    ):
        pl.semaphore_signal(barrier, inc=1, device_id=where, device_id_type=MESH)

    @pl.when(z > 0)
    def _():
        pl.semaphore_signal(barrier, inc=1, device_id=me.at(z=z - 1), device_id_type=MESH)

    @pl.when(z < NZ - 1)
    def _():
        pl.semaphore_signal(barrier, inc=1, device_id=me.at(z=z + 1), device_id_type=MESH)

    own_a, own_f = acc.at[0:SHARD_A], acc.at[SHARD_A : SHARD_A + SHARD_F]
    load_a = pltpu.make_async_copy(wa_in, own_a, sems.load.at[0])
    load_f = pltpu.make_async_copy(wf_in, own_f, sems.load.at[1])
    load_a.start()
    load_f.start()
    r.vector_pad[...] = jnp.zeros_like(r.vector_pad)
    r.vector_pad[0:3, 0:SHARD_A] = vector_in[...]
    wa[z, x, c, y, SHARD_A:FULL_A, :] = jnp.zeros((EXTRA, D), BF16)
    wa[z, x, c, y, SHARD_A:FULL_A, 0:128] = r.vector_pad[...].astype(BF16)

    def row_copy(kind, src, dst, slot):
        return remote(
            src, dst, sems.x_s.at[kind, slot], sems.x_r.at[kind, slot], me.at(y=1 - y)
        )

    def own_copy(kind, src, dst, slot):
        return pltpu.make_async_copy(src, dst, sems.own.at[kind, slot])

    def span(slot, half):
        return pl.ds(pl.multiple_of(slot * ROW + half * (ROW // 2), ROW // 2), ROW // 2)

    def take_rows(kind, source, target):
        sends = [
            row_copy(kind, source.at[2 * (1 - y) + slot], target.at[span(slot, y)], slot)
            for slot in range(OWN_ROWS)
        ]
        owns = [
            own_copy(kind, source.at[2 * y + slot], target.at[span(slot, y)], slot)
            for slot in range(OWN_ROWS)
        ]
        arrivals = [
            row_copy(kind, source.at[2 * y + slot], target.at[span(slot, 1 - y)], slot)
            for slot in range(OWN_ROWS)
        ]
        return sends, owns, arrivals

    def give_rows(kind, source, target):
        sends = [
            row_copy(kind, source.at[span(slot, 1 - y)], target.at[2 * y + slot], slot)
            for slot in range(OWN_ROWS)
        ]
        owns = [
            own_copy(kind, source.at[span(slot, y)], target.at[2 * y + slot], slot)
            for slot in range(OWN_ROWS)
        ]
        arrivals = [
            row_copy(kind, source.at[span(slot, y)], target.at[2 * (1 - y) + slot], slot)
            for slot in range(OWN_ROWS)
        ]
        return sends, owns, arrivals

    x_sends, x_owns, x_arrivals = take_rows(0, x_in, xs)
    dy_sends, dy_owns, dy_arrivals = take_rows(1, dy_in, dys)
    out_sends, out_owns, out_arrivals = give_rows(2, dys, out_y)
    dx_sends, dx_owns, dx_arrivals = give_rows(3, n1, out_dx)

    def start_all(copies):
        def run():
            for copy in copies:
                copy.start()

        return run

    gathers, scatters = [], []
    for piece, (first_row, *sizes) in enumerate(gather_pieces()):
        for order in range(2):
            buf = wa if piece < 2 else wf
            start = first_row + order * sizes[0]
            gathers.append(Gather(me, buf, start, sizes[order], order, 2 * piece + order, sems))
    places = (0, 1, 2, 3, 0, 1)
    for piece, (first_row, *sizes) in enumerate(scatter_pieces()):
        lone = piece == PIECES
        targets = (0, NZ) if piece < PIECES else (NZ - 1, NZ) if lone else (0, NZ - 1)
        for order in range(2):
            size, i = sizes[order], 2 * places[piece] + order
            landing = (
                r.rco if lone else r.rc,
                landing_refs[3 * i].at[:, :, 0:size],
                landing_refs[3 * i + 1].at[:, :, 0:size],
                landing_refs[3 * i + 2].at[0:size],
            )
            credit = r.credit.at[order]
            credits = (
                None if lone or piece == 0 else credit,
                None if lone or piece == len(places) - 1 else credit,
            )
            slot = order * sizes[0]
            scatters.append(
                Scatter(
                    me, wa if lone else wf, targets, first_row + slot, size, order,
                    2 * piece + order, sems, landing, grad_f if piece < PIECES else grad_a, slot,
                    credits,
                )
            )

    exchange = [copy.start for copy in x_sends + dy_sends + dx_sends]
    events = [event for one in gathers + scatters for event in one.events()] + exchange
    plan = Schedule(events)

    for copy in x_owns + dy_owns:
        copy.start()
    line_ends = jnp.where(z > 0, 1, 0).astype(jnp.int32) + jnp.where(z < NZ - 1, 1, 0).astype(
        jnp.int32
    )
    load_a.wait()
    wa[z, x, c, y, 0:SHARD_A, :] = own_a[...].astype(BF16)
    pl.semaphore_wait(barrier, 4 + line_ends)
    plan.step()
    load_f.wait()
    wf[z, x, c, y] = own_f[...].astype(BF16)
    plan.step()

    gvec[...] = jnp.zeros_like(gvec)
    r.gbu[...] = jnp.zeros_like(r.gbu)
    stat[...] = jnp.zeros_like(stat)
    for slot in range(OWN_ROWS):
        wide = jnp.broadcast_to(row_ids(slot).astype(F32), (128, ROW))
        tall = wide.T
        flag_rows = jnp.broadcast_to(row_flags(slot), (128, ROW))
        r.side[slot * ROW : (slot + 1) * ROW, :] = flag_rows.T
        lane = lax.broadcasted_iota(jnp.int32, (ROW, 128), 1) % HEAD_DIM
        same = tall == lane.astype(F32)
        r.ask[slot] = jnp.where(same & (lane < SEGMENTS), 1.0, 0.0).astype(BF16)
        r.bar[slot] = jnp.where(same | (lane >= SEGMENTS), 0.0, masked_score).astype(BF16)
        plan.step()
    ctx[...] = select_columns(False)
    fg[...] = select_columns(True)
    plan.step()
    plan.step()
    for one in gathers[:4]:
        one.finish()

    for q in range(4):
        blocks = jnp.concatenate(
            [
                wa[q, j // 4, (j // 2) % 2, j % 2, SHARD_A:FULL_A, 0:128]
                for j in range(8)
            ],
            axis=1,
        )
        vec[:, q * D : (q + 1) * D] = plain_dot(blocks, ctx[...])
        moved = plain_dot(blocks, fg[...])
        for k in range(PIECES):
            r.bu[k, :, q * 256 : (q + 1) * 256] = moved[:, k * 256 : (k + 1) * 256]

    plan.step(2)
    for copy in x_owns:
        copy.wait()
    for copy in x_arrivals:
        copy.wait_recv()

    scale = HEAD_DIM ** (-0.5)

    def project(i):
        rows = tile(i, 512)
        tokens = xs[rows, :]
        wide = tokens.astype(F32)
        stat[0:1, :] += lane_sums(wide * wide * r.side[rows, 1:2])
        for j in range(3):
            weights = flatten(wa[j, :, :, :, 0:SHARD_A, :])
            value = nt_dot(tokens, weights)
            if j == 0:
                value = (value + vector(0, 0)) * scale
            if j == 2:
                value = value + vector(0, 1)
            qkv[rows, j * D : (j + 1) * D] = value.astype(BF16)

    def lane_sums(value):
        total = column_sum(value)
        return sum(total[:, j * 128 : (j + 1) * 128] for j in range(D // 128))

    plan.loop(2, project)

    def columns(pair, block):
        return pl.ds(pl.multiple_of(block * D + pair * 128, 128), 128)

    def attend(i):
        slot, pair = i // (HEADS // 2), i % (HEADS // 2)
        rows = tile(slot, ROW)
        context, total = attention_pair(
            qkv[rows, columns(pair, 0)],
            qkv[rows, columns(pair, 1)],
            qkv[rows, columns(pair, 2)],
            r.ask[slot],
            r.bar[slot],
        )
        ctx[rows, columns(pair, 0)] = context.astype(BF16)
        r.totals[i] = total

    plan.loop(OWN_ROWS * HEADS // 2, attend)

    def attention_output(i):
        rows = tile(i, 256)
        weights = flatten(wa[3, :, :, :, 0:SHARD_A, :])
        out = nt_dot(ctx[rows, :], weights) + vector(0, 2)
        stat[1:2, :] += lane_sums(out * out * r.side[rows, 1:2])
        normed, inverse = normalize(xs[rows, :].astype(F32) + out)
        n1[rows, :] = normed.astype(BF16)
        r.side[rows, 0:1] = inverse
        fn[rows, :] = (normed * vector(2, 0) + vector(2, 1)).astype(BF16)

    plan.loop(4, attention_output)

    def up_rows(k):
        return flatten(flatten_lead(wf[0:2, :, :, :, k * PIECE : (k + 1) * PIECE, :]))

    def down_rows(k):
        return flatten(flatten_lead(wf[2:4, :, :, :, k * PIECE : (k + 1) * PIECE, :]))

    def flatten_lead(value):
        return value.reshape(-1, PIECE, D)

    for k in range(PIECES):
        plan.step()
        for one in gathers[4 + 2 * k : 6 + 2 * k]:
            one.finish()

        def feed(i, k=k):
            rows = tile(i, 512)
            up = nt_dot(fn[rows, :], up_rows(k)) + r.bu[k, 1:2, :]
            half = 0.5 * (1.0 + lax.erf(up * math.sqrt(0.5)))
            activated = (up * half).astype(BF16)
            act[k, rows, :] = activated
            slope[k, rows, :] = (
                half + up * (jnp.exp(-0.5 * up * up) * (1.0 / math.sqrt(2.0 * math.pi)))
            ).astype(BF16)
            value = plain_dot(activated, down_rows(k))
            if k == 0:
                acc[rows, :] = value
            else:
                acc[rows, :] += value

        plan.loop(2, feed)
    plan.step()

    for copy in dy_owns:
        copy.wait()
    for copy in dy_arrivals:
        copy.wait_recv()
    for one in gathers:
        one.drain()

    def second(i):
        rows = tile(i, 128)
        feed_out = acc[rows, :] + vector(0, 3)
        stat[2:3, :] += lane_sums(feed_out * feed_out * r.side[rows, 1:2])
        normed, inverse = normalize(fn[rows, :].astype(F32) + feed_out)
        grad = dys[rows, :].astype(F32)
        dys[rows, :] = (normed * vector(2, 2) + vector(2, 3)).astype(BF16)
        gvec[2:3, 2 * D : 3 * D] += column_sum(grad * normed)
        gvec[2:3, 3 * D :] += column_sum(grad)
        back = norm_back(grad * vector(2, 2), normed, inverse)
        acc[rows, :] = back
        low = back.astype(BF16)
        fg[rows, :] = low
        gvec[0:1, 3 * D :] += column_sum(low.astype(F32))

    repeat(TOKENS // 128, second)
    plan.step()

    start_all(out_sends + out_owns)()

    segments = lax.broadcasted_iota(jnp.int32, (SEGMENTS, ROW), 0)
    for slot in range(OWN_ROWS):
        member = jnp.where(segments == row_ids(slot), 1.0, 0.0) * row_flags(slot)
        sums = plain_dot(member.astype(BF16), dys[slot * ROW : (slot + 1) * ROW, :])
        counts = jnp.sum(member, axis=1, keepdims=True)
        r.pool_out[slot] = sums / jnp.maximum(counts, 1.0)
        total = row_flags(slot)
        stat[3:4, :] += sum(total[:, j * 128 : (j + 1) * 128] for j in range(ROW // 128))

    def half_lanes(which):
        return pl.ds(pl.multiple_of(which * (D // 2), 128), D // 2)

    pool_copy = remote(
        r.pool_out.at[:, :, half_lanes(1 - y)],
        r.pool_in,
        sems.pool_s.at[0],
        sems.pool_r.at[0],
        me.at(y=1 - y),
    )
    pool_copy.start()

    stat_partners = [
        me.core(),
        me.at(x=1 - x),
        me.at(y=1 - y),
        me.at(z=z + 1 - 2 * (z % 2)),
        me.at(z=(z + 2) % NZ),
    ]

    def stat_copy(step):
        return remote(
            stat,
            r.stat_in.at[step],
            sems.stat_s.at[step],
            sems.stat_r.at[step],
            stat_partners[step],
        )

    def stat_start(step):
        return lambda: stat_copy(step).start()

    def stat_end(step):
        def run():
            stat_copy(step).wait()
            stat[...] += r.stat_in[step]

        return run

    stat_start(0)()
    plan.step()
    for k in range(PIECES):

        def feed_back(i, k=k):
            rows = tile(i, 512)
            grad = nt_dot(fg[rows, :], down_rows(k)) * slope[k, rows, :].astype(F32)
            low = grad.astype(BF16)
            slope[k, rows, :] = low
            r.gbu[k, 0:1, :] += column_sum(low.astype(F32))
            acc[rows, :] += plain_dot(low, up_rows(k))

        plan.loop(2, feed_back)

        def weights_back(i, k=k):
            cols = tile(i, BLOCK // 2)
            down = tn_dot(act[k, :, cols], fg[...]).astype(BF16)
            up = tn_dot(slope[k, :, cols], fn[...]).astype(BF16)
            where = (slice(None), slice(None), slice(None), pl.ds(k * PIECE, PIECE))
            wf[(2 + i, *where)] = down.reshape(NX, NC, NY, PIECE, D)
            wf[(i, *where)] = up.reshape(NX, NC, NY, PIECE, D)

        plan.loop(2, weights_back)
        stat_end(k)()
        stat_start(k + 1)()

    def first(i):
        rows = tile(i, 128)
        grad = acc[rows, :]
        normed = n1[rows, :].astype(F32)
        gvec[2:3, 0:D] += column_sum(grad * normed)
        gvec[2:3, D : 2 * D] += column_sum(grad)
        stream = norm_back(grad * vector(2, 0), normed, r.side[rows, 0:1])
        acc[rows, :] = stream
        low = stream.astype(BF16)
        fg[rows, :] = low
        gvec[0:1, 2 * D : 3 * D] += column_sum(low.astype(F32))

    plan.loop(TOKENS // 128, first)

    def context_back(i):
        rows = tile(i, 512)
        fn[rows, :] = plain_dot(fg[rows, :], flatten(wa[3, :, :, :, 0:SHARD_A, :])).astype(BF16)

    plan.loop(2, context_back)
    stat_end(3)()
    stat_start(4)()

    def outer_back(i):
        cols = pl.ds(pl.multiple_of(i * (D // 2), 128), D // 2)
        value = tn_dot(fg[:, cols], ctx[...]).astype(BF16)
        wa[3, i, :, :, 0:SHARD_A, :] = value.reshape(NC, NY, SHARD_A, D)

    plan.loop(2, outer_back)

    ctx[...] = select_columns(False)
    fg[...] = select_columns(True)

    def vectors_back(q, buf):
        row = lax.broadcasted_iota(jnp.int32, (8, 1), 0)
        plain = nt_dot(gvec[:, q * D : (q + 1) * D].astype(BF16), ctx[...])
        piled = jnp.concatenate(
            [r.gbu[k, :, q * 256 : (q + 1) * 256] for k in range(PIECES)], axis=1
        )
        moved = nt_dot(piled.astype(BF16), fg[...])
        low = jnp.where(row == 1, jnp.broadcast_to(moved[0:1, :], plain.shape), plain)
        low = jnp.concatenate([low, jnp.zeros_like(low)], axis=0).astype(BF16)
        for j in range(8):
            buf[q, j // 4, (j // 2) % 2, j % 2, SHARD_A:FULL_A, 0:128] = low[
                :, j * 128 : (j + 1) * 128
            ]

    vectors_back(3, wa)
    plan.step()

    def attend_back_pair(slot, pair):
        rows = tile(slot, ROW)
        grads = attention_pair_back(
            qkv[rows, columns(pair, 0)],
            qkv[rows, columns(pair, 1)],
            qkv[rows, columns(pair, 2)],
            fn[rows, columns(pair, 0)],
            r.ask[slot],
            r.bar[slot],
            r.totals[slot * (HEADS // 2) + pair],
        )
        for j in range(3):
            low = grads[j].astype(BF16)
            if j == 0:
                low = low * jnp.asarray(scale, BF16)
            qkv[rows, columns(pair, j)] = low
            if j != 1:
                gvec[0:1, columns(pair, j // 2)] += column_sum(low.astype(F32))

    def input_back(slot):
        rows = pl.ds(slot * ROW, ROW)
        value = acc[rows, :]
        for j in range(3):
            value += plain_dot(
                qkv[rows, j * D : (j + 1) * D], flatten(wa[j, :, :, :, 0:SHARD_A, :])
            )
        n1[rows, :] = value.astype(BF16)
        dx_owns[slot].start()

    plan.loop(HEADS // 2, functools.partial(attend_back_pair, 0))
    input_back(0)
    plan.step()
    plan.loop(HEADS // 2, functools.partial(attend_back_pair, 1))
    stat_end(4)()
    plan.step()
    for one in scatters[:4]:
        one.drain()

    free = r.free
    for where in (me.at(x=1 - x), me.at(y=1 - y)):
        pl.semaphore_signal(free, inc=1, device_id=where, device_id_type=MESH)

    @pl.when(z > 0)
    def _():
        pl.semaphore_signal(free, inc=1, device_id=me.at(z=z - 1), device_id_type=MESH)

    @pl.when(z < NZ - 1)
    def _():
        pl.semaphore_signal(free, inc=1, device_id=me.at(z=z + 1), device_id_type=MESH)

    for j in range(3):

        def inner_back(i, j=j):
            cols = pl.ds(pl.multiple_of(j * D + i * (D // 2), 128), D // 2)
            value = tn_dot(qkv[:, cols], xs[...]).astype(BF16)
            wf[j, i, :, :, 0:SHARD_A, :] = value.reshape(NC, NY, SHARD_A, D)

        plan.loop(2, inner_back)
    for q in range(3):
        vectors_back(q, wf)
    pl.semaphore_wait(free, 2 + line_ends)
    plan.step()
    input_back(1)
    plan.step(2)

    assert plan.place == len(PLAN)
    for one in scatters[4:]:
        one.drain()
    pool_copy.wait()
    for slot in range(OWN_ROWS):
        out_pooled[2 * y + slot] = r.pool_out[slot, :, half_lanes(y)]
        out_pooled[2 * (1 - y) + slot] = r.pool_in[slot]
    out_stats[...] = stat[...]
    for copies in (x_sends, dy_sends, out_sends, dx_sends):
        for copy in copies:
            copy.wait_send()
    for copies in (out_owns, dx_owns):
        for copy in copies:
            copy.wait()
    for copies in (out_arrivals, dx_arrivals):
        for copy in copies:
            copy.wait_recv()


def finish_kernel(
    y_in,
    dx_in,
    pooled_in,
    stats,
    grad_a,
    grad_f,
    *more,
):
    states, results, sems = more[:9], more[9:-1], more[-1]
    out_y, out_dx, out_pooled, out_rms = results[:4]
    copies = [
        pltpu.make_async_copy(y_in, out_y, sems.at[0]),
        pltpu.make_async_copy(dx_in, out_dx, sems.at[1]),
    ]
    for copy in copies:
        copy.start()
    out_pooled[...] = pooled_in[...]
    totals = jnp.sum(stats[...], axis=1, keepdims=True)
    rms = jnp.sqrt(totals[0:3] / D / totals[3:4])
    for i in range(3):
        out_rms[i] = rms[i, 0]
    rates = (
        (rate_attention, weight_decay),
        (rate_feedforward, weight_decay),
        (rate_vectors, 0.0),
    )
    gradients = (grad_a.at[0:SHARD_A], grad_f, grad_a.at[SHARD_A : SHARD_A + 3, 0:SHARD_A])
    for i in range(3):
        weight, first, second = states[3 * i : 3 * i + 3]
        new = adamw_update(weight[...], gradients[i][...], first[...], second[...], *rates[i])
        for ref, value in zip(results[4 + 4 * i : 8 + 4 * i], new):
            ref[...] = value
    for copy in copies:
        copy.wait()


def fused_shards(
    inputs,
    segment_ids,
    token_flags,
    output_grad,
    attention_weights,
    feedforward_weights,
    layer_vectors,
    attention_first,
    attention_second,
    feedforward_first,
    feedforward_second,
    vector_first,
    vector_second,
):
    any_space = pl.BlockSpec(memory_space=pl.ANY)
    vmem = pl.BlockSpec(memory_space=pltpu.VMEM)
    smem = pl.BlockSpec(memory_space=pltpu.SMEM)
    rows = jax.ShapeDtypeStruct(inputs.shape, BF16)
    pooled = jax.ShapeDtypeStruct((inputs.shape[0], SEGMENTS, D // NY), F32)
    semaphores = [pltpu.SemaphoreType.DMA(shape) for shape in SEM_SHAPES.values()]
    passed = pl.pallas_call(
        fused_kernel,
        out_shape=(
            rows,
            rows,
            pooled,
            jax.ShapeDtypeStruct((8, 128), F32),
            jax.ShapeDtypeStruct((FULL_A, D), F32),
            jax.ShapeDtypeStruct((SHARD_F, D), F32),
        ),
        in_specs=[any_space] * 4 + [vmem] * 3,
        out_specs=(any_space, any_space, vmem, vmem, vmem, vmem),
        scratch_shapes=list(scratch().values()) + landing_shapes() + semaphores,
        compiler_params=pltpu.CompilerParams(
            collective_id=0, has_side_effects=True, vmem_limit_bytes=65_000 * 1024
        ),
        name="layer",
    )(
        inputs,
        output_grad,
        attention_weights.T,
        feedforward_weights.T,
        layer_vectors,
        segment_ids,
        token_flags,
    )
    states = (
        attention_weights.T,
        attention_first.T,
        attention_second.T,
        feedforward_weights.T,
        feedforward_first.T,
        feedforward_second.T,
        layer_vectors,
        vector_first,
        vector_second,
    )

    def updated(shape):
        wide = jax.ShapeDtypeStruct(shape, F32)
        return (wide, wide, wide, jax.ShapeDtypeStruct(shape, BF16))

    results = pl.pallas_call(
        finish_kernel,
        out_shape=(rows, rows, pooled, jax.ShapeDtypeStruct((3,), F32))
        + updated((SHARD_A, D))
        + updated((SHARD_F, D))
        + updated(layer_vectors.shape),
        in_specs=[vmem] * 15,
        out_specs=(any_space, any_space, vmem, smem) + (vmem,) * 12,
        scratch_shapes=[pltpu.SemaphoreType.DMA((2,))],
        compiler_params=pltpu.CompilerParams(vmem_limit_bytes=65_000 * 1024),
        name="finish",
    )(*passed, *states)
    return results[:4] + tuple(value.T for value in results[4:12]) + results[12:]


def solution(mesh):
    fused = mesh.shape["fsdp"] == NZ * NX * NC and mesh.shape["seq"] == NY
    rows = P("fsdp", "seq", None)
    table = P("fsdp", None)
    owned = P(None, ("fsdp", "seq"))
    return jax.shard_map(
        fused_shards if fused else plain_shards,
        mesh=mesh,
        in_specs=(rows, table, table, rows) + (owned,) * 9,
        out_specs=(rows, rows, P("fsdp", None, "seq"), P()) + (owned,) * 12,
        check_vma=False,
    )
```

```python
import functools
import math
import types

import jax
import jax.numpy as jnp
from jax import lax
from jax.experimental import pallas as pl
from jax.experimental.pallas import tpu as pltpu
from jax.sharding import PartitionSpec as P

D = 768
HEADS = 12
HEAD_DIM = 64
FF = 3072
SEGMENTS = 8
STEP = 5


norm_epsilon = 1e-12
adam_epsilon = 1e-08
beta_first = 0.5
beta_second = 0.5
weight_decay = 0.01
rate_attention = 0.04
rate_feedforward = 0.03
rate_vectors = 0.2
masked_score = -1e30


def plain_dot(left_side, right_side):
    return jnp.dot(left_side, right_side, preferred_element_type=jnp.float32)


def contract_rows(left_side, right_side):
    return lax.dot_general(
        left_side, right_side, (((0,), (0,)), ((), ())), preferred_element_type=jnp.float32
    )


def contract_columns(left_side, right_side):
    return lax.dot_general(
        left_side, right_side, (((1,), (1,)), ((), ())), preferred_element_type=jnp.float32
    )


def normalize(stream):
    average = jnp.mean(stream, axis=-1, keepdims=True)
    centered = stream - average
    variance = jnp.mean(centered * centered, axis=-1, keepdims=True)
    inverse = lax.rsqrt(variance + norm_epsilon)
    return (centered * inverse, inverse)


def norm_back(grad_normed, normed, inverse):
    return inverse * (
        grad_normed
        - jnp.mean(grad_normed, axis=-1, keepdims=True)
        - normed * jnp.mean(grad_normed * normed, axis=-1, keepdims=True)
    )


def gelu_slope(value):
    return 0.5 * (1.0 + lax.erf(value * math.sqrt(0.5))) + value * jnp.exp(
        -0.5 * value * value
    ) / math.sqrt(2.0 * math.pi)


def masked_scores(queries, key_part, query_ids, key_ids):
    scores = jnp.einsum("rqhd,rkhd->rhqk", queries, key_part, preferred_element_type=jnp.float32)
    same_segment = query_ids[:, None, :, None] == key_ids[:, None, None, :]
    return jnp.where(same_segment, scores, masked_score)


def attend_block(pieces):
    queries, key_part, value_part, query_ids, key_ids = pieces
    scores = masked_scores(queries, key_part, query_ids, key_ids)
    largest = jnp.max(scores, axis=-1, keepdims=True)
    exponent = jnp.exp(scores - largest)
    denominator = jnp.sum(exponent, axis=-1, keepdims=True)
    soft_weights = (exponent / denominator).astype(jnp.bfloat16)
    context = jnp.einsum(
        "rhqk,rkhd->rqhd", soft_weights, value_part, preferred_element_type=jnp.float32
    )
    return (context, (largest + jnp.log(denominator))[..., 0])


def attend_back(pieces):
    queries, key_part, value_part, query_ids, key_ids, log_total, grad_context = pieces
    scores = masked_scores(queries, key_part, query_ids, key_ids)
    soft_again = jnp.exp(scores - log_total[..., None])
    grad_soft = jnp.einsum(
        "rqhd,rkhd->rhqk", grad_context, value_part, preferred_element_type=jnp.float32
    )
    inner_sum = jnp.sum(soft_again * grad_soft, axis=-1, keepdims=True)
    grad_scores = (soft_again * (grad_soft - inner_sum)).astype(jnp.bfloat16)
    grad_queries = jnp.einsum(
        "rhqk,rkhd->rqhd", grad_scores, key_part, preferred_element_type=jnp.float32
    )
    grad_keys = jnp.einsum(
        "rhqk,rqhd->rkhd", grad_scores, queries, preferred_element_type=jnp.float32
    )
    grad_values = jnp.einsum(
        "rhqk,rqhd->rkhd",
        soft_again.astype(jnp.bfloat16),
        grad_context,
        preferred_element_type=jnp.float32,
    )
    return (grad_queries, grad_keys, grad_values)


def adamw_update(weight, gradient, first_moment, second_moment, step_rate, decay_rate):
    first_new = beta_first * first_moment + (1.0 - beta_first) * gradient
    second_new = beta_second * second_moment + (1.0 - beta_second) * gradient * gradient
    correction_first = 1.0 - beta_first**STEP
    correction_second = 1.0 - beta_second**STEP
    update = (
        first_new / correction_first / (jnp.sqrt(second_new / correction_second) + adam_epsilon)
    )
    weight_new = weight - step_rate * (update + decay_rate * weight)
    return (weight_new, first_new, second_new, weight_new.astype(jnp.bfloat16))


def plain_shards(
    inputs,
    segment_ids,
    token_flags,
    output_grad,
    attention_weights,
    feedforward_weights,
    layer_vectors,
    attention_first,
    attention_second,
    feedforward_first,
    feedforward_second,
    vector_first,
    vector_second,
):
    row_count, local_span, model_width = inputs.shape
    full_length = segment_ids.shape[1]
    score_scale = HEAD_DIM ** (-0.5)
    inputs_here, grad_here = (inputs, output_grad)
    offset = lax.axis_index("seq") * local_span
    query_ids = lax.dynamic_slice_in_dim(segment_ids, offset, local_span, 1)
    work_flags = lax.dynamic_slice_in_dim(token_flags, offset, local_span, 1).astype(jnp.float32)
    work_span = inputs_here.shape[1]
    attention_full, feedforward_full, vector_low = (
        lax.all_gather(attention_weights.astype(jnp.bfloat16), ("fsdp", "seq"), axis=1, tiled=True),
        lax.all_gather(
            feedforward_weights.astype(jnp.bfloat16), ("fsdp", "seq"), axis=1, tiled=True
        ),
        lax.all_gather(layer_vectors.astype(jnp.bfloat16), ("fsdp", "seq"), axis=1, tiled=True),
    )
    vector_wide = vector_low.astype(jnp.float32)
    tokens = inputs_here.reshape(-1, D)
    tokens_wide = tokens.astype(jnp.float32)
    projected = plain_dot(tokens, attention_full[:, : 3 * D])
    queries = ((projected[:, :D] + vector_wide[0, :D]) * score_scale).astype(jnp.bfloat16)
    key_part = projected[:, D : 2 * D].astype(jnp.bfloat16)
    value_part = (projected[:, 2 * D :] + vector_wide[0, D : 2 * D]).astype(jnp.bfloat16)
    key_rows, value_rows = (
        lax.all_gather(key_part.reshape(row_count, work_span, D), "seq", axis=1, tiled=True),
        lax.all_gather(value_part.reshape(row_count, work_span, D), "seq", axis=1, tiled=True),
    )
    group_rows = math.gcd(row_count, max(1, 512 // work_span))
    block_count = row_count // group_rows
    query_blocks = queries.reshape(block_count, group_rows, work_span, HEADS, HEAD_DIM)
    key_blocks = key_rows.reshape(block_count, group_rows, full_length, HEADS, HEAD_DIM)
    value_blocks = value_rows.reshape(block_count, group_rows, full_length, HEADS, HEAD_DIM)
    query_id_blocks = query_ids.reshape(block_count, group_rows, work_span)
    key_id_blocks = segment_ids.reshape(block_count, group_rows, full_length)
    context, log_total = lax.map(
        attend_block, (query_blocks, key_blocks, value_blocks, query_id_blocks, key_id_blocks)
    )
    context_low = context.reshape(-1, D).astype(jnp.bfloat16)
    attention_out = (
        plain_dot(context_low, attention_full[:, 3 * D :]) + vector_wide[0, 2 * D : 3 * D]
    )
    first_normed, first_inverse = normalize(tokens_wide + attention_out)
    first_norm = (first_normed * vector_wide[2, :D] + vector_wide[2, D : 2 * D]).astype(
        jnp.bfloat16
    )
    up_value = plain_dot(first_norm, feedforward_full[:, :FF]) + vector_wide[1]
    activated = jax.nn.gelu(up_value, approximate=False).astype(jnp.bfloat16)
    feed_out = contract_columns(activated, feedforward_full[:, FF:]) + vector_wide[0, 3 * D :]
    second_normed, second_inverse = normalize(first_norm.astype(jnp.float32) + feed_out)
    layer_output = (second_normed * vector_wide[2, 2 * D : 3 * D] + vector_wide[2, 3 * D :]).astype(
        jnp.bfloat16
    )
    output_rows = layer_output.reshape(row_count, work_span, D)
    flat_flags = work_flags.reshape(-1)
    squares = jnp.stack(
        [
            jnp.sum(flat_flags * jnp.mean(tokens_wide * tokens_wide, axis=-1)),
            jnp.sum(flat_flags * jnp.mean(attention_out * attention_out, axis=-1)),
            jnp.sum(flat_flags * jnp.mean(feed_out * feed_out, axis=-1)),
        ]
    )
    square_total, flag_total = lax.psum((squares, jnp.sum(flat_flags)), ("fsdp", "seq"))
    stream_rms = jnp.sqrt(square_total / flag_total)
    segment_range = jnp.arange(SEGMENTS, dtype=jnp.int32)
    members = (query_ids[:, None, :] == segment_range[None, :, None]).astype(
        jnp.float32
    ) * work_flags[:, None, :]
    partial_pool = jnp.einsum(
        "rsl,rld->rsd",
        members.astype(jnp.bfloat16),
        output_rows,
        preferred_element_type=jnp.float32,
    )
    pool_share = lax.psum_scatter(
        partial_pool.astype(jnp.bfloat16), "seq", scatter_dimension=2, tiled=True
    ).astype(jnp.float32)
    full_members = (segment_ids[:, None, :] == segment_range[None, :, None]).astype(jnp.float32)
    full_members = full_members * token_flags[:, None, :].astype(jnp.float32)
    counts = jnp.sum(full_members, axis=2)
    pooled = pool_share / jnp.maximum(counts, 1.0)[:, :, None]
    attention_back, feedforward_back, vector_again = (
        lax.all_gather(attention_weights.astype(jnp.bfloat16), ("fsdp", "seq"), axis=1, tiled=True),
        lax.all_gather(
            feedforward_weights.astype(jnp.bfloat16), ("fsdp", "seq"), axis=1, tiled=True
        ),
        lax.all_gather(layer_vectors.astype(jnp.bfloat16), ("fsdp", "seq"), axis=1, tiled=True),
    )
    vector_back = vector_again.astype(jnp.float32)
    grad_out = grad_here.reshape(-1, D).astype(jnp.float32)
    grad_gain_second = jnp.sum(grad_out * second_normed, axis=0)
    grad_shift_second = jnp.sum(grad_out, axis=0)
    grad_second = norm_back(grad_out * vector_back[2, 2 * D : 3 * D], second_normed, second_inverse)
    grad_feed = grad_second.astype(jnp.bfloat16)
    grad_bias_down = jnp.sum(grad_feed.astype(jnp.float32), axis=0)
    grad_down = contract_rows(grad_feed, activated)
    grad_activated = plain_dot(grad_feed, feedforward_back[:, FF:])
    grad_up = (grad_activated * gelu_slope(up_value)).astype(jnp.bfloat16)
    grad_bias_up = jnp.sum(grad_up.astype(jnp.float32), axis=0)
    grad_up_weight = contract_rows(first_norm, grad_up)
    grad_first = grad_second + contract_columns(grad_up, feedforward_back[:, :FF])
    grad_feedforward = jnp.concatenate([grad_up_weight, grad_down], axis=1)
    grad_gain_first = jnp.sum(grad_first * first_normed, axis=0)
    grad_shift_first = jnp.sum(grad_first, axis=0)
    grad_stream = norm_back(grad_first * vector_back[2, :D], first_normed, first_inverse)
    grad_attention_out = grad_stream.astype(jnp.bfloat16)
    grad_bias_out = jnp.sum(grad_attention_out.astype(jnp.float32), axis=0)
    grad_out_weight = contract_rows(context_low, grad_attention_out)
    grad_context = contract_columns(grad_attention_out, attention_back[:, 3 * D :]).astype(
        jnp.bfloat16
    )
    grad_query, grad_key_rows, grad_value_rows = lax.map(
        attend_back,
        (
            query_blocks,
            key_blocks,
            value_blocks,
            query_id_blocks,
            key_id_blocks,
            log_total,
            grad_context.reshape(block_count, group_rows, work_span, HEADS, HEAD_DIM),
        ),
    )
    key_share, value_share = (
        lax.psum_scatter(
            grad_key_rows.reshape(row_count, full_length, D).astype(jnp.bfloat16),
            "seq",
            scatter_dimension=1,
            tiled=True,
        ).astype(jnp.float32),
        lax.psum_scatter(
            grad_value_rows.reshape(row_count, full_length, D).astype(jnp.bfloat16),
            "seq",
            scatter_dimension=1,
            tiled=True,
        ).astype(jnp.float32),
    )
    grad_query_low = grad_query.reshape(-1, D).astype(jnp.bfloat16) * score_scale
    grad_key_low = key_share.reshape(-1, D).astype(jnp.bfloat16)
    grad_value_low = value_share.reshape(-1, D).astype(jnp.bfloat16)
    grad_projected = jnp.concatenate([grad_query_low, grad_key_low, grad_value_low], axis=1)
    grad_bias_query = jnp.sum(grad_query_low.astype(jnp.float32), axis=0)
    grad_bias_value = jnp.sum(grad_value_low.astype(jnp.float32), axis=0)
    grad_in_weight = contract_rows(tokens, grad_projected)
    input_rows = (
        grad_stream + contract_columns(grad_projected, attention_back[:, : 3 * D])
    ).astype(jnp.bfloat16)
    input_rows = input_rows.reshape(row_count, work_span, D)
    grad_attention = jnp.concatenate([grad_in_weight, grad_out_weight], axis=1)
    grad_vectors = jnp.stack(
        [
            jnp.concatenate([grad_bias_query, grad_bias_value, grad_bias_out, grad_bias_down]),
            grad_bias_up,
            jnp.concatenate(
                [grad_gain_first, grad_shift_first, grad_gain_second, grad_shift_second]
            ),
        ]
    )
    attention_share, feedforward_share, vector_share = (
        lax.psum_scatter(grad_attention, ("fsdp", "seq"), scatter_dimension=1, tiled=True),
        lax.psum_scatter(grad_feedforward, ("fsdp", "seq"), scatter_dimension=1, tiled=True),
        lax.psum_scatter(grad_vectors, ("fsdp", "seq"), scatter_dimension=1, tiled=True),
    )
    attention_new, attention_first_new, attention_second_new, attention_low = adamw_update(
        attention_weights,
        attention_share,
        attention_first,
        attention_second,
        rate_attention,
        weight_decay,
    )
    feedforward_new, feedforward_first_new, feedforward_second_new, feedforward_low = adamw_update(
        feedforward_weights,
        feedforward_share,
        feedforward_first,
        feedforward_second,
        rate_feedforward,
        weight_decay,
    )
    vectors_new, vector_first_new, vector_second_new, vectors_low = adamw_update(
        layer_vectors, vector_share, vector_first, vector_second, rate_vectors, 0.0
    )
    return (
        output_rows,
        input_rows,
        pooled,
        stream_rms,
        attention_new,
        attention_first_new,
        attention_second_new,
        attention_low,
        feedforward_new,
        feedforward_first_new,
        feedforward_second_new,
        feedforward_low,
        vectors_new,
        vector_first_new,
        vector_second_new,
        vectors_low,
    )


MESH = pl.DeviceIdType.MESH
F32 = jnp.float32
BF16 = jnp.bfloat16

NZ, NX, NC, NY = 4, 2, 2, 2
ROW = 512
OWN_ROWS = 2
TOKENS = OWN_ROWS * ROW
SHARD_A = 96
SHARD_F = 192
EXTRA = 16
FULL_A = SHARD_A + EXTRA
PIECES = 3
PIECE = SHARD_F // PIECES
BLOCK = FF // PIECES
SPLIT_F = 48
SIZES_F = (SPLIT_F, PIECE - SPLIT_F)
GATHER_A = ((48, 16), (32, 16))
SCATTER_A = ((48, 16), (32, 16))
SCATTER_O = (64, 48)


def tn_dot(left_side, right_side):
    return contract_rows(left_side, right_side)


def nt_dot(left_side, right_side):
    return contract_columns(left_side, right_side)


def column_sum(value):
    return jnp.sum(value, axis=0, keepdims=True)


def row_mean(value):
    return jnp.mean(value, axis=-1, keepdims=True)


def remote(src, dst, send, recv, where):
    return pltpu.make_async_remote_copy(
        src_ref=src,
        dst_ref=dst,
        send_sem=send,
        recv_sem=recv,
        device_id=where,
        device_id_type=MESH,
    )


PLAN = (
    (0, 15, 30, 45), (), (16, 282), (1,), (),
    (
        17, 18, 23, 46, 2, 3, 8, 31, 60, 75, 19, 20, 47, 48, 9, 4, 5, 32,
        33, 90, 105, 10, 21, 22, 283, 49, 50, 38, 6, 7, 28, 29, 34, 35, 24, 51,
        52, 11, 12, 76, 25, 53, 13, 14, 36, 37, 39, 40, 61, 77, 78, 106, 26, 27,
        41, 42, 43, 44, 54, 55, 62, 63, 91, 120, 135, 79, 80, 58, 59, 56, 57, 68,
        83, 107, 108,
    ),
    (84, 85), (), (64, 65, 69, 70, 113), (81, 82, 86, 87, 92, 93, 109, 110, 98, 114, 115, 136),
    (284,), (88, 89, 66, 67, 116, 117), (143, 285), (), (71, 72, 111, 112, 94, 95, 121),
    (73, 74, 137, 138), (99, 100), (), (96, 97), (101, 102), (122, 123), (128, 139, 140), (),
    (103, 104), (), (124, 125), (), (118, 119, 129, 141, 142, 144, 145, 130),
    (126, 127, 146, 147, 148, 149), (), (131, 132), (133, 134), (), (), (), (), (), (), (), (),
    (), (150, 161), (), (151, 152, 162, 163), (), (153, 154, 164, 165, 172, 183), (),
    (173, 174, 184, 185), (155, 156), (166, 167, 186, 187, 194, 205), (), (), (175, 176), (), (),
    (), (), (195,), (196, 206, 207), (157, 158, 168, 169), (), (188, 189, 208, 209), (216, 227),
    (177, 178, 217, 218, 228, 229), (159, 170, 190, 191, 197, 198), (210, 211), (160, 231),
    (179, 180, 192), (), (199, 200, 212, 213, 220, 286), (171, 193), (), (181, 233),
    (201, 202, 214), (), (182, 215), (), (222,), (235,), (), (203,), (236,), (), (238, 249),
    (224, 237, 204, 239, 240, 250, 251, 287),
    (
        260, 271, 225, 252, 255, 261, 241, 244, 262, 272, 273, 254, 257, 256, 243, 246, 258, 263,
        266, 245, 277, 226, 274, 268, 259, 279, 265, 247, 276, 248, 267, 278, 269, 280, 270, 281,
    ),

)


class Place:
    def __init__(self):
        f = lax.axis_index("fsdp")
        self.z = f // (NX * NC)
        self.x = (f // NC) % NX
        self.c = f % NC
        self.y = lax.axis_index("seq")

    def at(self, z=None, x=None, c=None, y=None):
        z = self.z if z is None else z
        x = self.x if x is None else x
        c = self.c if c is None else c
        y = self.y if y is None else y
        return ((z * NX + x) * NC + c, y)

    def core(self):
        return self.at(c=1 - self.c)

    def first(self, order):
        return self.at(y=1 - self.y) if order == 0 else self.at(x=1 - self.x)

    def last(self, order):
        return self.at(x=1 - self.x) if order == 0 else self.at(y=1 - self.y)


class Gather:
    def __init__(self, me, buf, start, size, order, index, sems):
        self.me, self.buf, self.order, self.index = me, buf, order, index
        self.rows = pl.ds(start, size)
        self.sems = sems

    def own(self):
        me = self.me
        return self.buf.at[me.z, me.x, me.c, me.y, self.rows]

    def near(self):
        me = self.me
        if self.order == 0:
            return self.buf.at[me.z, me.x, me.c, 1 - me.y, self.rows]
        return self.buf.at[me.z, 1 - me.x, me.c, me.y, self.rows]

    def bundle(self, zz, far):
        me = self.me
        if self.order == 0:
            x = 1 - me.x if far else me.x
            return self.buf.at[zz, x, me.c, :, self.rows]
        y = 1 - me.y if far else me.y
        return self.buf.at[zz, :, me.c, y, self.rows]

    def quad(self, zz, other):
        c = 1 - self.me.c if other else self.me.c
        return self.buf.at[zz, :, c, :, self.rows]

    def first_copy(self, arriving=False):
        s, i = self.sems, self.index
        ref = self.near() if arriving else self.own()
        return remote(ref, ref, s.a_s.at[i], s.a_r.at[i], self.me.first(self.order))

    def line_copy(self, zz, up):
        s, i = self.sems, self.index
        ref = self.bundle(zz, False)
        step = 1 if up else -1
        return remote(
            ref,
            ref,
            (s.up_s if up else s.dn_s).at[i, zz],
            s.z_r.at[i, zz],
            self.me.at(z=self.me.z + step),
        )

    def last_copy(self, zz, arriving=False):
        s, i = self.sems, self.index
        ref = self.bundle(zz, arriving)
        return remote(ref, ref, s.b_s.at[i, zz], s.b_r.at[i, zz], self.me.last(self.order))

    def core_copy(self, zz, arriving=False):
        s, i = self.sems, self.index
        ref = self.quad(zz, arriving)
        return remote(ref, ref, s.c_s.at[i, zz], s.c_r.at[i, zz], self.me.core())

    def one_way(self, step, up, act):
        zz = self.me.z - step if up else self.me.z + step
        pl.when((zz >= 0) if up else (zz < NZ))(lambda: act(zz))

    def send_line(self, zz, up):
        z = self.me.z
        if up:

            @pl.when(z < NZ - 1)
            def _():
                self.line_copy(zz, True).start()

        else:

            @pl.when(z > 0)
            def _():
                self.line_copy(zz, False).start()

    def start(self):
        self.first_copy().start()

    def spread(self):
        self.first_copy(True).wait_recv()
        z = self.me.z
        self.send_line(z, True)
        self.send_line(z, False)
        self.last_copy(z).start()

    def line(self, step, up):
        def act(zz):
            self.line_copy(zz, up).wait_recv()
            self.send_line(zz, up)
            self.last_copy(zz).start()

        self.one_way(step, up, act)

    def cross(self, step, up):
        def act(zz):
            self.last_copy(zz, True).wait_recv()
            self.core_copy(zz).start()

        self.one_way(step, up, act)

    def finish(self):
        for zz in range(NZ):
            self.core_copy(zz, True).wait_recv()

    def events(self):
        ways = ((1, True), (1, False), (2, True), (2, False), (3, True), (3, False))
        return (
            [self.start, self.spread]
            + [functools.partial(self.line, *way) for way in ways]
            + [functools.partial(self.cross, *way) for way in ((0, True),) + ways]
        )

    def drain(self):
        z = self.me.z
        self.first_copy().wait_send()
        for zz in range(NZ):
            self.last_copy(zz).wait_send()
            self.core_copy(zz).wait_send()

            @pl.when((zz <= z) & (z < NZ - 1))
            def _():
                self.line_copy(zz, True).wait_send()

            @pl.when((zz >= z) & (z > 0))
            def _():
                self.line_copy(zz, False).wait_send()


class Scatter:
    def __init__(self, me, buf, targets, start, size, order, index, sems, landing, out, slot, credits):
        self.me, self.buf, self.order, self.index = me, buf, order, index
        self.rows = pl.ds(start, size)
        self.lo, self.hi = targets
        self.sems = sems
        self.rc, self.rb, self.rz, self.ra = landing
        self.out = out
        self.slot = pl.ds(slot, size)
        self.after, self.before = credits

    def part(self, zz, far, other=False):
        me = self.me
        c = 1 - me.c if other else me.c
        if self.order == 0:
            return self.buf.at[zz, 1 - me.x if far else me.x, c, :, self.rows]
        return self.buf.at[zz, :, c, 1 - me.y if far else me.y, self.rows]

    def planes(self, far, other):
        me = self.me
        c = 1 - me.c if other else me.c
        if self.order == 0:
            return self.buf.at[self.planes_z(), 1 - me.x if far else me.x, c, :, self.rows]
        return self.buf.at[self.planes_z(), :, c, 1 - me.y if far else me.y, self.rows]

    def planes_z(self):
        return pl.ds(self.lo, self.hi - self.lo)

    def got_core(self, far, zz=None):
        half = 1 if far else 0
        if zz is None:
            return self.rc.at[half, 0 : self.hi - self.lo, :, self.slot]
        return self.rc.at[half, zz - self.lo, :, self.slot]

    def core_copy(self, far):
        s, i = self.sems, self.index
        half = 1 if far else 0
        return remote(
            self.planes(far, True),
            self.got_core(far),
            s.rc_s.at[i, half],
            s.rc_r.at[i, half],
            self.me.core(),
        )

    def last_copy(self, zz):
        s, i = self.sems, self.index
        return remote(
            self.part(zz, True),
            self.rb.at[zz - self.lo],
            s.rb_s.at[i, zz],
            s.rb_r.at[i, zz],
            self.me.last(self.order),
        )

    def line_slot(self, zz, at, down):
        if self.hi - self.lo == 1:
            return zz - self.lo
        return zz if down else jnp.where(zz == at, NZ, zz)

    def line_copy(self, zz, down):
        s, i = self.sems, self.index
        to = self.me.z - 1 if down else self.me.z + 1
        slot = self.line_slot(zz, to, down)
        return remote(
            self.part(zz, False),
            self.rz.at[slot],
            s.rz_s.at[i, zz],
            s.rz_r.at[i, slot],
            self.me.at(z=to),
        )

    def line_wait(self, slot):
        s, i = self.sems, self.index
        remote(
            self.rz.at[slot],
            self.rz.at[slot],
            s.rz_s.at[i, 0],
            s.rz_r.at[i, slot],
            self.me.core(),
        ).wait_recv()

    def home(self, mine):
        me = self.me
        if self.order == 0:
            y = me.y if mine else 1 - me.y
            return self.buf.at[me.z, me.x, me.c, y, self.rows], y
        x = me.x if mine else 1 - me.x
        return self.buf.at[me.z, x, me.c, me.y, self.rows], x

    def first_copy(self):
        s, i = self.sems, self.index
        return remote(
            self.home(False)[0],
            self.ra,
            s.ra_s.at[i],
            s.ra_r.at[i],
            self.me.first(self.order),
        )

    def by_distance(self, dist, act):
        act_down, act_up = (lambda zz: act(zz, True)), (lambda zz: act(zz, False))
        self.one_way(dist, True, act_down)
        if dist > 0:
            self.one_way(dist, False, act_up)

    def aims(self, zz):
        return (zz >= self.lo) & (zz < self.hi)

    def one_way(self, dist, down, act):
        zz = self.me.z - dist if down else self.me.z + dist
        pl.when(self.aims(zz))(lambda: act(zz))

    def start(self):
        if self.after is not None:
            pl.semaphore_wait(self.after, 1)
        self.core_copy(True).start()
        self.core_copy(False).start()

    def cross(self):
        self.core_copy(True).wait_recv()
        for dist in range(NZ - 1, -1, -1):

            def act(zz, down):
                ref = self.part(zz, True)
                got = self.got_core(True, zz)
                ref[...] = (ref[...].astype(F32) + got[...].astype(F32)).astype(BF16)
                self.last_copy(zz).start()

            self.by_distance(dist, act)

    def keep(self):
        self.core_copy(False).wait_recv()
        for zz in range(self.lo, self.hi):
            ref = self.part(zz, False)
            got = self.got_core(False, zz)
            ref[...] = (ref[...].astype(F32) + got[...].astype(F32)).astype(BF16)
        if self.before is not None:
            pl.semaphore_signal(
                self.before, inc=1, device_id=self.me.core(), device_id_type=MESH
            )

    def line(self, dist, down):
        z = self.me.z

        def act(zz):
            self.last_copy(zz).wait_recv()
            ref = self.part(zz, False)
            outer = z < NZ - 1 if down else z > 0
            total = ref[...].astype(F32) + self.rb[zz - self.lo].astype(F32)
            slot = self.line_slot(zz, z, True)

            @pl.when(outer)
            def _():
                self.line_wait(slot)
                ref[...] = (total + self.rz[slot].astype(F32)).astype(BF16)

            @pl.when(jnp.logical_not(outer))
            def _():
                ref[...] = total.astype(BF16)

            self.line_copy(zz, down).start()

        self.one_way(dist, down, act)

    def events(self):
        ways = ((3, True), (3, False), (2, True), (2, False), (1, True), (1, False))
        return (
            [self.start, self.cross, self.keep]
            + [functools.partial(self.line, *way) for way in ways]
            + [self.settle, self.finish]
        )

    def settle(self):
        pl.when(self.aims(self.me.z))(self.settle_here)

    def settle_here(self):
        z = self.me.z
        self.last_copy(z).wait_recv()
        far_ref, far = self.home(False)
        near_ref, near = self.home(True)
        here = z - self.lo
        above, below = self.line_slot(z, z, True), self.line_slot(z, z, False)
        self.out[self.rows, :] = near_ref[...].astype(F32) + self.rb[here, near].astype(F32)
        total = far_ref[...].astype(F32) + self.rb[here, far].astype(F32)

        @pl.when(z == 0)
        def _():
            self.line_wait(above)
            far_ref[...] = (total + self.rz[above, far].astype(F32)).astype(BF16)
            self.out[self.rows, :] += self.rz[above, near].astype(F32)

        @pl.when(z == NZ - 1)
        def _():
            self.line_wait(below)
            far_ref[...] = (total + self.rz[below, far].astype(F32)).astype(BF16)
            self.out[self.rows, :] += self.rz[below, near].astype(F32)

        @pl.when((z > 0) & (z < NZ - 1))
        def _():
            self.line_wait(above)
            self.line_wait(below)
            far_ref[...] = (
                total + (self.rz[above, far].astype(F32) + self.rz[below, far].astype(F32))
            ).astype(BF16)
            self.out[self.rows, :] += self.rz[above, near].astype(F32) + self.rz[
                below, near
            ].astype(F32)

        self.first_copy().start()

    def finish(self):
        @pl.when(self.aims(self.me.z))
        def _():
            self.first_copy().wait_recv()
            self.out[self.rows, :] += self.ra[...].astype(F32)

    def drain(self):
        z = self.me.z
        self.core_copy(True).wait_send()
        self.core_copy(False).wait_send()
        pl.when(self.aims(z))(lambda: self.first_copy().wait_send())
        for zz in range(self.lo, self.hi):
            self.last_copy(zz).wait_send()

            @pl.when(zz < z)
            def _():
                self.line_copy(zz, True).wait_send()

            @pl.when(zz > z)
            def _():
                self.line_copy(zz, False).wait_send()


class Schedule:
    def __init__(self, events):
        self.events, self.place = events, 0

    def take(self):
        chosen = PLAN[self.place]
        self.place += 1

        def run():
            for number in chosen:
                self.events[number]()

        return run if chosen else None

    def step(self, count=1):
        for _ in range(count):
            run = self.take()
            if run is not None:
                run()

    def loop(self, count, body):
        runs = [self.take() for _ in range(count)]

        @pl.loop(0, count)
        def _(i):
            body(i)
            for place, run in enumerate(runs):
                if run is not None:
                    pl.when(i == place)(run)


def repeat(count, body):
    pl.loop(0, count)(body)


def flatten(value):
    return value.reshape(-1, value.shape[-1])


def masked_halves(pair, other):
    first = lax.broadcasted_iota(jnp.int32, pair.shape, 1) < HEAD_DIM
    return jnp.where(first, pair, other), jnp.where(first, other, pair)


def attention_pair(queries, keys, values, ask, bar):
    values_turned = values.T
    queries_halves, keys_halves = masked_halves(queries, ask), masked_halves(keys, bar)
    scores = [nt_dot(keys_halves[half], queries_halves[half]) for half in range(2)]
    contexts, totals = [], []
    for half in range(2):
        largest = jnp.max(scores[half], axis=0, keepdims=True)
        exponent = jnp.exp(scores[half] - largest)
        total = column_sum(exponent)
        context = plain_dot(
            values_turned[half * HEAD_DIM : (half + 1) * HEAD_DIM, :], exponent.astype(BF16)
        )
        contexts.append(context * (1.0 / total))
        totals.append(largest + jnp.log(total))
    return jnp.concatenate(contexts, 0).T, jnp.concatenate(totals, 0)


def attention_pair_back(queries, keys, values, grad_context, ask, bar, log_total):
    keys_turned = keys.T
    zero = jnp.zeros_like(keys)
    queries_asked, keys_barred = masked_halves(queries, ask), masked_halves(keys, bar)
    queries_alone, values_alone = masked_halves(queries, zero), masked_halves(values, zero)
    grad_alone = masked_halves(grad_context, zero)
    width = ROW // 2
    parts = [(slice(0, width), 0), (slice(0, width), 1), (slice(width, ROW), 0), (slice(width, ROW), 1)]

    def scores_of(part):
        span, half = part
        return (
            nt_dot(keys_barred[half], queries_asked[half][span]),
            nt_dot(values_alone[half], grad_context[span]),
        )

    ahead = [scores_of(part) for part in parts[:2]]
    grad_queries = []
    grad_keys = grad_values = 0.0
    for place, (span, half) in enumerate(parts):
        if place + 2 < len(parts):
            ahead.append(scores_of(parts[place + 2]))
        scores, grad_soft = ahead[place]
        soft = jnp.exp(scores - log_total[half : half + 1, span])
        inner = column_sum(soft * grad_soft)
        grad_scores = (soft * (grad_soft - inner)).astype(BF16)
        grad_values += plain_dot(soft.astype(BF16), grad_alone[half][span])
        grad_keys += plain_dot(grad_scores, queries_alone[half][span])
        grad_queries.append(
            plain_dot(keys_turned[half * HEAD_DIM : (half + 1) * HEAD_DIM, :], grad_scores)
        )
    grad_queries = [jnp.concatenate(grad_queries[i : i + 2], 0).T for i in (0, 2)]
    return jnp.concatenate(grad_queries, 0), grad_keys, grad_values


def select_columns(permuted):
    row = lax.broadcasted_iota(jnp.int32, (8 * 128, D), 0)
    col = lax.broadcasted_iota(jnp.int32, (8 * 128, D), 1)
    lane = row % 128
    source = (row // 128) * SHARD_A + lane
    if permuted:
        piece = col // 256
        rest = col % 256
        col = (rest // PIECE) * SHARD_F + piece * PIECE + rest % PIECE
    return jnp.where((source == col) & (lane < SHARD_A), 1.0, 0.0).astype(BF16)


SEM_SHAPES = dict(
    a_s=(10,),
    a_r=(10,),
    z_r=(10, NZ),
    up_s=(10, NZ),
    dn_s=(10, NZ),
    b_s=(10, NZ),
    b_r=(10, NZ),
    c_s=(10, NZ),
    c_r=(10, NZ),
    rc_s=(12, 2),
    rc_r=(12, 2),
    rb_s=(12, NZ),
    rb_r=(12, NZ),
    rz_s=(12, NZ),
    rz_r=(12, NZ + 1),
    ra_s=(12,),
    ra_r=(12,),
    x_s=(4, 2),
    x_r=(4, 2),
    own=(4, 2),
    pool_s=(1,),
    pool_r=(1,),
    stat_s=(5,),
    stat_r=(5,),
    load=(2,),
)


def gather_pieces():
    return [(0, *GATHER_A[0]), (sum(GATHER_A[0]), *GATHER_A[1])] + [
        (k * PIECE, SPLIT_F, PIECE - SPLIT_F) for k in range(PIECES)
    ]


def scatter_pieces():
    return (
        gather_pieces()[2:]
        + [(0, *SCATTER_O)]
        + [(0, *SCATTER_A[0]), (sum(SCATTER_A[0]), *SCATTER_A[1])]
    )


def scratch():
    return dict(
        wa=pltpu.VMEM((NZ, NX, NC, NY, FULL_A, D), BF16),
        wf=pltpu.VMEM((NZ, NX, NC, NY, SHARD_F, D), BF16),
        rc=pltpu.VMEM((2, NZ, 2, PIECE, D), BF16),
        xs=pltpu.VMEM((TOKENS, D), BF16),
        dys=pltpu.VMEM((TOKENS, D), BF16),
        ctx=pltpu.VMEM((TOKENS, D), BF16),
        n1=pltpu.VMEM((TOKENS, D), BF16),
        fn=pltpu.VMEM((TOKENS, D), BF16),
        fg=pltpu.VMEM((TOKENS, D), BF16),
        qkv=pltpu.VMEM((TOKENS, 3 * D), BF16),
        act=pltpu.VMEM((PIECES, TOKENS, BLOCK), BF16),
        slope=pltpu.VMEM((PIECES, TOKENS, BLOCK), BF16),
        acc=pltpu.VMEM((TOKENS, D), F32),
        ask=pltpu.VMEM((OWN_ROWS, ROW, 128), BF16),
        bar=pltpu.VMEM((OWN_ROWS, ROW, 128), BF16),
        rco=pltpu.VMEM((2, 1, 2, FULL_A, D), BF16),
        totals=pltpu.VMEM((OWN_ROWS * HEADS // 2, 2, ROW), F32),
        side=pltpu.VMEM((TOKENS, 128), F32),
        vec=pltpu.VMEM((16, 4 * D), F32),
        bu=pltpu.VMEM((PIECES, 16, BLOCK), F32),
        gvec=pltpu.VMEM((8, 4 * D), F32),
        gbu=pltpu.VMEM((PIECES, 8, BLOCK), F32),
        stat=pltpu.VMEM((8, 128), F32),
        stat_in=pltpu.VMEM((5, 8, 128), F32),
        pool_out=pltpu.VMEM((OWN_ROWS, 8, D), F32),
        vector_pad=pltpu.VMEM((EXTRA, 128), F32),
        pool_in=pltpu.VMEM((OWN_ROWS, 8, D // 2), F32),
        credit=pltpu.SemaphoreType.REGULAR((2,)),
        free=pltpu.SemaphoreType.REGULAR,
    )


def landing_shapes():
    shapes = []
    shared = [tuple(map(max, SIZES_F, sizes)) for sizes in SCATTER_A]
    places = [(sizes, NZ) for sizes in (*shared, SIZES_F)] + [(SCATTER_O, 1)]
    for sizes, targets in places:
        for size in sizes:
            shapes += [
                pltpu.VMEM((targets, 2, size, D), BF16),
                pltpu.VMEM((targets + 1 if targets > 1 else 1, 2, size, D), BF16),
                pltpu.VMEM((size, D), BF16),
            ]
    return shapes


def fused_kernel(
    x_in,
    dy_in,
    wa_in,
    wf_in,
    vector_in,
    ids,
    flags,
    out_y,
    out_dx,
    out_pooled,
    out_stats,
    grad_a,
    grad_f,
    *more,
):
    names, sem_names = tuple(scratch()), tuple(SEM_SHAPES)
    landings = len(landing_shapes())
    r = types.SimpleNamespace(**dict(zip(names, more)))
    landing_refs = more[len(names) : len(names) + landings]
    sems = types.SimpleNamespace(**dict(zip(sem_names, more[len(names) + landings :])))
    me = Place()
    z, x, c, y = me.z, me.x, me.c, me.y
    wa, wf, xs, dys, ctx = r.wa, r.wf, r.xs, r.dys, r.ctx
    n1, fn, fg, qkv, acc = r.n1, r.fn, r.fg, r.qkv, r.acc
    act, slope, vec, gvec, stat = r.act, r.slope, r.vec, r.gvec, r.stat

    def tile(i, size):
        return pl.ds(pl.multiple_of(i * size, size), size)

    def row_ids(slot):
        return ids[pl.ds(2 * y + slot, 1), :]

    def row_flags(slot):
        return flags[pl.ds(2 * y + slot, 1), :].astype(F32)

    def vector(row, quarter):
        return vec[row : row + 1, quarter * D : (quarter + 1) * D]

    barrier = pltpu.get_barrier_semaphore()
    for where in (
        me.core(),
        me.at(x=1 - x),
        me.at(y=1 - y),
        me.at(z=(z + 2) % NZ),
    ):
        pl.semaphore_signal(barrier, inc=1, device_id=where, device_id_type=MESH)

    @pl.when(z > 0)
    def _():
        pl.semaphore_signal(barrier, inc=1, device_id=me.at(z=z - 1), device_id_type=MESH)

    @pl.when(z < NZ - 1)
    def _():
        pl.semaphore_signal(barrier, inc=1, device_id=me.at(z=z + 1), device_id_type=MESH)

    own_a, own_f = acc.at[0:SHARD_A], acc.at[SHARD_A : SHARD_A + SHARD_F]
    load_a = pltpu.make_async_copy(wa_in, own_a, sems.load.at[0])
    load_f = pltpu.make_async_copy(wf_in, own_f, sems.load.at[1])
    load_a.start()
    load_f.start()
    r.vector_pad[...] = jnp.zeros_like(r.vector_pad)
    r.vector_pad[0:3, 0:SHARD_A] = vector_in[...]
    wa[z, x, c, y, SHARD_A:FULL_A, :] = jnp.zeros((EXTRA, D), BF16)
    wa[z, x, c, y, SHARD_A:FULL_A, 0:128] = r.vector_pad[...].astype(BF16)

    def row_copy(kind, src, dst, slot):
        return remote(
            src, dst, sems.x_s.at[kind, slot], sems.x_r.at[kind, slot], me.at(y=1 - y)
        )

    def own_copy(kind, src, dst, slot):
        return pltpu.make_async_copy(src, dst, sems.own.at[kind, slot])

    def span(slot, half):
        return pl.ds(pl.multiple_of(slot * ROW + half * (ROW // 2), ROW // 2), ROW // 2)

    def take_rows(kind, source, target):
        sends = [
            row_copy(kind, source.at[2 * (1 - y) + slot], target.at[span(slot, y)], slot)
            for slot in range(OWN_ROWS)
        ]
        owns = [
            own_copy(kind, source.at[2 * y + slot], target.at[span(slot, y)], slot)
            for slot in range(OWN_ROWS)
        ]
        arrivals = [
            row_copy(kind, source.at[2 * y + slot], target.at[span(slot, 1 - y)], slot)
            for slot in range(OWN_ROWS)
        ]
        return sends, owns, arrivals

    def give_rows(kind, source, target):
        sends = [
            row_copy(kind, source.at[span(slot, 1 - y)], target.at[2 * y + slot], slot)
            for slot in range(OWN_ROWS)
        ]
        owns = [
            own_copy(kind, source.at[span(slot, y)], target.at[2 * y + slot], slot)
            for slot in range(OWN_ROWS)
        ]
        arrivals = [
            row_copy(kind, source.at[span(slot, y)], target.at[2 * (1 - y) + slot], slot)
            for slot in range(OWN_ROWS)
        ]
        return sends, owns, arrivals

    x_sends, x_owns, x_arrivals = take_rows(0, x_in, xs)
    dy_sends, dy_owns, dy_arrivals = take_rows(1, dy_in, dys)
    out_sends, out_owns, out_arrivals = give_rows(2, dys, out_y)
    dx_sends, dx_owns, dx_arrivals = give_rows(3, n1, out_dx)

    def start_all(copies):
        def run():
            for copy in copies:
                copy.start()

        return run

    gathers, scatters = [], []
    for piece, (first_row, *sizes) in enumerate(gather_pieces()):
        for order in range(2):
            buf = wa if piece < 2 else wf
            start = first_row + order * sizes[0]
            gathers.append(Gather(me, buf, start, sizes[order], order, 2 * piece + order, sems))
    places = (0, 1, 2, 3, 0, 1)
    for piece, (first_row, *sizes) in enumerate(scatter_pieces()):
        lone = piece == PIECES
        targets = (0, NZ) if piece < PIECES else (NZ - 1, NZ) if lone else (0, NZ - 1)
        for order in range(2):
            size, i = sizes[order], 2 * places[piece] + order
            landing = (
                r.rco if lone else r.rc,
                landing_refs[3 * i].at[:, :, 0:size],
                landing_refs[3 * i + 1].at[:, :, 0:size],
                landing_refs[3 * i + 2].at[0:size],
            )
            credit = r.credit.at[order]
            credits = (
                None if lone or piece == 0 else credit,
                None if lone or piece == len(places) - 1 else credit,
            )
            slot = order * sizes[0]
            scatters.append(
                Scatter(
                    me, wa if lone else wf, targets, first_row + slot, size, order,
                    2 * piece + order, sems, landing, grad_f if piece < PIECES else grad_a, slot,
                    credits,
                )
            )

    exchange = [copy.start for copy in x_sends + dy_sends + dx_sends]
    events = [event for one in gathers + scatters for event in one.events()] + exchange
    plan = Schedule(events)

    for copy in x_owns + dy_owns:
        copy.start()
    line_ends = jnp.where(z > 0, 1, 0).astype(jnp.int32) + jnp.where(z < NZ - 1, 1, 0).astype(
        jnp.int32
    )
    load_a.wait()
    wa[z, x, c, y, 0:SHARD_A, :] = own_a[...].astype(BF16)
    pl.semaphore_wait(barrier, 4 + line_ends)
    plan.step()
    load_f.wait()
    wf[z, x, c, y] = own_f[...].astype(BF16)
    plan.step()

    gvec[...] = jnp.zeros_like(gvec)
    r.gbu[...] = jnp.zeros_like(r.gbu)
    stat[...] = jnp.zeros_like(stat)
    for slot in range(OWN_ROWS):
        wide = jnp.broadcast_to(row_ids(slot).astype(F32), (128, ROW))
        tall = wide.T
        flag_rows = jnp.broadcast_to(row_flags(slot), (128, ROW))
        r.side[slot * ROW : (slot + 1) * ROW, :] = flag_rows.T
        lane = lax.broadcasted_iota(jnp.int32, (ROW, 128), 1) % HEAD_DIM
        same = tall == lane.astype(F32)
        r.ask[slot] = jnp.where(same & (lane < SEGMENTS), 1.0, 0.0).astype(BF16)
        r.bar[slot] = jnp.where(same | (lane >= SEGMENTS), 0.0, masked_score).astype(BF16)
        plan.step()
    ctx[...] = select_columns(False)
    fg[...] = select_columns(True)
    plan.step()
    plan.step()
    for one in gathers[:4]:
        one.finish()

    for q in range(4):
        blocks = jnp.concatenate(
            [
                wa[q, j // 4, (j // 2) % 2, j % 2, SHARD_A:FULL_A, 0:128]
                for j in range(8)
            ],
            axis=1,
        )
        vec[:, q * D : (q + 1) * D] = plain_dot(blocks, ctx[...])
        moved = plain_dot(blocks, fg[...])
        for k in range(PIECES):
            r.bu[k, :, q * 256 : (q + 1) * 256] = moved[:, k * 256 : (k + 1) * 256]

    plan.step(2)
    for copy in x_owns:
        copy.wait()
    for copy in x_arrivals:
        copy.wait_recv()

    scale = HEAD_DIM ** (-0.5)

    def project(i):
        rows = tile(i, 512)
        tokens = xs[rows, :]
        wide = tokens.astype(F32)
        stat[0:1, :] += lane_sums(wide * wide * r.side[rows, 1:2])
        for j in range(3):
            weights = flatten(wa[j, :, :, :, 0:SHARD_A, :])
            value = nt_dot(tokens, weights)
            if j == 0:
                value = (value + vector(0, 0)) * scale
            if j == 2:
                value = value + vector(0, 1)
            qkv[rows, j * D : (j + 1) * D] = value.astype(BF16)

    def lane_sums(value):
        total = column_sum(value)
        return sum(total[:, j * 128 : (j + 1) * 128] for j in range(D // 128))

    plan.loop(2, project)

    def columns(pair, block):
        return pl.ds(pl.multiple_of(block * D + pair * 128, 128), 128)

    def attend(i):
        slot, pair = i // (HEADS // 2), i % (HEADS // 2)
        rows = tile(slot, ROW)
        context, total = attention_pair(
            qkv[rows, columns(pair, 0)],
            qkv[rows, columns(pair, 1)],
            qkv[rows, columns(pair, 2)],
            r.ask[slot],
            r.bar[slot],
        )
        ctx[rows, columns(pair, 0)] = context.astype(BF16)
        r.totals[i] = total

    plan.loop(OWN_ROWS * HEADS // 2, attend)

    def attention_output(i):
        rows = tile(i, 256)
        weights = flatten(wa[3, :, :, :, 0:SHARD_A, :])
        out = nt_dot(ctx[rows, :], weights) + vector(0, 2)
        stat[1:2, :] += lane_sums(out * out * r.side[rows, 1:2])
        normed, inverse = normalize(xs[rows, :].astype(F32) + out)
        n1[rows, :] = normed.astype(BF16)
        r.side[rows, 0:1] = inverse
        fn[rows, :] = (normed * vector(2, 0) + vector(2, 1)).astype(BF16)

    plan.loop(4, attention_output)

    def up_rows(k):
        return flatten(flatten_lead(wf[0:2, :, :, :, k * PIECE : (k + 1) * PIECE, :]))

    def down_rows(k):
        return flatten(flatten_lead(wf[2:4, :, :, :, k * PIECE : (k + 1) * PIECE, :]))

    def flatten_lead(value):
        return value.reshape(-1, PIECE, D)

    for k in range(PIECES):
        plan.step()
        for one in gathers[4 + 2 * k : 6 + 2 * k]:
            one.finish()

        def feed(i, k=k):
            rows = tile(i, 512)
            up = nt_dot(fn[rows, :], up_rows(k)) + r.bu[k, 1:2, :]
            half = 0.5 * (1.0 + lax.erf(up * math.sqrt(0.5)))
            activated = (up * half).astype(BF16)
            act[k, rows, :] = activated
            slope[k, rows, :] = (
                half + up * (jnp.exp(-0.5 * up * up) * (1.0 / math.sqrt(2.0 * math.pi)))
            ).astype(BF16)
            value = plain_dot(activated, down_rows(k))
            if k == 0:
                acc[rows, :] = value
            else:
                acc[rows, :] += value

        plan.loop(2, feed)
    plan.step()

    for copy in dy_owns:
        copy.wait()
    for copy in dy_arrivals:
        copy.wait_recv()
    for one in gathers:
        one.drain()

    def second(i):
        rows = tile(i, 128)
        feed_out = acc[rows, :] + vector(0, 3)
        stat[2:3, :] += lane_sums(feed_out * feed_out * r.side[rows, 1:2])
        normed, inverse = normalize(fn[rows, :].astype(F32) + feed_out)
        grad = dys[rows, :].astype(F32)
        dys[rows, :] = (normed * vector(2, 2) + vector(2, 3)).astype(BF16)
        gvec[2:3, 2 * D : 3 * D] += column_sum(grad * normed)
        gvec[2:3, 3 * D :] += column_sum(grad)
        back = norm_back(grad * vector(2, 2), normed, inverse)
        acc[rows, :] = back
        low = back.astype(BF16)
        fg[rows, :] = low
        gvec[0:1, 3 * D :] += column_sum(low.astype(F32))

    repeat(TOKENS // 128, second)
    plan.step()

    start_all(out_sends + out_owns)()

    segments = lax.broadcasted_iota(jnp.int32, (SEGMENTS, ROW), 0)
    for slot in range(OWN_ROWS):
        member = jnp.where(segments == row_ids(slot), 1.0, 0.0) * row_flags(slot)
        sums = plain_dot(member.astype(BF16), dys[slot * ROW : (slot + 1) * ROW, :])
        counts = jnp.sum(member, axis=1, keepdims=True)
        r.pool_out[slot] = sums / jnp.maximum(counts, 1.0)
        total = row_flags(slot)
        stat[3:4, :] += sum(total[:, j * 128 : (j + 1) * 128] for j in range(ROW // 128))

    def half_lanes(which):
        return pl.ds(pl.multiple_of(which * (D // 2), 128), D // 2)

    pool_copy = remote(
        r.pool_out.at[:, :, half_lanes(1 - y)],
        r.pool_in,
        sems.pool_s.at[0],
        sems.pool_r.at[0],
        me.at(y=1 - y),
    )
    pool_copy.start()

    stat_partners = [
        me.core(),
        me.at(x=1 - x),
        me.at(y=1 - y),
        me.at(z=z + 1 - 2 * (z % 2)),
        me.at(z=(z + 2) % NZ),
    ]

    def stat_copy(step):
        return remote(
            stat,
            r.stat_in.at[step],
            sems.stat_s.at[step],
            sems.stat_r.at[step],
            stat_partners[step],
        )

    def stat_start(step):
        return lambda: stat_copy(step).start()

    def stat_end(step):
        def run():
            stat_copy(step).wait()
            stat[...] += r.stat_in[step]

        return run

    stat_start(0)()
    plan.step()
    for k in range(PIECES):

        def feed_back(i, k=k):
            rows = tile(i, 512)
            grad = nt_dot(fg[rows, :], down_rows(k)) * slope[k, rows, :].astype(F32)
            low = grad.astype(BF16)
            slope[k, rows, :] = low
            r.gbu[k, 0:1, :] += column_sum(low.astype(F32))
            acc[rows, :] += plain_dot(low, up_rows(k))

        plan.loop(2, feed_back)

        def weights_back(i, k=k):
            cols = tile(i, BLOCK // 2)
            down = tn_dot(act[k, :, cols], fg[...]).astype(BF16)
            up = tn_dot(slope[k, :, cols], fn[...]).astype(BF16)
            where = (slice(None), slice(None), slice(None), pl.ds(k * PIECE, PIECE))
            wf[(2 + i, *where)] = down.reshape(NX, NC, NY, PIECE, D)
            wf[(i, *where)] = up.reshape(NX, NC, NY, PIECE, D)

        plan.loop(2, weights_back)
        stat_end(k)()
        stat_start(k + 1)()

    def first(i):
        rows = tile(i, 128)
        grad = acc[rows, :]
        normed = n1[rows, :].astype(F32)
        gvec[2:3, 0:D] += column_sum(grad * normed)
        gvec[2:3, D : 2 * D] += column_sum(grad)
        stream = norm_back(grad * vector(2, 0), normed, r.side[rows, 0:1])
        acc[rows, :] = stream
        low = stream.astype(BF16)
        fg[rows, :] = low
        gvec[0:1, 2 * D : 3 * D] += column_sum(low.astype(F32))

    plan.loop(TOKENS // 128, first)

    def context_back(i):
        rows = tile(i, 512)
        fn[rows, :] = plain_dot(fg[rows, :], flatten(wa[3, :, :, :, 0:SHARD_A, :])).astype(BF16)

    plan.loop(2, context_back)
    stat_end(3)()
    stat_start(4)()

    def outer_back(i):
        cols = pl.ds(pl.multiple_of(i * (D // 2), 128), D // 2)
        value = tn_dot(fg[:, cols], ctx[...]).astype(BF16)
        wa[3, i, :, :, 0:SHARD_A, :] = value.reshape(NC, NY, SHARD_A, D)

    plan.loop(2, outer_back)

    ctx[...] = select_columns(False)
    fg[...] = select_columns(True)

    def vectors_back(q, buf):
        row = lax.broadcasted_iota(jnp.int32, (8, 1), 0)
        plain = nt_dot(gvec[:, q * D : (q + 1) * D].astype(BF16), ctx[...])
        piled = jnp.concatenate(
            [r.gbu[k, :, q * 256 : (q + 1) * 256] for k in range(PIECES)], axis=1
        )
        moved = nt_dot(piled.astype(BF16), fg[...])
        low = jnp.where(row == 1, jnp.broadcast_to(moved[0:1, :], plain.shape), plain)
        low = jnp.concatenate([low, jnp.zeros_like(low)], axis=0).astype(BF16)
        for j in range(8):
            buf[q, j // 4, (j // 2) % 2, j % 2, SHARD_A:FULL_A, 0:128] = low[
                :, j * 128 : (j + 1) * 128
            ]

    vectors_back(3, wa)
    plan.step()

    def attend_back_pair(slot, pair):
        rows = tile(slot, ROW)
        grads = attention_pair_back(
            qkv[rows, columns(pair, 0)],
            qkv[rows, columns(pair, 1)],
            qkv[rows, columns(pair, 2)],
            fn[rows, columns(pair, 0)],
            r.ask[slot],
            r.bar[slot],
            r.totals[slot * (HEADS // 2) + pair],
        )
        for j in range(3):
            low = grads[j].astype(BF16)
            if j == 0:
                low = low * jnp.asarray(scale, BF16)
            qkv[rows, columns(pair, j)] = low
            if j != 1:
                gvec[0:1, columns(pair, j // 2)] += column_sum(low.astype(F32))

    def input_back(slot):
        rows = pl.ds(slot * ROW, ROW)
        value = acc[rows, :]
        for j in range(3):
            value += plain_dot(
                qkv[rows, j * D : (j + 1) * D], flatten(wa[j, :, :, :, 0:SHARD_A, :])
            )
        n1[rows, :] = value.astype(BF16)
        dx_owns[slot].start()

    plan.loop(HEADS // 2, functools.partial(attend_back_pair, 0))
    input_back(0)
    plan.step()
    plan.loop(HEADS // 2, functools.partial(attend_back_pair, 1))
    stat_end(4)()
    plan.step()
    for one in scatters[:4]:
        one.drain()

    free = r.free
    for where in (me.at(x=1 - x), me.at(y=1 - y)):
        pl.semaphore_signal(free, inc=1, device_id=where, device_id_type=MESH)

    @pl.when(z > 0)
    def _():
        pl.semaphore_signal(free, inc=1, device_id=me.at(z=z - 1), device_id_type=MESH)

    @pl.when(z < NZ - 1)
    def _():
        pl.semaphore_signal(free, inc=1, device_id=me.at(z=z + 1), device_id_type=MESH)

    for j in range(3):

        def inner_back(i, j=j):
            cols = pl.ds(pl.multiple_of(j * D + i * (D // 2), 128), D // 2)
            value = tn_dot(qkv[:, cols], xs[...]).astype(BF16)
            wf[j, i, :, :, 0:SHARD_A, :] = value.reshape(NC, NY, SHARD_A, D)

        plan.loop(2, inner_back)
    for q in range(3):
        vectors_back(q, wf)
    pl.semaphore_wait(free, 2 + line_ends)
    plan.step()
    input_back(1)
    plan.step(2)

    assert plan.place == len(PLAN)
    for one in scatters[4:]:
        one.drain()
    pool_copy.wait()
    for slot in range(OWN_ROWS):
        out_pooled[2 * y + slot] = r.pool_out[slot, :, half_lanes(y)]
        out_pooled[2 * (1 - y) + slot] = r.pool_in[slot]
    out_stats[...] = stat[...]
    for copies in (x_sends, dy_sends, out_sends, dx_sends):
        for copy in copies:
            copy.wait_send()
    for copies in (out_owns, dx_owns):
        for copy in copies:
            copy.wait()
    for copies in (out_arrivals, dx_arrivals):
        for copy in copies:
            copy.wait_recv()


def finish_kernel(y_in, dx_in, pooled_in, stats, grad_a, grad_f, grad_v, *more):
    states, results = more[:9], more[9:]
    out_y, out_dx, out_pooled, out_rms = results[:4]
    out_y[...] = y_in[...]
    out_dx[...] = dx_in[...]
    out_pooled[...] = pooled_in[...]
    totals = jnp.sum(stats[...], axis=1, keepdims=True)
    rms = jnp.sqrt(totals[0:3] / D / totals[3:4])
    for i in range(3):
        out_rms[i] = rms[i, 0]
    rates = (
        (rate_attention, weight_decay),
        (rate_feedforward, weight_decay),
        (rate_vectors, 0.0),
    )
    gradients = (grad_a[...], grad_f[...], grad_v[0:3, 0:SHARD_A])
    for i in range(3):
        weight, first, second = states[3 * i : 3 * i + 3]
        new = adamw_update(weight[...], gradients[i], first[...], second[...], *rates[i])
        for ref, value in zip(results[4 + 4 * i : 8 + 4 * i], new):
            ref[...] = value


def fused_shards(
    inputs,
    segment_ids,
    token_flags,
    output_grad,
    attention_weights,
    feedforward_weights,
    layer_vectors,
    attention_first,
    attention_second,
    feedforward_first,
    feedforward_second,
    vector_first,
    vector_second,
):
    any_space = pl.BlockSpec(memory_space=pl.ANY)
    vmem = pl.BlockSpec(memory_space=pltpu.VMEM)
    smem = pl.BlockSpec(memory_space=pltpu.SMEM)
    rows = jax.ShapeDtypeStruct(inputs.shape, BF16)
    pooled = jax.ShapeDtypeStruct((inputs.shape[0], SEGMENTS, D // NY), F32)
    semaphores = [pltpu.SemaphoreType.DMA(shape) for shape in SEM_SHAPES.values()]
    passed = pl.pallas_call(
        fused_kernel,
        out_shape=(
            rows,
            rows,
            pooled,
            jax.ShapeDtypeStruct((8, 128), F32),
            jax.ShapeDtypeStruct((FULL_A, D), F32),
            jax.ShapeDtypeStruct((SHARD_F, D), F32),
        ),
        in_specs=[any_space] * 4 + [vmem] * 3,
        out_specs=(any_space, any_space, vmem, vmem, vmem, vmem),
        scratch_shapes=list(scratch().values()) + landing_shapes() + semaphores,
        compiler_params=pltpu.CompilerParams(
            collective_id=0, has_side_effects=True, vmem_limit_bytes=65_000 * 1024
        ),
        name="layer",
    )(
        inputs,
        output_grad,
        attention_weights.T,
        feedforward_weights.T,
        layer_vectors,
        segment_ids,
        token_flags,
    )
    states = (
        attention_weights.T,
        attention_first.T,
        attention_second.T,
        feedforward_weights.T,
        feedforward_first.T,
        feedforward_second.T,
        layer_vectors,
        vector_first,
        vector_second,
    )

    def updated(shape):
        wide = jax.ShapeDtypeStruct(shape, F32)
        return (wide, wide, wide, jax.ShapeDtypeStruct(shape, BF16))

    steps = 2

    def part(shape):
        return pl.BlockSpec((shape[0] // steps, *shape[1:]), lambda i: (i,) + (0,) * (len(shape) - 1))

    def whole(shape):
        return pl.BlockSpec(shape, lambda i: (0,) * len(shape))

    table_a, table_f, table_v = (SHARD_A, D), (SHARD_F, D), layer_vectors.shape
    results = pl.pallas_call(
        finish_kernel,
        grid=(steps,),
        out_shape=(rows, rows, pooled, jax.ShapeDtypeStruct((3,), F32))
        + updated(table_a)
        + updated(table_f)
        + updated(table_v),
        in_specs=[part(rows.shape), part(rows.shape), part(pooled.shape), whole((8, 128))]
        + [part(table_a), part(table_f), pl.BlockSpec((EXTRA, D), lambda i: (SHARD_A // EXTRA, 0))]
        + [part(table_a)] * 3
        + [part(table_f)] * 3
        + [whole(table_v)] * 3,
        out_specs=[part(rows.shape), part(rows.shape), part(pooled.shape), smem]
        + [part(table_a)] * 4
        + [part(table_f)] * 4
        + [whole(table_v)] * 4,
        compiler_params=pltpu.CompilerParams(vmem_limit_bytes=65_000 * 1024),
        name="finish",
    )(*passed, passed[4], *states)
    results = tuple(results)
    return results[:4] + tuple(value.T for value in results[4:12]) + results[12:]


def solution(mesh):
    fused = mesh.shape["fsdp"] == NZ * NX * NC and mesh.shape["seq"] == NY
    rows = P("fsdp", "seq", None)
    table = P("fsdp", None)
    owned = P(None, ("fsdp", "seq"))
    return jax.shard_map(
        fused_shards if fused else plain_shards,
        mesh=mesh,
        in_specs=(rows, table, table, rows) + (owned,) * 9,
        out_specs=(rows, rows, P("fsdp", None, "seq"), P()) + (owned,) * 12,
        check_vma=False,
    )
```

```python
import functools
import math
import types

import jax
import jax.numpy as jnp
from jax import lax
from jax.experimental import pallas as pl
from jax.experimental.pallas import tpu as pltpu
from jax.sharding import PartitionSpec as P

D = 768
HEADS = 12
HEAD_DIM = 64
FF = 3072
SEGMENTS = 8
STEP = 5


norm_epsilon = 1e-12
adam_epsilon = 1e-08
beta_first = 0.5
beta_second = 0.5
weight_decay = 0.01
rate_attention = 0.04
rate_feedforward = 0.03
rate_vectors = 0.2
masked_score = -1e30


def plain_dot(left_side, right_side):
    return jnp.dot(left_side, right_side, preferred_element_type=jnp.float32)


def contract_rows(left_side, right_side):
    return lax.dot_general(
        left_side, right_side, (((0,), (0,)), ((), ())), preferred_element_type=jnp.float32
    )


def contract_columns(left_side, right_side):
    return lax.dot_general(
        left_side, right_side, (((1,), (1,)), ((), ())), preferred_element_type=jnp.float32
    )


def normalize(stream):
    average = jnp.mean(stream, axis=-1, keepdims=True)
    centered = stream - average
    variance = jnp.mean(centered * centered, axis=-1, keepdims=True)
    inverse = lax.rsqrt(variance + norm_epsilon)
    return (centered * inverse, inverse)


def norm_back(grad_normed, normed, inverse):
    return inverse * (
        grad_normed
        - jnp.mean(grad_normed, axis=-1, keepdims=True)
        - normed * jnp.mean(grad_normed * normed, axis=-1, keepdims=True)
    )


def gelu_slope(value):
    return 0.5 * (1.0 + lax.erf(value * math.sqrt(0.5))) + value * jnp.exp(
        -0.5 * value * value
    ) / math.sqrt(2.0 * math.pi)


def masked_scores(queries, key_part, query_ids, key_ids):
    scores = jnp.einsum("rqhd,rkhd->rhqk", queries, key_part, preferred_element_type=jnp.float32)
    same_segment = query_ids[:, None, :, None] == key_ids[:, None, None, :]
    return jnp.where(same_segment, scores, masked_score)


def attend_block(pieces):
    queries, key_part, value_part, query_ids, key_ids = pieces
    scores = masked_scores(queries, key_part, query_ids, key_ids)
    largest = jnp.max(scores, axis=-1, keepdims=True)
    exponent = jnp.exp(scores - largest)
    denominator = jnp.sum(exponent, axis=-1, keepdims=True)
    soft_weights = (exponent / denominator).astype(jnp.bfloat16)
    context = jnp.einsum(
        "rhqk,rkhd->rqhd", soft_weights, value_part, preferred_element_type=jnp.float32
    )
    return (context, (largest + jnp.log(denominator))[..., 0])


def attend_back(pieces):
    queries, key_part, value_part, query_ids, key_ids, log_total, grad_context = pieces
    scores = masked_scores(queries, key_part, query_ids, key_ids)
    soft_again = jnp.exp(scores - log_total[..., None])
    grad_soft = jnp.einsum(
        "rqhd,rkhd->rhqk", grad_context, value_part, preferred_element_type=jnp.float32
    )
    inner_sum = jnp.sum(soft_again * grad_soft, axis=-1, keepdims=True)
    grad_scores = (soft_again * (grad_soft - inner_sum)).astype(jnp.bfloat16)
    grad_queries = jnp.einsum(
        "rhqk,rkhd->rqhd", grad_scores, key_part, preferred_element_type=jnp.float32
    )
    grad_keys = jnp.einsum(
        "rhqk,rqhd->rkhd", grad_scores, queries, preferred_element_type=jnp.float32
    )
    grad_values = jnp.einsum(
        "rhqk,rqhd->rkhd",
        soft_again.astype(jnp.bfloat16),
        grad_context,
        preferred_element_type=jnp.float32,
    )
    return (grad_queries, grad_keys, grad_values)


def adamw_update(weight, gradient, first_moment, second_moment, step_rate, decay_rate):
    first_new = beta_first * first_moment + (1.0 - beta_first) * gradient
    second_new = beta_second * second_moment + (1.0 - beta_second) * gradient * gradient
    correction_first = 1.0 - beta_first**STEP
    correction_second = 1.0 - beta_second**STEP
    update = (
        first_new / correction_first / (jnp.sqrt(second_new / correction_second) + adam_epsilon)
    )
    weight_new = weight - step_rate * (update + decay_rate * weight)
    return (weight_new, first_new, second_new, weight_new.astype(jnp.bfloat16))


def plain_shards(
    inputs,
    segment_ids,
    token_flags,
    output_grad,
    attention_weights,
    feedforward_weights,
    layer_vectors,
    attention_first,
    attention_second,
    feedforward_first,
    feedforward_second,
    vector_first,
    vector_second,
):
    row_count, local_span, model_width = inputs.shape
    full_length = segment_ids.shape[1]
    score_scale = HEAD_DIM ** (-0.5)
    inputs_here, grad_here = (inputs, output_grad)
    offset = lax.axis_index("seq") * local_span
    query_ids = lax.dynamic_slice_in_dim(segment_ids, offset, local_span, 1)
    work_flags = lax.dynamic_slice_in_dim(token_flags, offset, local_span, 1).astype(jnp.float32)
    work_span = inputs_here.shape[1]
    attention_full, feedforward_full, vector_low = (
        lax.all_gather(attention_weights.astype(jnp.bfloat16), ("fsdp", "seq"), axis=1, tiled=True),
        lax.all_gather(
            feedforward_weights.astype(jnp.bfloat16), ("fsdp", "seq"), axis=1, tiled=True
        ),
        lax.all_gather(layer_vectors.astype(jnp.bfloat16), ("fsdp", "seq"), axis=1, tiled=True),
    )
    vector_wide = vector_low.astype(jnp.float32)
    tokens = inputs_here.reshape(-1, D)
    tokens_wide = tokens.astype(jnp.float32)
    projected = plain_dot(tokens, attention_full[:, : 3 * D])
    queries = ((projected[:, :D] + vector_wide[0, :D]) * score_scale).astype(jnp.bfloat16)
    key_part = projected[:, D : 2 * D].astype(jnp.bfloat16)
    value_part = (projected[:, 2 * D :] + vector_wide[0, D : 2 * D]).astype(jnp.bfloat16)
    key_rows, value_rows = (
        lax.all_gather(key_part.reshape(row_count, work_span, D), "seq", axis=1, tiled=True),
        lax.all_gather(value_part.reshape(row_count, work_span, D), "seq", axis=1, tiled=True),
    )
    group_rows = math.gcd(row_count, max(1, 512 // work_span))
    block_count = row_count // group_rows
    query_blocks = queries.reshape(block_count, group_rows, work_span, HEADS, HEAD_DIM)
    key_blocks = key_rows.reshape(block_count, group_rows, full_length, HEADS, HEAD_DIM)
    value_blocks = value_rows.reshape(block_count, group_rows, full_length, HEADS, HEAD_DIM)
    query_id_blocks = query_ids.reshape(block_count, group_rows, work_span)
    key_id_blocks = segment_ids.reshape(block_count, group_rows, full_length)
    context, log_total = lax.map(
        attend_block, (query_blocks, key_blocks, value_blocks, query_id_blocks, key_id_blocks)
    )
    context_low = context.reshape(-1, D).astype(jnp.bfloat16)
    attention_out = (
        plain_dot(context_low, attention_full[:, 3 * D :]) + vector_wide[0, 2 * D : 3 * D]
    )
    first_normed, first_inverse = normalize(tokens_wide + attention_out)
    first_norm = (first_normed * vector_wide[2, :D] + vector_wide[2, D : 2 * D]).astype(
        jnp.bfloat16
    )
    up_value = plain_dot(first_norm, feedforward_full[:, :FF]) + vector_wide[1]
    activated = jax.nn.gelu(up_value, approximate=False).astype(jnp.bfloat16)
    feed_out = contract_columns(activated, feedforward_full[:, FF:]) + vector_wide[0, 3 * D :]
    second_normed, second_inverse = normalize(first_norm.astype(jnp.float32) + feed_out)
    layer_output = (second_normed * vector_wide[2, 2 * D : 3 * D] + vector_wide[2, 3 * D :]).astype(
        jnp.bfloat16
    )
    output_rows = layer_output.reshape(row_count, work_span, D)
    flat_flags = work_flags.reshape(-1)
    squares = jnp.stack(
        [
            jnp.sum(flat_flags * jnp.mean(tokens_wide * tokens_wide, axis=-1)),
            jnp.sum(flat_flags * jnp.mean(attention_out * attention_out, axis=-1)),
            jnp.sum(flat_flags * jnp.mean(feed_out * feed_out, axis=-1)),
        ]
    )
    square_total, flag_total = lax.psum((squares, jnp.sum(flat_flags)), ("fsdp", "seq"))
    stream_rms = jnp.sqrt(square_total / flag_total)
    segment_range = jnp.arange(SEGMENTS, dtype=jnp.int32)
    members = (query_ids[:, None, :] == segment_range[None, :, None]).astype(
        jnp.float32
    ) * work_flags[:, None, :]
    partial_pool = jnp.einsum(
        "rsl,rld->rsd",
        members.astype(jnp.bfloat16),
        output_rows,
        preferred_element_type=jnp.float32,
    )
    pool_share = lax.psum_scatter(
        partial_pool.astype(jnp.bfloat16), "seq", scatter_dimension=2, tiled=True
    ).astype(jnp.float32)
    full_members = (segment_ids[:, None, :] == segment_range[None, :, None]).astype(jnp.float32)
    full_members = full_members * token_flags[:, None, :].astype(jnp.float32)
    counts = jnp.sum(full_members, axis=2)
    pooled = pool_share / jnp.maximum(counts, 1.0)[:, :, None]
    attention_back, feedforward_back, vector_again = (
        lax.all_gather(attention_weights.astype(jnp.bfloat16), ("fsdp", "seq"), axis=1, tiled=True),
        lax.all_gather(
            feedforward_weights.astype(jnp.bfloat16), ("fsdp", "seq"), axis=1, tiled=True
        ),
        lax.all_gather(layer_vectors.astype(jnp.bfloat16), ("fsdp", "seq"), axis=1, tiled=True),
    )
    vector_back = vector_again.astype(jnp.float32)
    grad_out = grad_here.reshape(-1, D).astype(jnp.float32)
    grad_gain_second = jnp.sum(grad_out * second_normed, axis=0)
    grad_shift_second = jnp.sum(grad_out, axis=0)
    grad_second = norm_back(grad_out * vector_back[2, 2 * D : 3 * D], second_normed, second_inverse)
    grad_feed = grad_second.astype(jnp.bfloat16)
    grad_bias_down = jnp.sum(grad_feed.astype(jnp.float32), axis=0)
    grad_down = contract_rows(grad_feed, activated)
    grad_activated = plain_dot(grad_feed, feedforward_back[:, FF:])
    grad_up = (grad_activated * gelu_slope(up_value)).astype(jnp.bfloat16)
    grad_bias_up = jnp.sum(grad_up.astype(jnp.float32), axis=0)
    grad_up_weight = contract_rows(first_norm, grad_up)
    grad_first = grad_second + contract_columns(grad_up, feedforward_back[:, :FF])
    grad_feedforward = jnp.concatenate([grad_up_weight, grad_down], axis=1)
    grad_gain_first = jnp.sum(grad_first * first_normed, axis=0)
    grad_shift_first = jnp.sum(grad_first, axis=0)
    grad_stream = norm_back(grad_first * vector_back[2, :D], first_normed, first_inverse)
    grad_attention_out = grad_stream.astype(jnp.bfloat16)
    grad_bias_out = jnp.sum(grad_attention_out.astype(jnp.float32), axis=0)
    grad_out_weight = contract_rows(context_low, grad_attention_out)
    grad_context = contract_columns(grad_attention_out, attention_back[:, 3 * D :]).astype(
        jnp.bfloat16
    )
    grad_query, grad_key_rows, grad_value_rows = lax.map(
        attend_back,
        (
            query_blocks,
            key_blocks,
            value_blocks,
            query_id_blocks,
            key_id_blocks,
            log_total,
            grad_context.reshape(block_count, group_rows, work_span, HEADS, HEAD_DIM),
        ),
    )
    key_share, value_share = (
        lax.psum_scatter(
            grad_key_rows.reshape(row_count, full_length, D).astype(jnp.bfloat16),
            "seq",
            scatter_dimension=1,
            tiled=True,
        ).astype(jnp.float32),
        lax.psum_scatter(
            grad_value_rows.reshape(row_count, full_length, D).astype(jnp.bfloat16),
            "seq",
            scatter_dimension=1,
            tiled=True,
        ).astype(jnp.float32),
    )
    grad_query_low = grad_query.reshape(-1, D).astype(jnp.bfloat16) * score_scale
    grad_key_low = key_share.reshape(-1, D).astype(jnp.bfloat16)
    grad_value_low = value_share.reshape(-1, D).astype(jnp.bfloat16)
    grad_projected = jnp.concatenate([grad_query_low, grad_key_low, grad_value_low], axis=1)
    grad_bias_query = jnp.sum(grad_query_low.astype(jnp.float32), axis=0)
    grad_bias_value = jnp.sum(grad_value_low.astype(jnp.float32), axis=0)
    grad_in_weight = contract_rows(tokens, grad_projected)
    input_rows = (
        grad_stream + contract_columns(grad_projected, attention_back[:, : 3 * D])
    ).astype(jnp.bfloat16)
    input_rows = input_rows.reshape(row_count, work_span, D)
    grad_attention = jnp.concatenate([grad_in_weight, grad_out_weight], axis=1)
    grad_vectors = jnp.stack(
        [
            jnp.concatenate([grad_bias_query, grad_bias_value, grad_bias_out, grad_bias_down]),
            grad_bias_up,
            jnp.concatenate(
                [grad_gain_first, grad_shift_first, grad_gain_second, grad_shift_second]
            ),
        ]
    )
    attention_share, feedforward_share, vector_share = (
        lax.psum_scatter(grad_attention, ("fsdp", "seq"), scatter_dimension=1, tiled=True),
        lax.psum_scatter(grad_feedforward, ("fsdp", "seq"), scatter_dimension=1, tiled=True),
        lax.psum_scatter(grad_vectors, ("fsdp", "seq"), scatter_dimension=1, tiled=True),
    )
    attention_new, attention_first_new, attention_second_new, attention_low = adamw_update(
        attention_weights,
        attention_share,
        attention_first,
        attention_second,
        rate_attention,
        weight_decay,
    )
    feedforward_new, feedforward_first_new, feedforward_second_new, feedforward_low = adamw_update(
        feedforward_weights,
        feedforward_share,
        feedforward_first,
        feedforward_second,
        rate_feedforward,
        weight_decay,
    )
    vectors_new, vector_first_new, vector_second_new, vectors_low = adamw_update(
        layer_vectors, vector_share, vector_first, vector_second, rate_vectors, 0.0
    )
    return (
        output_rows,
        input_rows,
        pooled,
        stream_rms,
        attention_new,
        attention_first_new,
        attention_second_new,
        attention_low,
        feedforward_new,
        feedforward_first_new,
        feedforward_second_new,
        feedforward_low,
        vectors_new,
        vector_first_new,
        vector_second_new,
        vectors_low,
    )


MESH = pl.DeviceIdType.MESH
F32 = jnp.float32
BF16 = jnp.bfloat16

NZ, NX, NC, NY = 4, 2, 2, 2
ROW = 512
OWN_ROWS = 2
TOKENS = OWN_ROWS * ROW
SHARD_A = 96
SHARD_F = 192
EXTRA = 16
FULL_A = SHARD_A + EXTRA
PIECES = 3
PIECE = SHARD_F // PIECES
BLOCK = FF // PIECES
SPLIT_F = 48
SIZES_F = (SPLIT_F, PIECE - SPLIT_F)
GATHER_A = ((48, 16), (32, 16))
SCATTER_A = ((48, 16), (32, 16))
SCATTER_O = (64, 48)


def tn_dot(left_side, right_side):
    return contract_rows(left_side, right_side)


def nt_dot(left_side, right_side):
    return contract_columns(left_side, right_side)


def column_sum(value):
    return jnp.sum(value, axis=0, keepdims=True)


def row_mean(value):
    return jnp.mean(value, axis=-1, keepdims=True)


def remote(src, dst, send, recv, where):
    return pltpu.make_async_remote_copy(
        src_ref=src,
        dst_ref=dst,
        send_sem=send,
        recv_sem=recv,
        device_id=where,
        device_id_type=MESH,
    )


PLAN = (
    (0, 15, 30, 45), (), (16, 282), (1,), (),
    (
        17, 18, 23, 46, 2, 3, 8, 31, 60, 75, 19, 20, 47, 48, 9, 4, 5, 32,
        33, 90, 105, 10, 21, 22, 283, 49, 50, 38, 6, 7, 28, 29, 34, 35, 24, 51,
        52, 11, 12, 76, 25, 53, 13, 14, 36, 37, 39, 40, 61, 77, 78, 106, 26, 27,
        41, 42, 43, 44, 54, 55, 62, 63, 91, 120, 135, 79, 80, 58, 59, 56, 57, 68,
        83, 107, 108,
    ),
    (84, 85), (), (64, 65, 69, 70, 113), (81, 82, 86, 87, 92, 93, 109, 110, 98, 114, 115, 136),
    (284,), (88, 89, 66, 67, 116, 117), (143, 285), (), (71, 72, 111, 112, 94, 95, 121),
    (73, 74, 137, 138), (99, 100), (), (96, 97), (101, 102), (122, 123), (128, 139, 140), (),
    (103, 104), (), (124, 125), (), (118, 119, 129, 141, 142, 144, 145, 130),
    (126, 127, 146, 147, 148, 149), (), (131, 132), (133, 134), (), (), (), (), (), (), (), (),
    (), (150, 161), (), (151, 152, 162, 163), (), (153, 154, 164, 165, 172, 183), (),
    (173, 174, 184, 185), (155, 156), (166, 167, 186, 187, 194, 205), (), (), (175, 176), (), (),
    (), (), (195,), (196, 206, 207), (157, 158, 168, 169), (), (188, 189, 208, 209), (216, 227),
    (177, 178, 217, 218, 228, 229), (159, 170, 190, 191, 197, 198), (210, 211), (160, 231),
    (179, 180, 192), (), (199, 200, 212, 213, 220, 286), (171, 193), (), (181, 233),
    (201, 202, 214), (), (182, 215), (), (222,), (235,), (), (203,), (236,), (), (238, 249),
    (224, 237, 204, 239, 240, 250, 251, 287),
    (
        260, 271, 225, 252, 255, 261, 241, 244, 262, 272, 273, 254, 257, 256, 243, 246, 258, 263,
        266, 245, 277, 226, 274, 268, 259, 279, 265, 247, 276, 248, 267, 278, 269, 280, 270, 281,
    ),

)


class Place:
    def __init__(self):
        f = lax.axis_index("fsdp")
        self.z = f // (NX * NC)
        self.x = (f // NC) % NX
        self.c = f % NC
        self.y = lax.axis_index("seq")

    def at(self, z=None, x=None, c=None, y=None):
        z = self.z if z is None else z
        x = self.x if x is None else x
        c = self.c if c is None else c
        y = self.y if y is None else y
        return ((z * NX + x) * NC + c, y)

    def core(self):
        return self.at(c=1 - self.c)

    def first(self, order):
        return self.at(y=1 - self.y) if order == 0 else self.at(x=1 - self.x)

    def last(self, order):
        return self.at(x=1 - self.x) if order == 0 else self.at(y=1 - self.y)


class Gather:
    def __init__(self, me, buf, start, size, order, index, sems):
        self.me, self.buf, self.order, self.index = me, buf, order, index
        self.rows = pl.ds(start, size)
        self.sems = sems

    def own(self):
        me = self.me
        return self.buf.at[me.z, me.x, me.c, me.y, self.rows]

    def near(self):
        me = self.me
        if self.order == 0:
            return self.buf.at[me.z, me.x, me.c, 1 - me.y, self.rows]
        return self.buf.at[me.z, 1 - me.x, me.c, me.y, self.rows]

    def bundle(self, zz, far):
        me = self.me
        if self.order == 0:
            x = 1 - me.x if far else me.x
            return self.buf.at[zz, x, me.c, :, self.rows]
        y = 1 - me.y if far else me.y
        return self.buf.at[zz, :, me.c, y, self.rows]

    def quad(self, zz, other):
        c = 1 - self.me.c if other else self.me.c
        return self.buf.at[zz, :, c, :, self.rows]

    def first_copy(self, arriving=False):
        s, i = self.sems, self.index
        ref = self.near() if arriving else self.own()
        return remote(ref, ref, s.a_s.at[i], s.a_r.at[i], self.me.first(self.order))

    def line_copy(self, zz, up):
        s, i = self.sems, self.index
        ref = self.bundle(zz, False)
        step = 1 if up else -1
        return remote(
            ref,
            ref,
            (s.up_s if up else s.dn_s).at[i, zz],
            s.z_r.at[i, zz],
            self.me.at(z=self.me.z + step),
        )

    def last_copy(self, zz, arriving=False):
        s, i = self.sems, self.index
        ref = self.bundle(zz, arriving)
        return remote(ref, ref, s.b_s.at[i, zz], s.b_r.at[i, zz], self.me.last(self.order))

    def core_copy(self, zz, arriving=False):
        s, i = self.sems, self.index
        ref = self.quad(zz, arriving)
        return remote(ref, ref, s.c_s.at[i, zz], s.c_r.at[i, zz], self.me.core())

    def one_way(self, step, up, act):
        zz = self.me.z - step if up else self.me.z + step
        pl.when((zz >= 0) if up else (zz < NZ))(lambda: act(zz))

    def send_line(self, zz, up):
        z = self.me.z
        if up:

            @pl.when(z < NZ - 1)
            def _():
                self.line_copy(zz, True).start()

        else:

            @pl.when(z > 0)
            def _():
                self.line_copy(zz, False).start()

    def start(self):
        self.first_copy().start()

    def spread(self):
        self.first_copy(True).wait_recv()
        z = self.me.z
        self.send_line(z, True)
        self.send_line(z, False)
        self.last_copy(z).start()

    def line(self, step, up):
        def act(zz):
            self.line_copy(zz, up).wait_recv()
            self.send_line(zz, up)
            self.last_copy(zz).start()

        self.one_way(step, up, act)

    def cross(self, step, up):
        def act(zz):
            self.last_copy(zz, True).wait_recv()
            self.core_copy(zz).start()

        self.one_way(step, up, act)

    def finish(self):
        for zz in range(NZ):
            self.core_copy(zz, True).wait_recv()

    def events(self):
        ways = ((1, True), (1, False), (2, True), (2, False), (3, True), (3, False))
        return (
            [self.start, self.spread]
            + [functools.partial(self.line, *way) for way in ways]
            + [functools.partial(self.cross, *way) for way in ((0, True),) + ways]
        )

    def drain(self):
        z = self.me.z
        self.first_copy().wait_send()
        for zz in range(NZ):
            self.last_copy(zz).wait_send()
            self.core_copy(zz).wait_send()

            @pl.when((zz <= z) & (z < NZ - 1))
            def _():
                self.line_copy(zz, True).wait_send()

            @pl.when((zz >= z) & (z > 0))
            def _():
                self.line_copy(zz, False).wait_send()


class Scatter:
    def __init__(self, me, buf, targets, start, size, order, index, sems, landing, out, slot, credits):
        self.me, self.buf, self.order, self.index = me, buf, order, index
        self.rows = pl.ds(start, size)
        self.lo, self.hi = targets
        self.sems = sems
        self.rc, self.rb, self.rz, self.ra = landing
        self.out = out
        self.slot = pl.ds(slot, size)
        self.after, self.before = credits

    def part(self, zz, far, other=False):
        me = self.me
        c = 1 - me.c if other else me.c
        if self.order == 0:
            return self.buf.at[zz, 1 - me.x if far else me.x, c, :, self.rows]
        return self.buf.at[zz, :, c, 1 - me.y if far else me.y, self.rows]

    def planes(self, far, other):
        me = self.me
        c = 1 - me.c if other else me.c
        if self.order == 0:
            return self.buf.at[self.planes_z(), 1 - me.x if far else me.x, c, :, self.rows]
        return self.buf.at[self.planes_z(), :, c, 1 - me.y if far else me.y, self.rows]

    def planes_z(self):
        return pl.ds(self.lo, self.hi - self.lo)

    def got_core(self, far, zz=None):
        half = 1 if far else 0
        if zz is None:
            return self.rc.at[half, 0 : self.hi - self.lo, :, self.slot]
        return self.rc.at[half, zz - self.lo, :, self.slot]

    def core_copy(self, far):
        s, i = self.sems, self.index
        half = 1 if far else 0
        return remote(
            self.planes(far, True),
            self.got_core(far),
            s.rc_s.at[i, half],
            s.rc_r.at[i, half],
            self.me.core(),
        )

    def last_copy(self, zz):
        s, i = self.sems, self.index
        return remote(
            self.part(zz, True),
            self.rb.at[zz - self.lo],
            s.rb_s.at[i, zz],
            s.rb_r.at[i, zz],
            self.me.last(self.order),
        )

    def line_slot(self, zz, at, down):
        if self.hi - self.lo == 1:
            return zz - self.lo
        return zz if down else jnp.where(zz == at, NZ, zz)

    def line_copy(self, zz, down):
        s, i = self.sems, self.index
        to = self.me.z - 1 if down else self.me.z + 1
        slot = self.line_slot(zz, to, down)
        return remote(
            self.part(zz, False),
            self.rz.at[slot],
            s.rz_s.at[i, zz],
            s.rz_r.at[i, slot],
            self.me.at(z=to),
        )

    def line_wait(self, slot):
        s, i = self.sems, self.index
        remote(
            self.rz.at[slot],
            self.rz.at[slot],
            s.rz_s.at[i, 0],
            s.rz_r.at[i, slot],
            self.me.core(),
        ).wait_recv()

    def home(self, mine):
        me = self.me
        if self.order == 0:
            y = me.y if mine else 1 - me.y
            return self.buf.at[me.z, me.x, me.c, y, self.rows], y
        x = me.x if mine else 1 - me.x
        return self.buf.at[me.z, x, me.c, me.y, self.rows], x

    def first_copy(self):
        s, i = self.sems, self.index
        return remote(
            self.home(False)[0],
            self.ra,
            s.ra_s.at[i],
            s.ra_r.at[i],
            self.me.first(self.order),
        )

    def by_distance(self, dist, act):
        act_down, act_up = (lambda zz: act(zz, True)), (lambda zz: act(zz, False))
        self.one_way(dist, True, act_down)
        if dist > 0:
            self.one_way(dist, False, act_up)

    def aims(self, zz):
        return (zz >= self.lo) & (zz < self.hi)

    def one_way(self, dist, down, act):
        zz = self.me.z - dist if down else self.me.z + dist
        pl.when(self.aims(zz))(lambda: act(zz))

    def start(self):
        if self.after is not None:
            pl.semaphore_wait(self.after, 1)
        self.core_copy(True).start()
        self.core_copy(False).start()

    def cross(self):
        self.core_copy(True).wait_recv()
        for dist in range(NZ - 1, -1, -1):

            def act(zz, down):
                ref = self.part(zz, True)
                got = self.got_core(True, zz)
                ref[...] = (ref[...].astype(F32) + got[...].astype(F32)).astype(BF16)
                self.last_copy(zz).start()

            self.by_distance(dist, act)

    def keep(self):
        self.core_copy(False).wait_recv()
        for zz in range(self.lo, self.hi):
            ref = self.part(zz, False)
            got = self.got_core(False, zz)
            ref[...] = (ref[...].astype(F32) + got[...].astype(F32)).astype(BF16)
        if self.before is not None:
            pl.semaphore_signal(
                self.before, inc=1, device_id=self.me.core(), device_id_type=MESH
            )

    def line(self, dist, down):
        z = self.me.z

        def act(zz):
            self.last_copy(zz).wait_recv()
            ref = self.part(zz, False)
            outer = z < NZ - 1 if down else z > 0
            total = ref[...].astype(F32) + self.rb[zz - self.lo].astype(F32)
            slot = self.line_slot(zz, z, True)

            @pl.when(outer)
            def _():
                self.line_wait(slot)
                ref[...] = (total + self.rz[slot].astype(F32)).astype(BF16)

            @pl.when(jnp.logical_not(outer))
            def _():
                ref[...] = total.astype(BF16)

            self.line_copy(zz, down).start()

        self.one_way(dist, down, act)

    def events(self):
        ways = ((3, True), (3, False), (2, True), (2, False), (1, True), (1, False))
        return (
            [self.start, self.cross, self.keep]
            + [functools.partial(self.line, *way) for way in ways]
            + [self.settle, self.finish]
        )

    def settle(self):
        pl.when(self.aims(self.me.z))(self.settle_here)

    def settle_here(self):
        z = self.me.z
        self.last_copy(z).wait_recv()
        far_ref, far = self.home(False)
        near_ref, near = self.home(True)
        here = z - self.lo
        above, below = self.line_slot(z, z, True), self.line_slot(z, z, False)
        self.out[self.rows, :] = near_ref[...].astype(F32) + self.rb[here, near].astype(F32)
        total = far_ref[...].astype(F32) + self.rb[here, far].astype(F32)

        @pl.when(z == 0)
        def _():
            self.line_wait(above)
            far_ref[...] = (total + self.rz[above, far].astype(F32)).astype(BF16)
            self.out[self.rows, :] += self.rz[above, near].astype(F32)

        @pl.when(z == NZ - 1)
        def _():
            self.line_wait(below)
            far_ref[...] = (total + self.rz[below, far].astype(F32)).astype(BF16)
            self.out[self.rows, :] += self.rz[below, near].astype(F32)

        @pl.when((z > 0) & (z < NZ - 1))
        def _():
            self.line_wait(above)
            self.line_wait(below)
            far_ref[...] = (
                total + (self.rz[above, far].astype(F32) + self.rz[below, far].astype(F32))
            ).astype(BF16)
            self.out[self.rows, :] += self.rz[above, near].astype(F32) + self.rz[
                below, near
            ].astype(F32)

        self.first_copy().start()

    def finish(self):
        @pl.when(self.aims(self.me.z))
        def _():
            self.first_copy().wait_recv()
            self.out[self.rows, :] += self.ra[...].astype(F32)

    def drain(self):
        z = self.me.z
        self.core_copy(True).wait_send()
        self.core_copy(False).wait_send()
        pl.when(self.aims(z))(lambda: self.first_copy().wait_send())
        for zz in range(self.lo, self.hi):
            self.last_copy(zz).wait_send()

            @pl.when(zz < z)
            def _():
                self.line_copy(zz, True).wait_send()

            @pl.when(zz > z)
            def _():
                self.line_copy(zz, False).wait_send()


class Schedule:
    def __init__(self, events):
        self.events, self.place = events, 0

    def take(self):
        chosen = PLAN[self.place]
        self.place += 1

        def run():
            for number in chosen:
                self.events[number]()

        return run if chosen else None

    def step(self, count=1):
        for _ in range(count):
            run = self.take()
            if run is not None:
                run()

    def loop(self, count, body):
        runs = [self.take() for _ in range(count)]

        @pl.loop(0, count)
        def _(i):
            body(i)
            for place, run in enumerate(runs):
                if run is not None:
                    pl.when(i == place)(run)


def repeat(count, body):
    pl.loop(0, count)(body)


def flatten(value):
    return value.reshape(-1, value.shape[-1])


def masked_halves(pair, other):
    first = lax.broadcasted_iota(jnp.int32, pair.shape, 1) < HEAD_DIM
    return jnp.where(first, pair, other), jnp.where(first, other, pair)


def attention_pair(queries, keys, values, ask, bar):
    values_turned = values.T
    queries_halves, keys_halves = masked_halves(queries, ask), masked_halves(keys, bar)
    scores = [nt_dot(keys_halves[half], queries_halves[half]) for half in range(2)]
    contexts, totals = [], []
    for half in range(2):
        largest = jnp.max(scores[half], axis=0, keepdims=True)
        exponent = jnp.exp(scores[half] - largest)
        total = column_sum(exponent)
        context = plain_dot(
            values_turned[half * HEAD_DIM : (half + 1) * HEAD_DIM, :], exponent.astype(BF16)
        )
        contexts.append(context * (1.0 / total))
        totals.append(largest + jnp.log(total))
    return jnp.concatenate(contexts, 0).T, jnp.concatenate(totals, 0)


def attention_pair_back(queries, keys, values, grad_context, ask, bar, log_total):
    keys_turned = keys.T
    zero = jnp.zeros_like(keys)
    queries_asked, keys_barred = masked_halves(queries, ask), masked_halves(keys, bar)
    queries_alone, values_alone = masked_halves(queries, zero), masked_halves(values, zero)
    grad_alone = masked_halves(grad_context, zero)
    width = ROW // 2
    parts = [(slice(0, width), 0), (slice(0, width), 1), (slice(width, ROW), 0), (slice(width, ROW), 1)]

    def scores_of(part):
        span, half = part
        return (
            nt_dot(keys_barred[half], queries_asked[half][span]),
            nt_dot(values_alone[half], grad_context[span]),
        )

    ahead = [scores_of(part) for part in parts[:2]]
    grad_queries = []
    grad_keys = grad_values = 0.0
    for place, (span, half) in enumerate(parts):
        if place + 2 < len(parts):
            ahead.append(scores_of(parts[place + 2]))
        scores, grad_soft = ahead[place]
        soft = jnp.exp(scores - log_total[half : half + 1, span])
        inner = column_sum(soft * grad_soft)
        grad_scores = (soft * (grad_soft - inner)).astype(BF16)
        grad_values += plain_dot(soft.astype(BF16), grad_alone[half][span])
        grad_keys += plain_dot(grad_scores, queries_alone[half][span])
        grad_queries.append(
            plain_dot(keys_turned[half * HEAD_DIM : (half + 1) * HEAD_DIM, :], grad_scores)
        )
    grad_queries = [jnp.concatenate(grad_queries[i : i + 2], 0).T for i in (0, 2)]
    return jnp.concatenate(grad_queries, 0), grad_keys, grad_values


def select_columns(permuted):
    row = lax.broadcasted_iota(jnp.int32, (8 * 128, D), 0)
    col = lax.broadcasted_iota(jnp.int32, (8 * 128, D), 1)
    lane = row % 128
    source = (row // 128) * SHARD_A + lane
    if permuted:
        piece = col // 256
        rest = col % 256
        col = (rest // PIECE) * SHARD_F + piece * PIECE + rest % PIECE
    return jnp.where((source == col) & (lane < SHARD_A), 1.0, 0.0).astype(BF16)


SEM_SHAPES = dict(
    a_s=(10,),
    a_r=(10,),
    z_r=(10, NZ),
    up_s=(10, NZ),
    dn_s=(10, NZ),
    b_s=(10, NZ),
    b_r=(10, NZ),
    c_s=(10, NZ),
    c_r=(10, NZ),
    rc_s=(12, 2),
    rc_r=(12, 2),
    rb_s=(12, NZ),
    rb_r=(12, NZ),
    rz_s=(12, NZ),
    rz_r=(12, NZ + 1),
    ra_s=(12,),
    ra_r=(12,),
    x_s=(4, 2),
    x_r=(4, 2),
    own=(4, 2),
    pool_s=(1,),
    pool_r=(1,),
    stat_s=(5,),
    stat_r=(5,),
    load=(2,),
)


def gather_pieces():
    return [(0, *GATHER_A[0]), (sum(GATHER_A[0]), *GATHER_A[1])] + [
        (k * PIECE, SPLIT_F, PIECE - SPLIT_F) for k in range(PIECES)
    ]


def scatter_pieces():
    return (
        gather_pieces()[2:]
        + [(0, *SCATTER_O)]
        + [(0, *SCATTER_A[0]), (sum(SCATTER_A[0]), *SCATTER_A[1])]
    )


def scratch():
    return dict(
        wa=pltpu.VMEM((NZ, NX, NC, NY, FULL_A, D), BF16),
        wf=pltpu.VMEM((NZ, NX, NC, NY, SHARD_F, D), BF16),
        rc=pltpu.VMEM((2, NZ, 2, PIECE, D), BF16),
        xs=pltpu.VMEM((TOKENS, D), BF16),
        dys=pltpu.VMEM((TOKENS, D), BF16),
        ctx=pltpu.VMEM((TOKENS, D), BF16),
        n1=pltpu.VMEM((TOKENS, D), BF16),
        fn=pltpu.VMEM((TOKENS, D), BF16),
        fg=pltpu.VMEM((TOKENS, D), BF16),
        qkv=pltpu.VMEM((TOKENS, 3 * D), BF16),
        act=pltpu.VMEM((PIECES, TOKENS, BLOCK), BF16),
        slope=pltpu.VMEM((PIECES, TOKENS, BLOCK), BF16),
        acc=pltpu.VMEM((TOKENS, D), F32),
        ask=pltpu.VMEM((OWN_ROWS, ROW, 128), BF16),
        bar=pltpu.VMEM((OWN_ROWS, ROW, 128), BF16),
        rco=pltpu.VMEM((2, 1, 2, FULL_A, D), BF16),
        totals=pltpu.VMEM((OWN_ROWS * HEADS // 2, 2, ROW), F32),
        side=pltpu.VMEM((TOKENS, 128), F32),
        vec=pltpu.VMEM((16, 4 * D), F32),
        bu=pltpu.VMEM((PIECES, 16, BLOCK), F32),
        gvec=pltpu.VMEM((8, 4 * D), F32),
        gbu=pltpu.VMEM((PIECES, 8, BLOCK), F32),
        stat=pltpu.VMEM((8, 128), F32),
        stat_in=pltpu.VMEM((5, 8, 128), F32),
        pool_out=pltpu.VMEM((OWN_ROWS, 8, D), F32),
        vector_pad=pltpu.VMEM((EXTRA, 128), F32),
        pool_in=pltpu.VMEM((OWN_ROWS, 8, D // 2), F32),
        credit=pltpu.SemaphoreType.REGULAR((2,)),
        free=pltpu.SemaphoreType.REGULAR,
    )


def landing_shapes():
    shapes = []
    shared = [tuple(map(max, SIZES_F, sizes)) for sizes in SCATTER_A]
    places = [(sizes, NZ) for sizes in (*shared, SIZES_F)] + [(SCATTER_O, 1)]
    for sizes, targets in places:
        for size in sizes:
            shapes += [
                pltpu.VMEM((targets, 2, size, D), BF16),
                pltpu.VMEM((targets + 1 if targets > 1 else 1, 2, size, D), BF16),
                pltpu.VMEM((size, D), BF16),
            ]
    return shapes


def fused_kernel(
    x_in,
    dy_in,
    wa_in,
    wf_in,
    vector_in,
    ids,
    flags,
    out_y,
    out_dx,
    out_pooled,
    out_stats,
    grad_a,
    grad_f,
    *more,
):
    names, sem_names = tuple(scratch()), tuple(SEM_SHAPES)
    landings = len(landing_shapes())
    r = types.SimpleNamespace(**dict(zip(names, more)))
    landing_refs = more[len(names) : len(names) + landings]
    sems = types.SimpleNamespace(**dict(zip(sem_names, more[len(names) + landings :])))
    me = Place()
    z, x, c, y = me.z, me.x, me.c, me.y
    wa, wf, xs, dys, ctx = r.wa, r.wf, r.xs, r.dys, r.ctx
    n1, fn, fg, qkv, acc = r.n1, r.fn, r.fg, r.qkv, r.acc
    act, slope, vec, gvec, stat = r.act, r.slope, r.vec, r.gvec, r.stat

    def tile(i, size):
        return pl.ds(pl.multiple_of(i * size, size), size)

    def row_ids(slot):
        return ids[pl.ds(2 * y + slot, 1), :]

    def row_flags(slot):
        return flags[pl.ds(2 * y + slot, 1), :].astype(F32)

    def vector(row, quarter):
        return vec[row : row + 1, quarter * D : (quarter + 1) * D]

    barrier = pltpu.get_barrier_semaphore()
    for where in (
        me.core(),
        me.at(x=1 - x),
        me.at(y=1 - y),
        me.at(z=(z + 2) % NZ),
    ):
        pl.semaphore_signal(barrier, inc=1, device_id=where, device_id_type=MESH)

    @pl.when(z > 0)
    def _():
        pl.semaphore_signal(barrier, inc=1, device_id=me.at(z=z - 1), device_id_type=MESH)

    @pl.when(z < NZ - 1)
    def _():
        pl.semaphore_signal(barrier, inc=1, device_id=me.at(z=z + 1), device_id_type=MESH)

    own_a, own_f = acc.at[0:SHARD_A], acc.at[SHARD_A : SHARD_A + SHARD_F]
    load_a = pltpu.make_async_copy(wa_in, own_a, sems.load.at[0])
    load_f = pltpu.make_async_copy(wf_in, own_f, sems.load.at[1])
    load_a.start()
    load_f.start()
    r.vector_pad[...] = jnp.zeros_like(r.vector_pad)
    r.vector_pad[0:3, 0:SHARD_A] = vector_in[...]
    wa[z, x, c, y, SHARD_A:FULL_A, :] = jnp.zeros((EXTRA, D), BF16)
    wa[z, x, c, y, SHARD_A:FULL_A, 0:128] = r.vector_pad[...].astype(BF16)

    def row_copy(kind, src, dst, slot):
        return remote(
            src, dst, sems.x_s.at[kind, slot], sems.x_r.at[kind, slot], me.at(y=1 - y)
        )

    def own_copy(kind, src, dst, slot):
        return pltpu.make_async_copy(src, dst, sems.own.at[kind, slot])

    def span(slot, half):
        return pl.ds(pl.multiple_of(slot * ROW + half * (ROW // 2), ROW // 2), ROW // 2)

    def take_rows(kind, source, target):
        sends = [
            row_copy(kind, source.at[2 * (1 - y) + slot], target.at[span(slot, y)], slot)
            for slot in range(OWN_ROWS)
        ]
        owns = [
            own_copy(kind, source.at[2 * y + slot], target.at[span(slot, y)], slot)
            for slot in range(OWN_ROWS)
        ]
        arrivals = [
            row_copy(kind, source.at[2 * y + slot], target.at[span(slot, 1 - y)], slot)
            for slot in range(OWN_ROWS)
        ]
        return sends, owns, arrivals

    def give_rows(kind, source, target):
        sends = [
            row_copy(kind, source.at[span(slot, 1 - y)], target.at[2 * y + slot], slot)
            for slot in range(OWN_ROWS)
        ]
        owns = [
            own_copy(kind, source.at[span(slot, y)], target.at[2 * y + slot], slot)
            for slot in range(OWN_ROWS)
        ]
        arrivals = [
            row_copy(kind, source.at[span(slot, y)], target.at[2 * (1 - y) + slot], slot)
            for slot in range(OWN_ROWS)
        ]
        return sends, owns, arrivals

    x_sends, x_owns, x_arrivals = take_rows(0, x_in, xs)
    dy_sends, dy_owns, dy_arrivals = take_rows(1, dy_in, dys)
    out_sends, out_owns, out_arrivals = give_rows(2, dys, out_y)
    dx_sends, dx_owns, dx_arrivals = give_rows(3, n1, out_dx)

    def start_all(copies):
        def run():
            for copy in copies:
                copy.start()

        return run

    gathers, scatters = [], []
    for piece, (first_row, *sizes) in enumerate(gather_pieces()):
        for order in range(2):
            buf = wa if piece < 2 else wf
            start = first_row + order * sizes[0]
            gathers.append(Gather(me, buf, start, sizes[order], order, 2 * piece + order, sems))
    places = (0, 1, 2, 3, 0, 1)
    for piece, (first_row, *sizes) in enumerate(scatter_pieces()):
        lone = piece == PIECES
        targets = (0, NZ) if piece < PIECES else (NZ - 1, NZ) if lone else (0, NZ - 1)
        for order in range(2):
            size, i = sizes[order], 2 * places[piece] + order
            landing = (
                r.rco if lone else r.rc,
                landing_refs[3 * i].at[:, :, 0:size],
                landing_refs[3 * i + 1].at[:, :, 0:size],
                landing_refs[3 * i + 2].at[0:size],
            )
            credit = r.credit.at[order]
            credits = (
                None if lone or piece == 0 else credit,
                None if lone or piece == len(places) - 1 else credit,
            )
            slot = order * sizes[0]
            scatters.append(
                Scatter(
                    me, wa if lone else wf, targets, first_row + slot, size, order,
                    2 * piece + order, sems, landing, grad_f if piece < PIECES else grad_a, slot,
                    credits,
                )
            )

    exchange = [copy.start for copy in x_sends + dy_sends + dx_sends]
    events = [event for one in gathers + scatters for event in one.events()] + exchange
    plan = Schedule(events)

    for copy in x_owns + dy_owns:
        copy.start()
    line_ends = jnp.where(z > 0, 1, 0).astype(jnp.int32) + jnp.where(z < NZ - 1, 1, 0).astype(
        jnp.int32
    )
    load_a.wait()
    wa[z, x, c, y, 0:SHARD_A, :] = own_a[...].astype(BF16)
    pl.semaphore_wait(barrier, 4 + line_ends)
    plan.step()
    load_f.wait()
    wf[z, x, c, y] = own_f[...].astype(BF16)
    plan.step()

    gvec[...] = jnp.zeros_like(gvec)
    r.gbu[...] = jnp.zeros_like(r.gbu)
    stat[...] = jnp.zeros_like(stat)
    for slot in range(OWN_ROWS):
        wide = jnp.broadcast_to(row_ids(slot).astype(F32), (128, ROW))
        tall = wide.T
        flag_rows = jnp.broadcast_to(row_flags(slot), (128, ROW))
        r.side[slot * ROW : (slot + 1) * ROW, :] = flag_rows.T
        lane = lax.broadcasted_iota(jnp.int32, (ROW, 128), 1) % HEAD_DIM
        same = tall == lane.astype(F32)
        r.ask[slot] = jnp.where(same & (lane < SEGMENTS), 1.0, 0.0).astype(BF16)
        r.bar[slot] = jnp.where(same | (lane >= SEGMENTS), 0.0, masked_score).astype(BF16)
        plan.step()
    ctx[...] = select_columns(False)
    fg[...] = select_columns(True)
    plan.step()
    plan.step()
    for one in gathers[:4]:
        one.finish()

    for q in range(4):
        blocks = jnp.concatenate(
            [
                wa[q, j // 4, (j // 2) % 2, j % 2, SHARD_A:FULL_A, 0:128]
                for j in range(8)
            ],
            axis=1,
        )
        vec[:, q * D : (q + 1) * D] = plain_dot(blocks, ctx[...])
        moved = plain_dot(blocks, fg[...])
        for k in range(PIECES):
            r.bu[k, :, q * 256 : (q + 1) * 256] = moved[:, k * 256 : (k + 1) * 256]

    plan.step(2)
    for copy in x_owns:
        copy.wait()
    for copy in x_arrivals:
        copy.wait_recv()

    scale = HEAD_DIM ** (-0.5)

    def project(i):
        rows = tile(i, 512)
        tokens = xs[rows, :]
        wide = tokens.astype(F32)
        stat[0:1, :] += lane_sums(wide * wide * r.side[rows, 1:2])
        for j in range(3):
            weights = flatten(wa[j, :, :, :, 0:SHARD_A, :])
            value = nt_dot(tokens, weights)
            if j == 0:
                value = (value + vector(0, 0)) * scale
            if j == 2:
                value = value + vector(0, 1)
            qkv[rows, j * D : (j + 1) * D] = value.astype(BF16)

    def lane_sums(value):
        total = column_sum(value)
        return sum(total[:, j * 128 : (j + 1) * 128] for j in range(D // 128))

    plan.loop(2, project)

    def columns(pair, block):
        return pl.ds(pl.multiple_of(block * D + pair * 128, 128), 128)

    def attend(i):
        slot, pair = i // (HEADS // 2), i % (HEADS // 2)
        rows = tile(slot, ROW)
        context, total = attention_pair(
            qkv[rows, columns(pair, 0)],
            qkv[rows, columns(pair, 1)],
            qkv[rows, columns(pair, 2)],
            r.ask[slot],
            r.bar[slot],
        )
        ctx[rows, columns(pair, 0)] = context.astype(BF16)
        r.totals[i] = total

    plan.loop(OWN_ROWS * HEADS // 2, attend)

    def attention_output(i):
        rows = tile(i, 256)
        weights = flatten(wa[3, :, :, :, 0:SHARD_A, :])
        out = nt_dot(ctx[rows, :], weights) + vector(0, 2)
        stat[1:2, :] += lane_sums(out * out * r.side[rows, 1:2])
        normed, inverse = normalize(xs[rows, :].astype(F32) + out)
        n1[rows, :] = normed.astype(BF16)
        r.side[rows, 0:1] = inverse
        fn[rows, :] = (normed * vector(2, 0) + vector(2, 1)).astype(BF16)

    plan.loop(4, attention_output)

    def up_rows(k):
        return flatten(flatten_lead(wf[0:2, :, :, :, k * PIECE : (k + 1) * PIECE, :]))

    def down_rows(k):
        return flatten(flatten_lead(wf[2:4, :, :, :, k * PIECE : (k + 1) * PIECE, :]))

    def flatten_lead(value):
        return value.reshape(-1, PIECE, D)

    for k in range(PIECES):
        plan.step()
        for one in gathers[4 + 2 * k : 6 + 2 * k]:
            one.finish()

        def feed(i, k=k):
            rows = tile(i, 512)
            up = nt_dot(fn[rows, :], up_rows(k)) + r.bu[k, 1:2, :]
            half = 0.5 * (1.0 + lax.erf(up * math.sqrt(0.5)))
            activated = (up * half).astype(BF16)
            act[k, rows, :] = activated
            slope[k, rows, :] = (
                half + up * (jnp.exp(-0.5 * up * up) * (1.0 / math.sqrt(2.0 * math.pi)))
            ).astype(BF16)
            value = plain_dot(activated, down_rows(k))
            if k == 0:
                acc[rows, :] = value
            else:
                acc[rows, :] += value

        plan.loop(2, feed)
    plan.step()

    for copy in dy_owns:
        copy.wait()
    for copy in dy_arrivals:
        copy.wait_recv()
    for one in gathers:
        one.drain()

    def second(i):
        rows = tile(i, 256)
        feed_out = acc[rows, :] + vector(0, 3)
        stat[2:3, :] += lane_sums(feed_out * feed_out * r.side[rows, 1:2])
        normed, inverse = normalize(fn[rows, :].astype(F32) + feed_out)
        grad = dys[rows, :].astype(F32)
        dys[rows, :] = (normed * vector(2, 2) + vector(2, 3)).astype(BF16)
        gvec[2:3, 2 * D : 3 * D] += column_sum(grad * normed)
        gvec[2:3, 3 * D :] += column_sum(grad)
        back = norm_back(grad * vector(2, 2), normed, inverse)
        acc[rows, :] = back
        low = back.astype(BF16)
        fg[rows, :] = low
        gvec[0:1, 3 * D :] += column_sum(low.astype(F32))

    repeat(TOKENS // 256, second)
    plan.step()

    start_all(out_sends + out_owns)()

    segments = lax.broadcasted_iota(jnp.int32, (SEGMENTS, ROW), 0)
    for slot in range(OWN_ROWS):
        member = jnp.where(segments == row_ids(slot), 1.0, 0.0) * row_flags(slot)
        sums = plain_dot(member.astype(BF16), dys[slot * ROW : (slot + 1) * ROW, :])
        counts = jnp.sum(member, axis=1, keepdims=True)
        r.pool_out[slot] = sums / jnp.maximum(counts, 1.0)
        total = row_flags(slot)
        stat[3:4, :] += sum(total[:, j * 128 : (j + 1) * 128] for j in range(ROW // 128))

    def half_lanes(which):
        return pl.ds(pl.multiple_of(which * (D // 2), 128), D // 2)

    pool_copy = remote(
        r.pool_out.at[:, :, half_lanes(1 - y)],
        r.pool_in,
        sems.pool_s.at[0],
        sems.pool_r.at[0],
        me.at(y=1 - y),
    )
    pool_copy.start()

    stat_partners = [
        me.core(),
        me.at(x=1 - x),
        me.at(y=1 - y),
        me.at(z=z + 1 - 2 * (z % 2)),
        me.at(z=(z + 2) % NZ),
    ]

    def stat_copy(step):
        return remote(
            stat,
            r.stat_in.at[step],
            sems.stat_s.at[step],
            sems.stat_r.at[step],
            stat_partners[step],
        )

    def stat_start(step):
        return lambda: stat_copy(step).start()

    def stat_end(step):
        def run():
            stat_copy(step).wait()
            stat[...] += r.stat_in[step]

        return run

    stat_start(0)()
    plan.step()
    for k in range(PIECES):

        def feed_back(i, k=k):
            rows = tile(i, 512)
            grad = nt_dot(fg[rows, :], down_rows(k)) * slope[k, rows, :].astype(F32)
            low = grad.astype(BF16)
            slope[k, rows, :] = low
            r.gbu[k, 0:1, :] += column_sum(low.astype(F32))
            acc[rows, :] += plain_dot(low, up_rows(k))

        plan.loop(2, feed_back)

        def weights_back(i, k=k):
            cols = tile(i, BLOCK // 2)
            down = tn_dot(act[k, :, cols], fg[...]).astype(BF16)
            up = tn_dot(slope[k, :, cols], fn[...]).astype(BF16)
            where = (slice(None), slice(None), slice(None), pl.ds(k * PIECE, PIECE))
            wf[(2 + i, *where)] = down.reshape(NX, NC, NY, PIECE, D)
            wf[(i, *where)] = up.reshape(NX, NC, NY, PIECE, D)

        plan.loop(2, weights_back)
        stat_end(k)()
        stat_start(k + 1)()

    def first(i):
        rows = tile(i, 128)
        grad = acc[rows, :]
        normed = n1[rows, :].astype(F32)
        gvec[2:3, 0:D] += column_sum(grad * normed)
        gvec[2:3, D : 2 * D] += column_sum(grad)
        stream = norm_back(grad * vector(2, 0), normed, r.side[rows, 0:1])
        acc[rows, :] = stream
        low = stream.astype(BF16)
        fg[rows, :] = low
        gvec[0:1, 2 * D : 3 * D] += column_sum(low.astype(F32))

    plan.loop(TOKENS // 128, first)

    def context_back(i):
        rows = tile(i, 512)
        fn[rows, :] = plain_dot(fg[rows, :], flatten(wa[3, :, :, :, 0:SHARD_A, :])).astype(BF16)

    plan.loop(2, context_back)
    stat_end(3)()
    stat_start(4)()

    def outer_back(i):
        cols = pl.ds(pl.multiple_of(i * (D // 2), 128), D // 2)
        value = tn_dot(fg[:, cols], ctx[...]).astype(BF16)
        wa[3, i, :, :, 0:SHARD_A, :] = value.reshape(NC, NY, SHARD_A, D)

    plan.loop(2, outer_back)

    ctx[...] = select_columns(False)
    fg[...] = select_columns(True)

    def vectors_back(q, buf):
        row = lax.broadcasted_iota(jnp.int32, (8, 1), 0)
        plain = nt_dot(gvec[:, q * D : (q + 1) * D].astype(BF16), ctx[...])
        piled = jnp.concatenate(
            [r.gbu[k, :, q * 256 : (q + 1) * 256] for k in range(PIECES)], axis=1
        )
        moved = nt_dot(piled.astype(BF16), fg[...])
        low = jnp.where(row == 1, jnp.broadcast_to(moved[0:1, :], plain.shape), plain)
        low = jnp.concatenate([low, jnp.zeros_like(low)], axis=0).astype(BF16)
        for j in range(8):
            buf[q, j // 4, (j // 2) % 2, j % 2, SHARD_A:FULL_A, 0:128] = low[
                :, j * 128 : (j + 1) * 128
            ]

    vectors_back(3, wa)
    plan.step()

    def attend_back_pair(slot, pair):
        rows = tile(slot, ROW)
        grads = attention_pair_back(
            qkv[rows, columns(pair, 0)],
            qkv[rows, columns(pair, 1)],
            qkv[rows, columns(pair, 2)],
            fn[rows, columns(pair, 0)],
            r.ask[slot],
            r.bar[slot],
            r.totals[slot * (HEADS // 2) + pair],
        )
        for j in range(3):
            low = grads[j].astype(BF16)
            if j == 0:
                low = low * jnp.asarray(scale, BF16)
            qkv[rows, columns(pair, j)] = low
            if j != 1:
                gvec[0:1, columns(pair, j // 2)] += column_sum(low.astype(F32))

    def input_back(slot):
        rows = pl.ds(slot * ROW, ROW)
        value = acc[rows, :]
        for j in range(3):
            value += plain_dot(
                qkv[rows, j * D : (j + 1) * D], flatten(wa[j, :, :, :, 0:SHARD_A, :])
            )
        n1[rows, :] = value.astype(BF16)
        dx_owns[slot].start()

    plan.loop(HEADS // 2, functools.partial(attend_back_pair, 0))
    input_back(0)
    plan.step()
    plan.loop(HEADS // 2, functools.partial(attend_back_pair, 1))
    stat_end(4)()
    plan.step()
    for one in scatters[:4]:
        one.drain()

    free = r.free
    for where in (me.at(x=1 - x), me.at(y=1 - y)):
        pl.semaphore_signal(free, inc=1, device_id=where, device_id_type=MESH)

    @pl.when(z > 0)
    def _():
        pl.semaphore_signal(free, inc=1, device_id=me.at(z=z - 1), device_id_type=MESH)

    @pl.when(z < NZ - 1)
    def _():
        pl.semaphore_signal(free, inc=1, device_id=me.at(z=z + 1), device_id_type=MESH)

    for j in range(3):

        def inner_back(i, j=j):
            cols = pl.ds(pl.multiple_of(j * D + i * (D // 2), 128), D // 2)
            value = tn_dot(qkv[:, cols], xs[...]).astype(BF16)
            wf[j, i, :, :, 0:SHARD_A, :] = value.reshape(NC, NY, SHARD_A, D)

        plan.loop(2, inner_back)
    for q in range(3):
        vectors_back(q, wf)
    pl.semaphore_wait(free, 2 + line_ends)
    plan.step()
    input_back(1)
    plan.step(2)

    assert plan.place == len(PLAN)
    for one in scatters[4:]:
        one.drain()
    pool_copy.wait()
    for slot in range(OWN_ROWS):
        out_pooled[2 * y + slot] = r.pool_out[slot, :, half_lanes(y)]
        out_pooled[2 * (1 - y) + slot] = r.pool_in[slot]
    out_stats[...] = stat[...]
    for copies in (x_sends, dy_sends, out_sends, dx_sends):
        for copy in copies:
            copy.wait_send()
    for copies in (out_owns, dx_owns):
        for copy in copies:
            copy.wait()
    for copies in (out_arrivals, dx_arrivals):
        for copy in copies:
            copy.wait_recv()


def finish_kernel(y_in, dx_in, pooled_in, stats, grad_a, grad_f, grad_v, *more):
    states, results = more[:9], more[9:]
    out_y, out_dx, out_pooled, out_rms = results[:4]
    out_y[...] = y_in[...]
    out_dx[...] = dx_in[...]
    out_pooled[...] = pooled_in[...]
    totals = jnp.sum(stats[...], axis=1, keepdims=True)
    rms = jnp.sqrt(totals[0:3] / D / totals[3:4])
    for i in range(3):
        out_rms[i] = rms[i, 0]
    rates = (
        (rate_attention, weight_decay),
        (rate_feedforward, weight_decay),
        (rate_vectors, 0.0),
    )
    gradients = (grad_a[...], grad_f[...], grad_v[0:3, 0:SHARD_A])
    for i in range(3):
        weight, first, second = states[3 * i : 3 * i + 3]
        new = adamw_update(weight[...], gradients[i], first[...], second[...], *rates[i])
        for ref, value in zip(results[4 + 4 * i : 8 + 4 * i], new):
            ref[...] = value


def fused_shards(
    inputs,
    segment_ids,
    token_flags,
    output_grad,
    attention_weights,
    feedforward_weights,
    layer_vectors,
    attention_first,
    attention_second,
    feedforward_first,
    feedforward_second,
    vector_first,
    vector_second,
):
    any_space = pl.BlockSpec(memory_space=pl.ANY)
    vmem = pl.BlockSpec(memory_space=pltpu.VMEM)
    smem = pl.BlockSpec(memory_space=pltpu.SMEM)
    rows = jax.ShapeDtypeStruct(inputs.shape, BF16)
    pooled = jax.ShapeDtypeStruct((inputs.shape[0], SEGMENTS, D // NY), F32)
    semaphores = [pltpu.SemaphoreType.DMA(shape) for shape in SEM_SHAPES.values()]
    passed = pl.pallas_call(
        fused_kernel,
        out_shape=(
            rows,
            rows,
            pooled,
            jax.ShapeDtypeStruct((8, 128), F32),
            jax.ShapeDtypeStruct((FULL_A, D), F32),
            jax.ShapeDtypeStruct((SHARD_F, D), F32),
        ),
        in_specs=[any_space] * 4 + [vmem] * 3,
        out_specs=(any_space, any_space, vmem, vmem, vmem, vmem),
        scratch_shapes=list(scratch().values()) + landing_shapes() + semaphores,
        compiler_params=pltpu.CompilerParams(
            collective_id=0, has_side_effects=True, vmem_limit_bytes=65_000 * 1024
        ),
        name="layer",
    )(
        inputs,
        output_grad,
        attention_weights.T,
        feedforward_weights.T,
        layer_vectors,
        segment_ids,
        token_flags,
    )
    states = (
        attention_weights.T,
        attention_first.T,
        attention_second.T,
        feedforward_weights.T,
        feedforward_first.T,
        feedforward_second.T,
        layer_vectors,
        vector_first,
        vector_second,
    )

    def updated(shape):
        wide = jax.ShapeDtypeStruct(shape, F32)
        return (wide, wide, wide, jax.ShapeDtypeStruct(shape, BF16))

    steps = 2

    def part(shape):
        return pl.BlockSpec((shape[0] // steps, *shape[1:]), lambda i: (i,) + (0,) * (len(shape) - 1))

    def whole(shape):
        return pl.BlockSpec(shape, lambda i: (0,) * len(shape))

    table_a, table_f, table_v = (SHARD_A, D), (SHARD_F, D), layer_vectors.shape
    results = pl.pallas_call(
        finish_kernel,
        grid=(steps,),
        out_shape=(rows, rows, pooled, jax.ShapeDtypeStruct((3,), F32))
        + updated(table_a)
        + updated(table_f)
        + updated(table_v),
        in_specs=[part(rows.shape), part(rows.shape), part(pooled.shape), whole((8, 128))]
        + [part(table_a), part(table_f), pl.BlockSpec((EXTRA, D), lambda i: (SHARD_A // EXTRA, 0))]
        + [part(table_a)] * 3
        + [part(table_f)] * 3
        + [whole(table_v)] * 3,
        out_specs=[part(rows.shape), part(rows.shape), part(pooled.shape), smem]
        + [part(table_a)] * 4
        + [part(table_f)] * 4
        + [whole(table_v)] * 4,
        compiler_params=pltpu.CompilerParams(vmem_limit_bytes=65_000 * 1024),
        name="finish",
    )(*passed, passed[4], *states)
    results = tuple(results)
    return results[:4] + tuple(value.T for value in results[4:12]) + results[12:]


def solution(mesh):
    fused = mesh.shape["fsdp"] == NZ * NX * NC and mesh.shape["seq"] == NY
    rows = P("fsdp", "seq", None)
    table = P("fsdp", None)
    owned = P(None, ("fsdp", "seq"))
    return jax.shard_map(
        fused_shards if fused else plain_shards,
        mesh=mesh,
        in_specs=(rows, table, table, rows) + (owned,) * 9,
        out_specs=(rows, rows, P("fsdp", None, "seq"), P()) + (owned,) * 12,
        check_vma=False,
    )
```
